32 devices in a mesh: seq: 4 (over y, x), dec: 8 (over z, core).
Axes of the slice: x: 2, y: 2, z: 4, core: 2. Of those that a mesh axis runs over, the one named last changes fastest.
Arguments:
- latents: bfloat16 [4, 4, 12, 8, 1024], P('seq', None, None, 'dec'), may hold values from -6 to 6
- cache_lat: bfloat16 [4, 4, 12, 8, 512], P('seq', None, None, 'dec'), may hold values from -6 to 6
- cache_act: bfloat16 [4, 4, 12, 8, 12288], P('seq', None, None, 'dec'), may hold values from -0.25 to 2
- w_in: bfloat16 [27, 16, 384], replicated, may hold values from -0.3125 to 0.3125
- w_mid: bfloat16 [27, 384, 384], replicated, may hold values from -0.0625 to 0.0625
- norm_gain: float32 [384], replicated, may hold values from 0.1 to 1.9
- clip_group: int32 [4, 4], replicated, may hold values from 0 to 3, as said below
- band_rows: int32 [4, 8], replicated, may hold values from 2 to 96, as said below
Outputs:
- decoded: bfloat16 [4, 8, 96, 4, 16, 384], P('seq', 'dec')
The draws below stay inside these ranges and needn't reach their ends.
Inputs may be any that keep to these rules, and one draw needn't show every extreme that they name: For every sequence shard s, clip_group[s, :] names each of the 4 groups once. Each row of band_rows sums to 384; every band has 2 rows or more, and in each row one band has exactly 96 rows.
All inputs are finite; a program needn't handle non-finite values.
Results may differ from the reference program's by a relative error of at most 0.0029.
Values may be sent and summed in bfloat16 or wider, within the bound.
No kernel may reach another device: no remote copies, remote signals or barrier semaphores. Data moves between devices by JAX's collectives and lax.ppermute only.
A program may use at most 384 MiB of HBM per device.

```python
import jax
import jax.numpy as jnp
from jax import lax

ZC = 16
C = 384
F = 4
CT = 2
COLS = 16
H = 96
RD = 12
STACK = 384
CLIPS = 16
BAND_MAX = 96
N_SEQ = 4
N_DEC = 8


def draw_clip_group(key, part):
    shard_keys = jax.vmap(lambda shard_index: jax.random.fold_in(key, shard_index))(jnp.arange(N_SEQ))
    return jax.vmap(lambda one_key: jax.random.permutation(one_key, N_SEQ))(shard_keys).astype(jnp.int32)


def band_counts(one_key):
    owners = N_DEC
    mean_rows = N_SEQ * H // N_DEC
    order_key, step_key = jax.random.split(one_key)
    owner_order = jax.random.permutation(order_key, owners)
    rank_ids = jnp.arange(owners - 1, dtype=jnp.int32)
    deduct = mean_rows * (rank_ids + 1) // (owners - 1) - mean_rows * rank_ids // (owners - 1)
    by_position = jnp.concatenate([jnp.full((1,), 2 * mean_rows, jnp.int32), (mean_rows - deduct).astype(jnp.int32)])
    pair_count = (owners - 1) // 2
    upper_rows = by_position[1:1 + 2 * pair_count:2]
    lower_rows = by_position[2:2 + 2 * pair_count:2]
    shifted = jax.random.randint(step_key, (pair_count,), 2 - upper_rows, lower_rows - 1, dtype=jnp.int32)
    by_position = by_position.at[1:1 + 2 * pair_count:2].add(shifted)
    by_position = by_position.at[2:2 + 2 * pair_count:2].add(-shifted)
    return jnp.zeros((owners,), jnp.int32).at[owner_order].set(by_position)


def draw_band_rows(key, part):
    group_keys = jax.vmap(lambda group_index: jax.random.fold_in(key, 1000 + group_index))(jnp.arange(N_SEQ))
    return jax.vmap(band_counts)(group_keys).astype(jnp.int32)


def block_levels(rng, extent, shards, smallest, largest):
    level, own = 1.0, jax.random.fold_in(rng, 6)
    for position, shards_of in shards:
        draws = jnp.exp(jax.random.uniform(jax.random.fold_in(own, position), (shards_of,), jnp.float32, smallest / len(shards), largest / len(shards)))
        level = level * jnp.repeat(draws, extent[position] // shards_of).reshape([-1 if axis == position else 1 for axis in range(len(extent))])
    return level


def centred(own_key, shape, scale, limit, cuts=(), held_as=jnp.bfloat16):
    entries = scale * jax.random.normal(own_key, shape, jnp.float32)
    if cuts:
        entries = entries * block_levels(own_key, shape, cuts, -0.22, 0.18)
    return jnp.clip(entries, -limit, limit).astype(held_as)


def setup_inputs(seed: int = 0) -> dict:
    streams_of = jax.random.split(jax.random.key(seed), 9)
    latents = centred(streams_of[0], (N_SEQ, N_SEQ, RD, N_DEC, F * COLS * ZC), 1.0, 6.0, ((0, 4), (3, 8)))
    cache_lat = centred(streams_of[1], (N_SEQ, N_SEQ, RD, N_DEC, CT * COLS * ZC), 1.0, 6.0, ((0, 4), (3, 8)))
    cache_act = jnp.clip(-0.25 + 2.25 * jax.random.uniform(streams_of[2], (N_SEQ, N_SEQ, RD, N_DEC, CT * COLS * C), jnp.float32) ** block_levels(streams_of[2], (N_SEQ, N_SEQ, RD, N_DEC, CT * COLS * C), ((0, 4), (3, 8)), -0.2, 0.2), -0.25, 2.0).astype(jnp.bfloat16)
    w_in = centred(streams_of[3], (27, ZC, C), (27 * ZC) ** -0.5, 0.3125)
    w_mid = centred(streams_of[4], (27, C, C), (27 * C) ** -0.5, 0.0625)
    norm_gain = jnp.clip(1.0 + 0.18 * jax.random.normal(streams_of[5], (C,), jnp.float32), 0.1, 1.9)
    clip_group = draw_clip_group(jax.random.fold_in(streams_of[8], 71), 0)
    band_rows = draw_band_rows(jax.random.fold_in(streams_of[8], 71), 0)
    return {"latents": latents, "cache_lat": cache_lat, "cache_act": cache_act, "w_in": w_in, "w_mid": w_mid, "norm_gain": norm_gain, "clip_group": clip_group, "band_rows": band_rows}


EPSILON = 1e-06

def causal_conv(frames_in, weights):
    row_count = frames_in.shape[0]
    padded = jnp.pad(frames_in, ((1, 1), (0, 0), (1, 1), (0, 0)))
    total_sum = jnp.zeros((row_count * F * COLS, weights.shape[2]), jnp.float32)
    for time_tap in range(3):
        for row_tap in range(3):
            for col_tap in range(3):
                tap_rows = padded[row_tap:row_tap + row_count, time_tap:time_tap + F, col_tap:col_tap + COLS, :]
                total_sum = total_sum + jnp.dot(tap_rows.reshape(row_count * F * COLS, weights.shape[1]), weights[time_tap * 9 + row_tap * 3 + col_tap], preferred_element_type=jnp.float32)
    return total_sum.reshape(row_count, F, COLS, weights.shape[2])

def decode_clip(inputs, w_in, w_mid, norm_gain):
    latent, old_lat, old_act = inputs
    layer_in = jnp.concatenate([old_lat.reshape(H, CT, COLS, ZC), latent.reshape(H, F, COLS, ZC)], axis=1)
    first_out = causal_conv(layer_in, w_in)
    mean_square = lax.optimization_barrier(jnp.mean(first_out * first_out, axis=-1, keepdims=True))
    activated = jax.nn.silu(first_out * lax.rsqrt(mean_square + EPSILON) * norm_gain).astype(jnp.bfloat16)
    conv_input = jnp.concatenate([old_act.reshape(H, CT, COLS, C), activated], axis=1)
    return (first_out + causal_conv(conv_input, w_mid)).astype(jnp.bfloat16)

def reference(latents, cache_lat, cache_act, w_in, w_mid, norm_gain, clip_group, band_rows):
    clip_lat = latents.reshape(CLIPS, H, F * COLS * ZC)
    clip_old = cache_lat.reshape(CLIPS, H, CT * COLS * ZC)
    clip_act = cache_act.reshape(CLIPS, H, CT * COLS * C)
    decoded_clips = lax.map(lambda inputs: decode_clip(inputs, w_in, w_mid, norm_gain), (clip_lat, clip_old, clip_act))
    decoded_clips = decoded_clips.reshape(N_SEQ, N_SEQ, H, F, COLS, C)
    group_ids = jnp.arange(N_SEQ, dtype=jnp.int32)
    match_group = clip_group[:, :, None] == group_ids[None, None, :]
    chosen = lax.optimization_barrier(jnp.sum(jnp.where(match_group, group_ids[None, :, None], 0), axis=1)).astype(jnp.int32)
    stacks = decoded_clips[group_ids[None, :], chosen.T]
    stacks = stacks.reshape(N_SEQ, STACK, F, COLS, C)
    starts = (jnp.cumsum(band_rows, axis=1) - band_rows).astype(jnp.int32)
    offsets = jnp.arange(BAND_MAX, dtype=jnp.int32)
    live_mask = offsets[None, None, :] < band_rows[:, :, None]
    pick_rows = jnp.where(live_mask, starts[:, :, None] + offsets[None, None, :], 0).astype(jnp.int32)
    pick_rows = pick_rows.reshape(N_SEQ, N_DEC * BAND_MAX)
    gathered = jax.vmap(lambda stack_one, pick_one: stack_one[pick_one])(stacks, pick_rows)
    gathered = gathered.reshape(N_SEQ, N_DEC, BAND_MAX, F, COLS, C)
    return jnp.where(live_mask[:, :, :, None, None, None], gathered, jnp.zeros((), jnp.bfloat16))
```

```python
import functools

import jax
import jax.numpy as jnp
from jax import lax
from jax.experimental import pallas as pl
from jax.experimental.pallas import tpu as pltpu
from jax.sharding import PartitionSpec as P

F = 4
CT = 2
COLS = 16
LANES = 128
EPSILON = 1e-06
VMEM = 56 * 1024 * 1024
F32 = jnp.float32
BF16 = jnp.bfloat16


def ceil_to(value, unit):
    return (value + unit - 1) // unit * unit


def band_start(bands, group, owner, owners):
    total = jnp.int32(0)
    for other in range(owners):
        total = total + jnp.where(other < owner, bands[group, other], 0)
    return total


def first_unit(start, margin, source, owners, units, capacity):
    unit = (start - margin - source + owners - 1 + 2 * owners) // owners - 2
    return jnp.clip(unit, 0, units - capacity)


def clip_of(groups_ref, shard, group, clips):
    found = jnp.int32(0)
    for clip in range(clips):
        found = found + jnp.where(groups_ref[shard, clip] == group, clip, 0)
    return found


def pack_latents(groups_ref, lat_ref, old_ref, out_ref, scratch, *, per_owner, clips, rows):
    shard = lax.axis_index("seq")
    for row in range(per_owner):
        for frame in range(CT + F):
            for half in range(2):
                if frame < CT:
                    tile = frame * 2 + half
                    value = old_ref[row, :, tile * LANES : (tile + 1) * LANES]
                else:
                    tile = (frame - CT) * 2 + half
                    value = lat_ref[row, :, tile * LANES : (tile + 1) * LANES]
                at = row * 12 + half * (CT + F) + frame
                scratch[pl.ds(at, clips, stride=rows), :] = value.astype(F32)
    for group in range(clips):
        clip = clip_of(groups_ref, shard, group, clips)
        out_ref[group] = scratch[pl.ds(pl.multiple_of(clip * rows, 8), rows), :].astype(BF16)


def pack_caches(groups_ref, act_ref, out_ref, scratch, *, per_step, clips):
    shard = lax.axis_index("seq")
    tiles = act_ref.shape[2] // LANES
    depth = tiles // (CT * COLS)
    for row in range(per_step):
        for frame in range(CT):
            for col in range(COLS):
                for part in range(depth):
                    tile = (frame * COLS + col) * depth + part
                    at = row * tiles + (frame * depth + part) * COLS + col
                    value = act_ref[row, :, tile * LANES : (tile + 1) * LANES]
                    scratch[pl.ds(at, clips, stride=per_step * tiles), :] = value.astype(F32)
    for group in range(clips):
        clip = clip_of(groups_ref, shard, group, clips)
        size = per_step * tiles
        out_ref[group] = scratch[pl.ds(pl.multiple_of(clip * size, 8), size), :].astype(BF16)


def slice_latents(bands, in_ref, out_ref, scratch, *, owners, units, capacity, per_owner):
    group = lax.axis_index("seq")
    source = lax.axis_index("dec")
    rows = out_ref.shape[1]
    for shard in range(in_ref.shape[0]):
        size = per_owner * 12
        scratch[pl.ds(shard * size, in_ref.shape[1]), :] = in_ref[shard].astype(F32)
    for owner in range(owners):
        start = band_start(bands, group, owner, owners)
        unit = first_unit(start, 2, source, owners, units, capacity)
        out_ref[owner] = scratch[pl.ds(unit * 12, rows), :].astype(BF16)


def slice_caches(bands, in_ref, out_ref, sems, *, owners, units, capacity, tiles):
    group = lax.axis_index("seq")
    source = lax.axis_index("dec")
    copies = []
    for owner in range(owners):
        start = band_start(bands, group, owner, owners)
        unit = first_unit(start, 1, source, owners, units, capacity)
        copy = pltpu.make_async_copy(
            in_ref.at[pl.ds(pl.multiple_of(unit * tiles, 16), capacity * tiles)],
            out_ref.at[owner],
            sems.at[owner],
        )
        copy.start()
        copies.append(copy)
    for copy in copies:
        copy.wait()


def shift_columns(sums, width):
    rows = sums.shape[0]
    col = lax.rem(lax.broadcasted_iota(jnp.int32, (rows, width), 0), COLS)
    left = pltpu.roll(sums[:, :width], 1, 0)
    right = pltpu.roll(sums[:, 2 * width :], rows - 1, 0)
    total = sums[:, width : 2 * width] + jnp.where(col > 0, left, 0.0)
    return total + jnp.where(col < COLS - 1, right, 0.0)


def weight_copies(mid_ref, weights, sems, channels, time_taps):
    copies = []
    for tap in range(time_taps * 9):
        copies.append(
            pltpu.make_async_copy(
                mid_ref.at[tap],
                weights.at[
                    pl.ds(tap // 3 * channels, channels), pl.ds(tap % 3 * channels, channels)
                ],
                sems.at[tap],
            )
        )
    return copies


def new_frames(
    bands, lat_ref, win_ref, gain_ref, mid_ref, out_ref, part_ref,
    weights, table, xs, windows, first, act, sems,
    *, owners, units, capacity, height, block, band_max, channels,
):
    group = lax.axis_index("seq")
    owner = lax.axis_index("dec")
    live = bands[group, owner]
    start = band_start(bands, group, owner, owners)
    step = pl.program_id(0)
    ext = band_max + 4
    depth = channels // LANES
    zero_row = ext
    edge = lax.rem(height - lax.rem(start - 1 + height, height), height)

    @pl.when(step == 0)
    def _():
        copies = weight_copies(mid_ref, weights, sems, channels, 3)
        for copy in copies:
            copy.start()
        table[...] = jnp.zeros(table.shape, BF16)
        for tap in range(9):
            for col in range(4):
                for shift in range(3):
                    table[
                        pl.ds(tap * LANES + (col + shift + 1) * 16, 16),
                        pl.ds(col * channels, channels),
                    ] = win_ref[tap * 3 + shift]
        per_source = lat_ref.shape[1]
        for source in range(owners):
            xs[pl.ds(source * per_source, per_source), :] = lat_ref[source].astype(F32)
        lane = lax.broadcasted_iota(jnp.int32, (8, LANES), 1)

        def fill(row, carry):
            at = jnp.clip(start - 2 + row, 0, units * owners - 1)
            source = lax.rem(at, owners)
            unit = first_unit(start, 2, source, owners, units, capacity)
            slot = jnp.clip(at // owners - unit, 0, capacity - 1)
            base = source * per_source + slot * 12
            for tap in range(3):
                left = xs[pl.ds(base + tap, 8), :]
                right = xs[pl.ds(base + tap + CT + F, 8), :]
                left_up, left_down = pltpu.roll(left, 32, 1), pltpu.roll(left, 96, 1)
                right_up, right_down = pltpu.roll(right, 32, 1), pltpu.roll(right, 96, 1)
                into = pl.ds(row * F, 8)
                windows[0, tap, into, :] = jnp.where(lane < 32, 0.0, left_up)
                windows[1, tap, into, :] = jnp.where(lane < 96, left_down, right_down)
                windows[2, tap, into, :] = jnp.where(lane < 32, left_up, right_up)
                windows[3, tap, into, :] = jnp.where(lane < 96, right_down, 0.0)
            return carry

        lax.fori_loop(0, ext, fill, 0)
        for tap in range(3):
            for quarter in range(4):
                windows[quarter, tap, pl.ds(ext * F, 16), :] = jnp.zeros((16, LANES), F32)

        rows = ext * F
        at_row = lax.broadcasted_iota(jnp.int32, (rows, LANES), 0) // F
        above = ((at_row != edge) & (at_row != edge + height)).astype(F32)
        below = ((at_row != edge - 1) & (at_row != edge - 1 + height)).astype(F32)

        def convolve(quarter, carry):
            pieces = []
            for tap in range(3):
                for row_tap in range(3):
                    piece = windows[quarter, tap, pl.ds(row_tap * F, rows), :]
                    if row_tap == 0:
                        piece = piece * above
                    if row_tap == 2:
                        piece = piece * below
                    pieces.append(piece.astype(BF16))
            slab = jnp.concatenate(pieces, axis=1)
            for col in range(4):
                sums = jnp.dot(
                    slab, table[:, pl.ds(col * channels, channels)], preferred_element_type=F32
                )
                for part in range(depth):
                    first[part, pl.ds(quarter * 4 + col, rows, stride=COLS), :] = sums[
                        :, part * LANES : (part + 1) * LANES
                    ]
            return carry

        lax.fori_loop(0, 4, convolve, 0)
        gain = gain_ref[...]

        def activate(row, carry):
            into = pl.ds(pl.multiple_of(row * F * COLS, F * COLS), F * COLS)
            value = jnp.concatenate([first[part, into, :] for part in range(depth)], axis=1)
            mean_square = jnp.mean(value * value, axis=-1, keepdims=True)
            value = value * lax.rsqrt(mean_square + EPSILON) * gain
            value = value / (1.0 + jnp.exp(-value))
            act[row] = value.astype(BF16).reshape(F, COLS, channels)
            return carry

        lax.fori_loop(0, live + 2, activate, 0)
        act[zero_row] = jnp.zeros((F, COLS, channels), BF16)
        for copy in copies:
            copy.wait()

    begin = step * block

    @pl.when(begin < live)
    def _():
        source_rows = [[], [], []]
        for row in range(block):
            at = jnp.minimum(begin + row, live - 1) + 1
            is_first = (at == edge) | (at == edge + height)
            is_last = (at == edge - 1) | (at == edge - 1 + height)
            source_rows[0].append(jnp.where(is_first, zero_row, at - 1))
            source_rows[1].append(at)
            source_rows[2].append(jnp.where(is_last, zero_row, at + 1))

        def slab(frames):
            pieces = []
            for frame, count in frames:
                for row_tap in range(3):
                    parts = [
                        act[at, frame : frame + count].reshape(count * COLS, channels)
                        for at in source_rows[row_tap]
                    ]
                    pieces.append(jnp.concatenate(parts, axis=0))
            return jnp.concatenate(pieces, axis=1)

        def finish(frames, weight_from, frame_from, count):
            sums = jnp.dot(slab(frames), weights[weight_from:, :], preferred_element_type=F32)
            total = shift_columns(sums, channels)
            parts = []
            for row in range(block):
                at = (begin + row + 1) * F * COLS + frame_from * COLS
                into = pl.ds(pl.multiple_of(at, COLS), count * COLS)
                parts.append(
                    jnp.concatenate([first[part, into, :] for part in range(depth)], axis=1)
                )
            return total + jnp.concatenate(parts, axis=0)

        taps = 3 * channels
        late = finish([(0, 2), (1, 2), (2, 2)], 0, 2, 2)
        at_row = lax.broadcasted_iota(jnp.int32, late.shape, 0) // (2 * COLS)
        late = jnp.where(at_row < live - begin, late, 0.0)
        out_ref[...] = late.astype(BF16).reshape(block, 2, COLS, channels)
        part_ref[:, 1] = finish([(0, 1), (1, 1)], taps, 1, 1).reshape(block, COLS, channels)
        part_ref[:, 0] = finish([(0, 1)], 2 * taps, 0, 1).reshape(block, COLS, channels)

    @pl.when(begin >= live)
    def _():
        out_ref[...] = jnp.zeros(out_ref.shape, BF16)


def cached_frames(
    bands, cache_ref, part_ref, mid_ref, late_ref, out_ref, weights, cache, sems, cache_sem,
    *, owners, units, capacity, height, block, channels,
):
    del late_ref
    group = lax.axis_index("seq")
    owner = lax.axis_index("dec")
    live = bands[group, owner]
    start = band_start(bands, group, owner, owners)
    step = pl.program_id(0)
    depth = channels // LANES
    slots = owners * capacity
    edge = lax.rem(height - lax.rem(start - 1 + height, height), height)

    @pl.when(step == 0)
    def _():
        copies = weight_copies(mid_ref, weights, sems, channels, 2)
        load = pltpu.make_async_copy(cache_ref, cache.at[pl.ds(0, slots)], cache_sem)
        load.start()
        for copy in copies:
            copy.start()
        cache[slots] = jnp.zeros(cache.shape[1:], BF16)
        load.wait()
        for copy in copies:
            copy.wait()

    begin = step * block

    @pl.when(begin < live)
    def _():
        def slot_of(at):
            row = jnp.clip(start - 1 + at, 0, units * owners - 1)
            source = lax.rem(row, owners)
            unit = first_unit(start, 1, source, owners, units, capacity)
            return source * capacity + jnp.clip(row // owners - unit, 0, capacity - 1)

        source_rows = [[], [], []]
        for row in range(block):
            at = jnp.minimum(begin + row, live - 1) + 1
            is_first = (at == edge) | (at == edge + height)
            is_last = (at == edge - 1) | (at == edge - 1 + height)
            source_rows[0].append(jnp.where(is_first, slots, slot_of(at - 1)))
            source_rows[1].append(slot_of(at))
            source_rows[2].append(jnp.where(is_last, slots, slot_of(at + 1)))

        def slab(frames):
            pieces = []
            for frame in frames:
                for row_tap in range(3):
                    for part in range(depth):
                        from_tile = (frame * depth + part) * COLS
                        parts = [
                            cache[at, from_tile : from_tile + COLS, :]
                            for at in source_rows[row_tap]
                        ]
                        pieces.append(jnp.concatenate(parts, axis=0))
            return jnp.concatenate(pieces, axis=1)

        at_row = lax.broadcasted_iota(jnp.int32, (block * COLS, channels), 0) // COLS
        taps = 3 * channels
        for frame, frames in ((0, (0, 1)), (1, (1,))):
            sums = jnp.dot(
                slab(frames), weights[: len(frames) * taps, :], preferred_element_type=F32
            )
            total = shift_columns(sums, channels) + part_ref[:, frame].reshape(
                block * COLS, channels
            )
            total = jnp.where(at_row < live - begin, total, 0.0)
            out_ref[:, frame] = total.astype(BF16).reshape(block, COLS, channels)

    @pl.when(begin >= live)
    def _():
        out_ref[...] = jnp.zeros(out_ref.shape, BF16)


def params(**extra):
    return pltpu.CompilerParams(vmem_limit_bytes=VMEM, **extra)


def shards(latents, cache_lat, cache_act, w_in, w_mid, norm_gain, clip_group, band_rows):
    groups = lax.axis_size("seq")
    owners = lax.axis_size("dec")
    clips = latents.shape[1]
    per_owner = latents.shape[2]
    channels = w_mid.shape[2]
    units = groups * per_owner
    height = per_owner * owners
    stack_rows = groups * height
    band_max = 2 * stack_rows // owners
    lat_capacity = (band_max + 4 + owners - 1) // owners
    act_capacity = (band_max + 2 + owners - 1) // owners
    block = 8
    any_space = pl.BlockSpec(memory_space=pl.ANY)
    in_vmem = pl.BlockSpec(memory_space=pltpu.VMEM)

    def rows_first(array):
        return jnp.transpose(array[0, :, :, 0, :], (1, 0, 2))

    lat, old, act = rows_first(latents), rows_first(cache_lat), rows_first(cache_act)
    tiles = act.shape[2] // LANES
    lat_rows = ceil_to(per_owner * 12, 16)
    packed_lat = pl.pallas_call(
        functools.partial(pack_latents, per_owner=per_owner, clips=clips, rows=lat_rows),
        grid_spec=pltpu.PrefetchScalarGridSpec(
            num_scalar_prefetch=1,
            grid=(),
            in_specs=[in_vmem, in_vmem],
            out_specs=in_vmem,
            scratch_shapes=[pltpu.VMEM((clips * lat_rows, LANES), F32)],
        ),
        out_shape=jax.ShapeDtypeStruct((clips, lat_rows, LANES), BF16),
        compiler_params=params(),
        name="pack_latents",
    )(clip_group, lat, old)
    per_step = 3
    packed_act = pl.pallas_call(
        functools.partial(pack_caches, per_step=per_step, clips=clips),
        grid_spec=pltpu.PrefetchScalarGridSpec(
            num_scalar_prefetch=1,
            grid=(per_owner // per_step,),
            in_specs=[
                pl.BlockSpec((per_step, clips, act.shape[2]), lambda step, _: (step, 0, 0))
            ],
            out_specs=pl.BlockSpec(
                (clips, per_step * tiles, LANES), lambda step, _: (0, step, 0)
            ),
            scratch_shapes=[pltpu.VMEM((clips * per_step * tiles, LANES), F32)],
        ),
        out_shape=jax.ShapeDtypeStruct((clips, per_owner * tiles, LANES), BF16),
        compiler_params=params(),
        name="pack_caches",
    )(clip_group, act)

    def exchange(array, axis):
        return lax.all_to_all(array, axis, split_axis=0, concat_axis=0, tiled=True)

    group_lat = exchange(packed_lat, "seq")
    group_act = exchange(packed_act, "seq")
    slice_rows = ceil_to(lat_capacity * 12, 16)
    band_lat = pl.pallas_call(
        functools.partial(
            slice_latents, owners=owners, units=units, capacity=lat_capacity, per_owner=per_owner
        ),
        grid_spec=pltpu.PrefetchScalarGridSpec(
            num_scalar_prefetch=1,
            grid=(),
            in_specs=[in_vmem],
            out_specs=in_vmem,
            scratch_shapes=[pltpu.VMEM((units * 12 + lat_rows + slice_rows, LANES), F32)],
        ),
        out_shape=jax.ShapeDtypeStruct((owners, slice_rows, LANES), BF16),
        compiler_params=params(),
        name="slice_latents",
    )(band_rows, group_lat)
    band_lat = exchange(band_lat, "dec")
    band_act = pl.pallas_call(
        functools.partial(
            slice_caches, owners=owners, units=units, capacity=act_capacity, tiles=tiles
        ),
        grid_spec=pltpu.PrefetchScalarGridSpec(
            num_scalar_prefetch=1,
            grid=(),
            in_specs=[any_space],
            out_specs=any_space,
            scratch_shapes=[pltpu.SemaphoreType.DMA((owners,))],
        ),
        out_shape=jax.ShapeDtypeStruct((owners, act_capacity * tiles, LANES), BF16),
        compiler_params=params(),
        name="slice_caches",
    )(band_rows, group_act.reshape(units * tiles, LANES))
    band_lat, band_act = lax.optimization_barrier((band_lat, band_act))
    band_act = exchange(band_act, "dec")

    ext = band_max + 4
    late, part = pl.pallas_call(
        functools.partial(
            new_frames, owners=owners, units=units, capacity=lat_capacity, height=height,
            block=block, band_max=band_max, channels=channels,
        ),
        grid_spec=pltpu.PrefetchScalarGridSpec(
            num_scalar_prefetch=1,
            grid=(band_max // block,),
            in_specs=[in_vmem, in_vmem, in_vmem, any_space],
            out_specs=[
                pl.BlockSpec((block, 2, COLS, channels), lambda step, _: (step, 1, 0, 0)),
                pl.BlockSpec((block, 2, COLS, channels), lambda step, _: (step, 0, 0, 0)),
            ],
            scratch_shapes=[
                pltpu.VMEM((9 * channels, 3 * channels), BF16),
                pltpu.VMEM((9 * LANES, 4 * channels), BF16),
                pltpu.VMEM((owners * slice_rows + 16, LANES), F32),
                pltpu.VMEM((4, 3, ext * F + 16, LANES), F32),
                pltpu.VMEM((channels // LANES, (ext + block) * F * COLS, LANES), F32),
                pltpu.VMEM((ext + 1, F, COLS, channels), BF16),
                pltpu.SemaphoreType.DMA((27,)),
            ],
        ),
        out_shape=[
            jax.ShapeDtypeStruct((band_max, F, COLS, channels), BF16),
            jax.ShapeDtypeStruct((band_max, 2, COLS, channels), F32),
        ],
        compiler_params=params(dimension_semantics=("arbitrary",)),
        cost_estimate=pl.CostEstimate(
            flops=2 * band_max * 9 * COLS * 9 * channels * channels,
            bytes_accessed=16 * 1024 * 1024,
            transcendentals=0,
        ),
        name="new_frames",
    )(band_rows, band_lat, w_in, norm_gain.reshape(1, channels), w_mid)

    slots = owners * act_capacity
    decoded = pl.pallas_call(
        functools.partial(
            cached_frames, owners=owners, units=units, capacity=act_capacity, height=height,
            block=block, channels=channels,
        ),
        grid_spec=pltpu.PrefetchScalarGridSpec(
            num_scalar_prefetch=1,
            grid=(band_max // block,),
            in_specs=[
                any_space,
                pl.BlockSpec((block, 2, COLS, channels), lambda step, _: (step, 0, 0, 0)),
                any_space,
                any_space,
            ],
            out_specs=pl.BlockSpec(
                (block, 2, COLS, channels), lambda step, _: (step, 0, 0, 0)
            ),
            scratch_shapes=[
                pltpu.VMEM((6 * channels, 3 * channels), BF16),
                pltpu.VMEM((slots + 1, tiles, LANES), BF16),
                pltpu.SemaphoreType.DMA((18,)),
                pltpu.SemaphoreType.DMA,
            ],
        ),
        out_shape=jax.ShapeDtypeStruct((band_max, F, COLS, channels), BF16),
        input_output_aliases={4: 0},
        compiler_params=params(dimension_semantics=("arbitrary",)),
        cost_estimate=pl.CostEstimate(
            flops=2 * band_max * 3 * COLS * 9 * channels * channels,
            bytes_accessed=16 * 1024 * 1024,
            transcendentals=0,
        ),
        name="cached_frames",
    )(band_rows, band_act.reshape(slots, tiles, LANES), part, w_mid, late)
    return decoded.reshape((1, 1) + decoded.shape)


def solution(mesh):
    placed = (
        P("seq", None, None, "dec", None),
        P("seq", None, None, "dec", None),
        P("seq", None, None, "dec", None),
        P(),
        P(),
        P(),
        P(),
        P(),
    )
    return jax.shard_map(
        shards,
        mesh=mesh,
        in_specs=placed,
        out_specs=P("seq", "dec", None, None, None, None),
        check_vma=False,
    )
```

```python
import functools

import jax
import jax.numpy as jnp
from jax import lax
from jax.experimental import pallas as pl
from jax.experimental.pallas import tpu as pltpu
from jax.sharding import PartitionSpec as P

F = 4
CT = 2
COLS = 16
LANES = 128
EPSILON = 1e-06
F32 = jnp.float32
BF16 = jnp.bfloat16


def band_start(bands, group, owner, owners):
    total = jnp.int32(0)
    for other in range(owners):
        total = total + jnp.where(other < owner, bands[group, other], 0)
    return total


def first_unit(start, margin, source, owners, units, capacity):
    unit = (start - margin - source + owners - 1 + 2 * owners) // owners - 2
    return jnp.clip(unit, 0, units - capacity)


def clip_of(groups_ref, shard, group, clips):
    found = jnp.int32(0)
    for clip in range(clips):
        found = found + jnp.where(groups_ref[shard, clip] == group, clip, 0)
    return found


def pick_latents(groups_ref, in_ref, out_ref, scratch, *, per_owner, clips):
    group = lax.axis_index("seq")
    size = per_owner * 12
    for shard in range(clips):
        for row in range(per_owner):
            for frame in range(CT + F):
                for half in range(2):
                    tile = frame * 2 + half
                    value = in_ref[shard, row, :, tile * LANES : (tile + 1) * LANES]
                    at = shard * size + row * 12 + half * (CT + F) + frame
                    scratch[pl.ds(at, clips, stride=clips * size), :] = value.astype(F32)
    parts = []
    for shard in range(clips):
        clip = clip_of(groups_ref, shard, group, clips)
        parts.append(scratch[pl.ds((clip * clips + shard) * size, size), :])
    out_ref[...] = jnp.concatenate(parts, axis=0).astype(BF16)


def pack_caches(groups_ref, act_ref, out_ref, scratch, *, per_step, clips):
    shard = lax.axis_index("seq")
    tiles = act_ref.shape[2] // LANES
    depth = tiles // (CT * COLS)
    for row in range(per_step):
        for frame in range(CT):
            for col in range(COLS):
                for part in range(depth):
                    tile = (frame * COLS + col) * depth + part
                    at = row * tiles + (frame * depth + part) * COLS + col
                    value = act_ref[row, :, tile * LANES : (tile + 1) * LANES]
                    scratch[pl.ds(at, clips, stride=per_step * tiles), :] = value.astype(F32)
    for group in range(clips):
        clip = clip_of(groups_ref, shard, group, clips)
        size = per_step * tiles
        out_ref[group] = scratch[pl.ds(pl.multiple_of(clip * size, 8), size), :].astype(BF16)


def slice_caches(bands, in_ref, out_ref, sems, *, owners, units, capacity, tiles):
    group = lax.axis_index("seq")
    source = lax.axis_index("dec")
    copies = []
    for owner in range(owners):
        start = band_start(bands, group, owner, owners)
        unit = first_unit(start, 1, source, owners, units, capacity)
        copy = pltpu.make_async_copy(
            in_ref.at[pl.ds(pl.multiple_of(unit * tiles, 16), capacity * tiles)],
            out_ref.at[owner],
            sems.at[owner],
        )
        copy.start()
        copies.append(copy)
    for copy in copies:
        copy.wait()


def shift_columns(sums, width):
    rows = sums.shape[0]
    col = lax.rem(lax.broadcasted_iota(jnp.int32, (rows, width), 0), COLS)
    left = pltpu.roll(sums[:, :width], 1, 0)
    right = pltpu.roll(sums[:, 2 * width :], rows - 1, 0)
    total = sums[:, width : 2 * width] + jnp.where(col > 0, left, 0.0)
    return total + jnp.where(col < COLS - 1, right, 0.0)


def new_frames(
    bands, lat_ref, win_ref, gain_ref, mid_ref, out_ref, part_ref,
    weights, table, xs, windows, first, act, sem,
    *, owners, units, height, block, band_max, channels,
):
    group = lax.axis_index("seq")
    owner = lax.axis_index("dec")
    live = bands[group, owner]
    start = band_start(bands, group, owner, owners)
    step = pl.program_id(0)
    ext = band_max + 4
    depth = channels // LANES
    zero_row = ext
    edge = lax.rem(height - lax.rem(start - 1 + height, height), height)

    @pl.when(step == 0)
    def _():
        load = pltpu.make_async_copy(mid_ref, weights, sem)
        load.start()
        table[...] = jnp.zeros(table.shape, BF16)
        for tap in range(9):
            for col in range(4):
                for shift in range(3):
                    table[
                        pl.ds(tap * LANES + (col + shift + 1) * 16, 16),
                        pl.ds(col * channels, channels),
                    ] = win_ref[tap * 3 + shift]
        per_source = lat_ref.shape[1]
        for source in range(owners):
            xs[pl.ds(source * per_source, per_source), :] = lat_ref[source].astype(F32)
        lane = lax.broadcasted_iota(jnp.int32, (8, LANES), 1)

        def fill(row, carry):
            at = jnp.clip(start - 2 + row, 0, units * owners - 1)
            base = lax.rem(at, owners) * per_source + lax.div(at, owners) * 12
            for tap in range(3):
                left = xs[pl.ds(base + tap, 8), :]
                right = xs[pl.ds(base + tap + CT + F, 8), :]
                left_up, left_down = pltpu.roll(left, 32, 1), pltpu.roll(left, 96, 1)
                right_up, right_down = pltpu.roll(right, 32, 1), pltpu.roll(right, 96, 1)
                into = pl.ds(row * F, 8)
                windows[0, tap, into, :] = jnp.where(lane < 32, 0.0, left_up)
                windows[1, tap, into, :] = jnp.where(lane < 96, left_down, right_down)
                windows[2, tap, into, :] = jnp.where(lane < 32, left_up, right_up)
                windows[3, tap, into, :] = jnp.where(lane < 96, right_down, 0.0)
            return carry

        lax.fori_loop(0, ext, fill, 0, unroll=4)
        for tap in range(3):
            for quarter in range(4):
                windows[quarter, tap, pl.ds(ext * F, 16), :] = jnp.zeros((16, LANES), F32)

        rows = ext * F
        at_row = lax.broadcasted_iota(jnp.int32, (rows, LANES), 0) // F
        above = ((at_row != edge) & (at_row != edge + height)).astype(F32)
        below = ((at_row != edge - 1) & (at_row != edge - 1 + height)).astype(F32)

        def convolve(quarter, carry):
            pieces = []
            for tap in range(3):
                for row_tap in range(3):
                    piece = windows[quarter, tap, pl.ds(row_tap * F, rows), :]
                    if row_tap == 0:
                        piece = piece * above
                    if row_tap == 2:
                        piece = piece * below
                    pieces.append(piece.astype(BF16))
            slab = jnp.concatenate(pieces, axis=1)
            for col in range(4):
                sums = jnp.dot(
                    slab, table[:, pl.ds(col * channels, channels)], preferred_element_type=F32
                )
                for part in range(depth):
                    first[part, pl.ds(quarter * 4 + col, rows, stride=COLS), :] = sums[
                        :, part * LANES : (part + 1) * LANES
                    ]
            return carry

        lax.fori_loop(0, 4, convolve, 0)
        gain = gain_ref[...]

        def activate(chunk, carry):
            for at in range(4):
                row = chunk * 4 + at
                into = pl.ds(pl.multiple_of(row * F * COLS, F * COLS), F * COLS)
                value = jnp.concatenate([first[part, into, :] for part in range(depth)], axis=1)
                mean_square = jnp.mean(value * value, axis=-1, keepdims=True)
                value = value * lax.rsqrt(mean_square + EPSILON) * gain
                value = value / (1.0 + jnp.exp(-value))
                act[row] = value.astype(BF16).reshape(F, COLS, channels)
            return carry

        lax.fori_loop(0, lax.div(live + 5, 4), activate, 0)
        act[zero_row] = jnp.zeros((F, COLS, channels), BF16)
        load.wait()

    begin = step * block

    @pl.when(begin < live)
    def _():
        source_rows = [[], [], []]
        for row in range(block):
            at = jnp.minimum(begin + row, live - 1) + 1
            is_first = (at == edge) | (at == edge + height)
            is_last = (at == edge - 1) | (at == edge - 1 + height)
            source_rows[0].append(jnp.where(is_first, zero_row, at - 1))
            source_rows[1].append(at)
            source_rows[2].append(jnp.where(is_last, zero_row, at + 1))

        def slab(frames):
            pieces = []
            for frame, count in frames:
                for row_tap in range(3):
                    parts = [
                        act[at, frame : frame + count].reshape(count * COLS, channels)
                        for at in source_rows[row_tap]
                    ]
                    pieces.append(jnp.concatenate(parts, axis=0))
            return jnp.concatenate(pieces, axis=1)

        def finish(frames, weight_from, frame_from, count):
            sums = jnp.dot(slab(frames), weights[weight_from:, :], preferred_element_type=F32)
            total = shift_columns(sums, channels)
            parts = []
            for row in range(block):
                at = (begin + row + 1) * F * COLS + frame_from * COLS
                into = pl.ds(pl.multiple_of(at, COLS), count * COLS)
                parts.append(
                    jnp.concatenate([first[part, into, :] for part in range(depth)], axis=1)
                )
            return total + jnp.concatenate(parts, axis=0)

        taps = 3 * channels
        late = finish([(0, 2), (1, 2), (2, 2)], 0, 2, 2)
        at_row = lax.broadcasted_iota(jnp.int32, late.shape, 0) // (2 * COLS)
        late = jnp.where(at_row < live - begin, late, 0.0)
        out_ref[...] = late.astype(BF16).reshape(block, 2, COLS, channels)
        part_ref[:, 1] = finish([(0, 1), (1, 1)], taps, 1, 1).reshape(block, COLS, channels)
        part_ref[:, 0] = finish([(0, 1)], 2 * taps, 0, 1).reshape(block, COLS, channels)

    @pl.when(begin >= live)
    def _():
        out_ref[...] = jnp.zeros(out_ref.shape, BF16)


def cached_frames(
    bands, cache_ref, part_ref, mid_ref, late_ref, out_ref, weights, cache, sem, cache_sem,
    *, owners, units, capacity, height, block, channels,
):
    del late_ref
    group = lax.axis_index("seq")
    owner = lax.axis_index("dec")
    live = bands[group, owner]
    start = band_start(bands, group, owner, owners)
    step = pl.program_id(0)
    depth = channels // LANES
    slots = owners * capacity
    edge = lax.rem(height - lax.rem(start - 1 + height, height), height)

    @pl.when(step == 0)
    def _():
        load = pltpu.make_async_copy(cache_ref, cache.at[pl.ds(0, slots)], cache_sem)
        load.start()
        load_mid = pltpu.make_async_copy(mid_ref.at[pl.ds(0, 6 * channels)], weights, sem)
        load_mid.start()
        cache[slots] = jnp.zeros(cache.shape[1:], BF16)
        load.wait()
        load_mid.wait()

    begin = step * block

    @pl.when(begin < live)
    def _():
        def slot_of(at):
            row = jnp.clip(start - 1 + at, 0, units * owners - 1)
            source = lax.rem(row, owners)
            unit = first_unit(start, 1, source, owners, units, capacity)
            return source * capacity + jnp.clip(row // owners - unit, 0, capacity - 1)

        source_rows = [[], [], []]
        for row in range(block):
            at = jnp.minimum(begin + row, live - 1) + 1
            is_first = (at == edge) | (at == edge + height)
            is_last = (at == edge - 1) | (at == edge - 1 + height)
            source_rows[0].append(jnp.where(is_first, slots, slot_of(at - 1)))
            source_rows[1].append(slot_of(at))
            source_rows[2].append(jnp.where(is_last, slots, slot_of(at + 1)))

        def slab(frames):
            pieces = []
            for frame in frames:
                for row_tap in range(3):
                    for part in range(depth):
                        from_tile = (frame * depth + part) * COLS
                        parts = [
                            cache[at, from_tile : from_tile + COLS, :]
                            for at in source_rows[row_tap]
                        ]
                        pieces.append(jnp.concatenate(parts, axis=0))
            return jnp.concatenate(pieces, axis=1)

        at_row = lax.broadcasted_iota(jnp.int32, (block * COLS, channels), 0) // COLS
        taps = 3 * channels
        for frame, frames in ((0, (0, 1)), (1, (1,))):
            sums = jnp.dot(
                slab(frames), weights[: len(frames) * taps, :], preferred_element_type=F32
            )
            total = shift_columns(sums, channels) + part_ref[:, frame].reshape(
                block * COLS, channels
            )
            total = jnp.where(at_row < live - begin, total, 0.0)
            out_ref[:, frame] = total.astype(BF16).reshape(block, COLS, channels)

    @pl.when(begin >= live)
    def _():
        out_ref[...] = jnp.zeros(out_ref.shape, BF16)


def params(mebibytes, **extra):
    return pltpu.CompilerParams(vmem_limit_bytes=mebibytes * 1024 * 1024, **extra)


def shards(latents, cache_lat, cache_act, w_in, w_mid, norm_gain, clip_group, band_rows):
    groups = lax.axis_size("seq")
    owners = lax.axis_size("dec")
    clips = latents.shape[1]
    per_owner = latents.shape[2]
    channels = w_mid.shape[2]
    units = groups * per_owner
    height = per_owner * owners
    stack_rows = groups * height
    band_max = 2 * stack_rows // owners
    act_capacity = (band_max + 2 + owners - 1) // owners
    block = 16 if band_max % 16 == 0 else 8
    any_space = pl.BlockSpec(memory_space=pl.ANY)
    in_vmem = pl.BlockSpec(memory_space=pltpu.VMEM)

    def rows_first(array):
        return jnp.transpose(array[0, :, :, 0, :], (1, 0, 2))

    lat, old, act = rows_first(latents), rows_first(cache_lat), rows_first(cache_act)
    tiles = act.shape[2] // LANES
    mid = w_mid.reshape(9, 3, channels, channels).transpose(0, 2, 1, 3)
    mid = mid.reshape(9 * channels, 3 * channels)
    all_lat = lax.all_gather(jnp.concatenate([old, lat], axis=2), "seq")
    group_lat = pl.pallas_call(
        functools.partial(pick_latents, per_owner=per_owner, clips=clips),
        grid_spec=pltpu.PrefetchScalarGridSpec(
            num_scalar_prefetch=1,
            grid=(),
            in_specs=[in_vmem],
            out_specs=in_vmem,
            scratch_shapes=[
                pltpu.VMEM((clips * units * 12, LANES), F32),
            ],
        ),
        out_shape=jax.ShapeDtypeStruct((units * 12, LANES), BF16),
        compiler_params=params(16),
        name="pick_latents",
    )(clip_group, all_lat)
    group_lat = lax.all_gather(group_lat, "dec")
    per_step = 3
    packed_act = pl.pallas_call(
        functools.partial(pack_caches, per_step=per_step, clips=clips),
        grid_spec=pltpu.PrefetchScalarGridSpec(
            num_scalar_prefetch=1,
            grid=(per_owner // per_step,),
            in_specs=[
                pl.BlockSpec((per_step, clips, act.shape[2]), lambda step, _: (step, 0, 0))
            ],
            out_specs=pl.BlockSpec(
                (clips, per_step * tiles, LANES), lambda step, _: (0, step, 0)
            ),
            scratch_shapes=[pltpu.VMEM((clips * per_step * tiles, LANES), F32)],
        ),
        out_shape=jax.ShapeDtypeStruct((clips, per_owner * tiles, LANES), BF16),
        compiler_params=params(24),
        name="pack_caches",
    )(clip_group, act)

    def exchange(array, axis):
        return lax.all_to_all(array, axis, split_axis=0, concat_axis=0, tiled=True)

    group_act = exchange(packed_act, "seq")
    band_act = pl.pallas_call(
        functools.partial(
            slice_caches, owners=owners, units=units, capacity=act_capacity, tiles=tiles
        ),
        grid_spec=pltpu.PrefetchScalarGridSpec(
            num_scalar_prefetch=1,
            grid=(),
            in_specs=[in_vmem],
            out_specs=any_space,
            scratch_shapes=[pltpu.SemaphoreType.DMA((owners,))],
        ),
        out_shape=jax.ShapeDtypeStruct((owners, act_capacity * tiles, LANES), BF16),
        compiler_params=params(24),
        name="slice_caches",
    )(band_rows, group_act.reshape(units * tiles, LANES))
    group_lat, band_act = lax.optimization_barrier((group_lat, band_act))
    band_act = exchange(band_act, "dec")

    ext = band_max + 4
    late, part = pl.pallas_call(
        functools.partial(
            new_frames, owners=owners, units=units, height=height,
            block=block, band_max=band_max, channels=channels,
        ),
        grid_spec=pltpu.PrefetchScalarGridSpec(
            num_scalar_prefetch=1,
            grid=(band_max // block,),
            in_specs=[in_vmem, in_vmem, in_vmem, any_space],
            out_specs=[
                pl.BlockSpec((block, 2, COLS, channels), lambda step, _: (step, 1, 0, 0)),
                pl.BlockSpec((block, 2, COLS, channels), lambda step, _: (step, 0, 0, 0)),
            ],
            scratch_shapes=[
                pltpu.VMEM((9 * channels, 3 * channels), BF16),
                pltpu.VMEM((9 * LANES, 4 * channels), BF16),
                pltpu.VMEM((owners * units * 12 + 16, LANES), F32),
                pltpu.VMEM((4, 3, ext * F + 16, LANES), F32),
                pltpu.VMEM((channels // LANES, (ext + block) * F * COLS, LANES), F32),
                pltpu.VMEM((ext + 1, F, COLS, channels), BF16),
                pltpu.SemaphoreType.DMA,
            ],
        ),
        out_shape=[
            jax.ShapeDtypeStruct((band_max, F, COLS, channels), BF16),
            jax.ShapeDtypeStruct((band_max, 2, COLS, channels), F32),
        ],
        compiler_params=params(50, dimension_semantics=("arbitrary",)),
        cost_estimate=pl.CostEstimate(
            flops=2 * band_max * 9 * COLS * 9 * channels * channels,
            bytes_accessed=16 * 1024 * 1024,
            transcendentals=0,
        ),
        name="new_frames",
    )(band_rows, group_lat, w_in, norm_gain.reshape(1, channels), mid)

    slots = owners * act_capacity
    decoded = pl.pallas_call(
        functools.partial(
            cached_frames, owners=owners, units=units, capacity=act_capacity, height=height,
            block=block, channels=channels,
        ),
        grid_spec=pltpu.PrefetchScalarGridSpec(
            num_scalar_prefetch=1,
            grid=(band_max // block,),
            in_specs=[
                any_space,
                pl.BlockSpec((block, 2, COLS, channels), lambda step, _: (step, 0, 0, 0)),
                any_space,
                any_space,
            ],
            out_specs=pl.BlockSpec(
                (block, 2, COLS, channels), lambda step, _: (step, 0, 0, 0)
            ),
            scratch_shapes=[
                pltpu.VMEM((6 * channels, 3 * channels), BF16),
                pltpu.VMEM((slots + 1, tiles, LANES), BF16),
                pltpu.SemaphoreType.DMA,
                pltpu.SemaphoreType.DMA,
            ],
        ),
        out_shape=jax.ShapeDtypeStruct((band_max, F, COLS, channels), BF16),
        input_output_aliases={4: 0},
        compiler_params=params(24, dimension_semantics=("arbitrary",)),
        cost_estimate=pl.CostEstimate(
            flops=2 * band_max * 3 * COLS * 9 * channels * channels,
            bytes_accessed=16 * 1024 * 1024,
            transcendentals=0,
        ),
        name="cached_frames",
    )(band_rows, band_act.reshape(slots, tiles, LANES), part, mid, late)
    return decoded.reshape((1, 1) + decoded.shape)


def solution(mesh):
    placed = (
        P("seq", None, None, "dec", None),
        P("seq", None, None, "dec", None),
        P("seq", None, None, "dec", None),
        P(),
        P(),
        P(),
        P(),
        P(),
    )
    return jax.shard_map(
        shards,
        mesh=mesh,
        in_specs=placed,
        out_specs=P("seq", "dec", None, None, None, None),
        check_vma=False,
    )
```

```python
import functools

import jax
import jax.numpy as jnp
from jax import lax
from jax.experimental import pallas as pl
from jax.experimental.pallas import tpu as pltpu
from jax.sharding import PartitionSpec as P

F = 4
CT = 2
COLS = 16
LANES = 128
EPSILON = 1e-06
F32 = jnp.float32
BF16 = jnp.bfloat16


def band_start(bands, group, owner, owners):
    total = jnp.int32(0)
    for other in range(owners):
        total = total + jnp.where(other < owner, bands[group, other], 0)
    return total


def first_unit(start, margin, source, owners, units, capacity):
    unit = (start - margin - source + owners - 1 + 2 * owners) // owners - 2
    return jnp.clip(unit, 0, units - capacity)


def clip_of(groups_ref, shard, group, clips):
    found = jnp.int32(0)
    for clip in range(clips):
        found = found + jnp.where(groups_ref[shard, clip] == group, clip, 0)
    return found


def pack_latents(groups_ref, lat_ref, old_ref, *refs, per_owner, clips):
    *outs, scratch = refs
    shard = lax.axis_index("seq")
    rows = outs[0].shape[0]
    for row in range(per_owner):
        for frame in range(CT + F):
            for half in range(2):
                if frame < CT:
                    tile = frame * 2 + half
                    value = old_ref[row, :, tile * LANES : (tile + 1) * LANES]
                else:
                    tile = (frame - CT) * 2 + half
                    value = lat_ref[row, :, tile * LANES : (tile + 1) * LANES]
                at = row * 12 + half * (CT + F) + frame
                scratch[pl.ds(at, clips, stride=rows), :] = value.astype(F32)
    for other in range(clips):
        clip = clip_of(groups_ref, shard, shard ^ other, clips)
        outs[other][...] = scratch[pl.ds(pl.multiple_of(clip * rows, 8), rows), :].astype(BF16)


def pack_caches(groups_ref, act_ref, *refs, per_step, clips):
    *outs, scratch = refs
    shard = lax.axis_index("seq")
    tiles = act_ref.shape[2] // LANES
    depth = tiles // (CT * COLS)
    size = per_step * tiles
    for row in range(per_step):
        for frame in range(CT):
            for col in range(COLS):
                for part in range(depth):
                    tile = (frame * COLS + col) * depth + part
                    at = row * tiles + (frame * depth + part) * COLS + col
                    value = act_ref[row, :, tile * LANES : (tile + 1) * LANES]
                    scratch[pl.ds(at, clips, stride=size), :] = value.astype(F32)
    for other in range(clips):
        clip = clip_of(groups_ref, shard, shard ^ other, clips)
        outs[other][...] = scratch[pl.ds(pl.multiple_of(clip * size, 8), size), :].astype(BF16)


def slice_latents(bands, *refs, owners, units, capacity, per_owner):
    *ins, out_ref, scratch = refs
    group = lax.axis_index("seq")
    source = lax.axis_index("dec")
    rows = out_ref.shape[1]
    size = per_owner * 12
    for other, in_ref in enumerate(ins):
        scratch[pl.ds((group ^ other) * size, size), :] = in_ref[:size, :].astype(F32)
    value = pltpu.roll(scratch[: units * 12, :], 64, 1)
    lane = lax.broadcasted_iota(jnp.int32, value.shape, 1)
    for width in (32, 16):
        up, down = pltpu.roll(value, width, 1), pltpu.roll(value, LANES - width, 1)
        value = jnp.where(lane & width == 0, down, up)
    scratch[: units * 12, :] = value
    for owner in range(owners):
        start = band_start(bands, group, owner, owners)
        unit = first_unit(start, 2, source, owners, units, capacity)
        out_ref[owner] = scratch[pl.ds(unit * 12, rows), :].astype(BF16)


def slice_caches(bands, *refs, owners, units, capacity, tiles):
    *ins, out_ref, scratch, in_sems, sems = refs
    group = lax.axis_index("seq")
    source = lax.axis_index("dec")
    size = ins[0].shape[0]
    copies = []
    for other, in_ref in enumerate(ins):
        into = pl.ds(pl.multiple_of((group ^ other) * size, 16), size)
        copies.append(pltpu.make_async_copy(in_ref, scratch.at[into], in_sems.at[other]))
    for copy in copies:
        copy.start()
    for copy in copies:
        copy.wait()
    copies = []
    for owner in range(owners):
        start = band_start(bands, group, owner, owners)
        unit = first_unit(start, 1, source, owners, units, capacity)
        copies.append(
            pltpu.make_async_copy(
                scratch.at[pl.ds(pl.multiple_of(unit * tiles, 16), capacity * tiles)],
                out_ref.at[owner],
                sems.at[owner],
            )
        )
    for copy in copies:
        copy.start()
    for copy in copies:
        copy.wait()


def shift_columns(sums, width):
    rows = sums.shape[0]
    col = lax.rem(lax.broadcasted_iota(jnp.int32, (rows, width), 0), COLS)
    left = pltpu.roll(sums[:, :width], 1, 0)
    right = pltpu.roll(sums[:, 2 * width :], rows - 1, 0)
    total = sums[:, width : 2 * width] + jnp.where(col > 0, left, 0.0)
    return total + jnp.where(col < COLS - 1, right, 0.0)


def weight_copies(mid_ref, weights, sems, channels):
    copies = []
    for tap in range(27):
        into = weights.at[
            pl.ds(tap // 3 * channels, channels), pl.ds(tap % 3 * channels, channels)
        ]
        copies.append(pltpu.make_async_copy(mid_ref.at[tap], into, sems.at[tap]))
    return copies


def new_frames(
    bands, lat_ref, win_ref, gain_ref, mid_ref, out_ref, part_ref, early_ref,
    weights, table, xs, windows, first, act, sems, out_sem,
    *, owners, units, capacity, height, block, band_max, channels,
):
    group = lax.axis_index("seq")
    owner = lax.axis_index("dec")
    live = bands[group, owner]
    start = band_start(bands, group, owner, owners)
    step = pl.program_id(0)
    ext = band_max + 4
    zero_row = ext
    edge = lax.rem(height - lax.rem(start - 1 + height, height), height)
    early = pltpu.make_async_copy(weights.at[pl.ds(0, 6 * channels)], early_ref, out_sem)

    def clip_edges(at):
        is_first = (at == edge) | (at == edge + height)
        is_last = (at == edge - 1) | (at == edge - 1 + height)
        return is_first, is_last

    @pl.when(step == 0)
    def _():
        copies = weight_copies(mid_ref, weights, sems, channels)
        for copy in copies:
            copy.start()
        table[...] = jnp.zeros(table.shape, BF16)
        for time_tap in range(3):
            for row_tap in range(3):
                for col_tap in range(3):
                    into = row_tap * 2 * LANES + (0, 64, LANES)[time_tap]
                    into += ((0, 112, 96), (0, -16, -32), (0, 112, 96))[time_tap][col_tap]
                    table[pl.ds(into, 16), :] = win_ref[time_tap * 9 + row_tap * 3 + col_tap]
        per_source = lat_ref.shape[1]
        for source in range(owners):
            value = lat_ref[source].astype(F32)
            xs[0, pl.ds(source * per_source, per_source), :] = value
            xs[1, pl.ds(source * per_source, per_source), :] = pltpu.roll(value, 64, 1)
        windows[zero_row] = jnp.zeros(windows.shape[1:], BF16)
        act[zero_row] = jnp.zeros((F, COLS, channels), BF16)
        lane = lax.broadcasted_iota(jnp.int32, (8, LANES), 1)
        col = lax.broadcasted_iota(jnp.int32, (8, LANES), 0)
        low = (lane < 16) | (lane >= 96)
        left_end = (col == 0) & ((lane & 63) < 16)
        right_end = (col == 7) & ((lane & 63) >= 32) & ((lane & 63) < 48)

        def fill(chunk, carry):
            for at in range(4):
                row = chunk * 4 + at
                stack_row = jnp.clip(start - 2 + row, 0, units * owners - 1)
                source = lax.rem(stack_row, owners)
                unit = first_unit(start, 2, source, owners, units, capacity)
                slot = jnp.clip(lax.div(stack_row, owners) - unit, 0, capacity - 1)
                base = source * per_source + slot * 12
                at_low, at_high = {}, {}
                for frame in range(CT + F):
                    for half in range(2):
                        at_row = pl.ds(base + half * (CT + F) + frame, 1)
                        for rolled, into in enumerate((at_low, at_high)):
                            value = jnp.broadcast_to(xs[rolled, at_row, :], (8, LANES))
                            into[half, frame] = pltpu.roll(value, 0, 1, stride=16, stride_axis=0)
                for frame in range(F):
                    pair = [
                        jnp.where(low, at_low[half, frame], at_high[half, frame + 1])
                        for half in range(2)
                    ]
                    last = [at_low[half, frame + 2] for half in range(2)]
                    for lanes, (left, right) in enumerate((pair, last)):
                        near = jnp.where(left_end, 0.0, jnp.where(right_end, right, left))
                        far = jnp.where(right_end, 0.0, jnp.where(left_end, left, right))
                        windows[
                            row,
                            frame * COLS : (frame + 1) * COLS,
                            lanes * LANES : (lanes + 1) * LANES,
                        ] = jnp.concatenate([near, far], axis=0).astype(BF16)
            return carry

        lax.fori_loop(0, lax.div(live + 7, 4), fill, 0)
        gain = gain_ref[...]

        def activate(chunk, carry):
            source_rows = [[], [], []]
            for at in range(4):
                row = chunk * 4 + at
                is_first, is_last = clip_edges(row)
                source_rows[0].append(jnp.where(is_first, zero_row, row))
                source_rows[1].append(jnp.minimum(row + 1, ext - 1))
                source_rows[2].append(jnp.where(is_last, zero_row, jnp.minimum(row + 2, ext - 1)))
            slab = jnp.concatenate(
                [
                    jnp.concatenate([windows[at] for at in source_rows[row_tap]], axis=0)
                    for row_tap in range(3)
                ],
                axis=1,
            )
            size = F * COLS
            sums = jnp.dot(slab, table[...], preferred_element_type=F32)
            first[pl.ds(pl.multiple_of(chunk * 4 * size, size), 4 * size), :] = sums
            for at in range(4):
                value = sums[at * size : (at + 1) * size]
                mean_square = jnp.mean(value * value, axis=-1, keepdims=True)
                value = value * lax.rsqrt(mean_square + EPSILON) * gain
                value = value / (1.0 + jnp.exp(-value))
                act[chunk * 4 + at] = value.astype(BF16).reshape(F, COLS, channels)
            return carry

        lax.fori_loop(0, lax.div(live + 5, 4), activate, 0)
        for copy in copies:
            copy.wait()
        early.start()

    @pl.when(step == pl.num_programs(0) - 1)
    def _():
        early.wait()

    begin = step * block

    @pl.when(begin < live)
    def _():
        source_rows = [[], [], []]
        for row in range(block):
            at = jnp.minimum(begin + row, live - 1) + 1
            is_first, is_last = clip_edges(at)
            source_rows[0].append(jnp.where(is_first, zero_row, at - 1))
            source_rows[1].append(at)
            source_rows[2].append(jnp.where(is_last, zero_row, at + 1))

        def slab(frames):
            pieces = []
            for frame, count in frames:
                for row_tap in range(3):
                    parts = [
                        act[at, frame : frame + count].reshape(count * COLS, channels)
                        for at in source_rows[row_tap]
                    ]
                    pieces.append(jnp.concatenate(parts, axis=0))
            return jnp.concatenate(pieces, axis=1)

        def finish(frames, weight_from, frame_from, count):
            sums = jnp.dot(slab(frames), weights[weight_from:, :], preferred_element_type=F32)
            total = shift_columns(sums, channels)
            parts = []
            for row in range(block):
                at = (begin + row + 1) * F * COLS + frame_from * COLS
                into = pl.ds(pl.multiple_of(at, COLS), count * COLS)
                parts.append(first[into, :])
            return total + jnp.concatenate(parts, axis=0)

        taps = 3 * channels
        late = finish([(0, 2), (1, 2), (2, 2)], 0, 2, 2)
        at_row = lax.broadcasted_iota(jnp.int32, late.shape, 0) // (2 * COLS)
        late = jnp.where(at_row < live - begin, late, 0.0)
        out_ref[...] = late.astype(BF16).reshape(block, 2, COLS, channels)
        part_ref[:, 1] = finish([(0, 1), (1, 1)], taps, 1, 1).reshape(block, COLS, channels)
        part_ref[:, 0] = finish([(0, 1)], 2 * taps, 0, 1).reshape(block, COLS, channels)

    @pl.when(begin >= live)
    def _():
        out_ref[...] = jnp.zeros(out_ref.shape, BF16)


def cached_frames(
    bands, cache_ref, part_ref, mid_ref, late_ref, out_ref, weights, cache, sem, cache_sem,
    *, owners, units, capacity, height, block, channels,
):
    del late_ref
    group = lax.axis_index("seq")
    owner = lax.axis_index("dec")
    live = bands[group, owner]
    start = band_start(bands, group, owner, owners)
    step = pl.program_id(0)
    depth = channels // LANES
    slots = owners * capacity
    edge = lax.rem(height - lax.rem(start - 1 + height, height), height)

    @pl.when(step == 0)
    def _():
        load = pltpu.make_async_copy(cache_ref, cache.at[pl.ds(0, slots)], cache_sem)
        load.start()
        load_mid = pltpu.make_async_copy(mid_ref, weights, sem)
        load_mid.start()
        cache[slots] = jnp.zeros(cache.shape[1:], BF16)
        load.wait()
        load_mid.wait()

    begin = step * block

    @pl.when(begin < live)
    def _():
        def slot_of(at):
            row = jnp.clip(start - 1 + at, 0, units * owners - 1)
            source = lax.rem(row, owners)
            unit = first_unit(start, 1, source, owners, units, capacity)
            return source * capacity + jnp.clip(row // owners - unit, 0, capacity - 1)

        source_rows = [[], [], []]
        for row in range(block):
            at = jnp.minimum(begin + row, live - 1) + 1
            is_first = (at == edge) | (at == edge + height)
            is_last = (at == edge - 1) | (at == edge - 1 + height)
            source_rows[0].append(jnp.where(is_first, slots, slot_of(at - 1)))
            source_rows[1].append(slot_of(at))
            source_rows[2].append(jnp.where(is_last, slots, slot_of(at + 1)))

        def slab(frames):
            pieces = []
            for frame in frames:
                for row_tap in range(3):
                    for part in range(depth):
                        from_tile = (frame * depth + part) * COLS
                        parts = [
                            cache[at, from_tile : from_tile + COLS, :]
                            for at in source_rows[row_tap]
                        ]
                        pieces.append(jnp.concatenate(parts, axis=0))
            return jnp.concatenate(pieces, axis=1)

        at_row = lax.broadcasted_iota(jnp.int32, (block * COLS, channels), 0) // COLS
        taps = 3 * channels
        for frame, frames in ((0, (0, 1)), (1, (1,))):
            sums = jnp.dot(
                slab(frames), weights[: len(frames) * taps, :], preferred_element_type=F32
            )
            total = shift_columns(sums, channels) + part_ref[:, frame].reshape(
                block * COLS, channels
            )
            total = jnp.where(at_row < live - begin, total, 0.0)
            out_ref[:, frame] = total.astype(BF16).reshape(block, COLS, channels)

    @pl.when(begin >= live)
    def _():
        out_ref[...] = jnp.zeros(out_ref.shape, BF16)


def params(mebibytes, **extra):
    return pltpu.CompilerParams(vmem_limit_bytes=mebibytes * 1024 * 1024, **extra)


def shards(latents, cache_lat, cache_act, w_in, w_mid, norm_gain, clip_group, band_rows):
    groups = lax.axis_size("seq")
    owners = lax.axis_size("dec")
    clips = latents.shape[1]
    per_owner = latents.shape[2]
    channels = w_mid.shape[2]
    units = groups * per_owner
    height = per_owner * owners
    stack_rows = groups * height
    band_max = 2 * stack_rows // owners
    act_capacity = (band_max + 2 + owners - 1) // owners
    block = 16 if band_max % 16 == 0 else 8
    any_space = pl.BlockSpec(memory_space=pl.ANY)
    in_vmem = pl.BlockSpec(memory_space=pltpu.VMEM)

    def rows_first(array):
        return jnp.transpose(array[0, :, :, 0, :], (1, 0, 2))

    lat, old, act = rows_first(latents), rows_first(cache_lat), rows_first(cache_act)
    tiles = act.shape[2] // LANES
    lat_rows = (per_owner * 12 + 15) // 16 * 16
    packed_lat = pl.pallas_call(
        functools.partial(pack_latents, per_owner=per_owner, clips=clips),
        grid_spec=pltpu.PrefetchScalarGridSpec(
            num_scalar_prefetch=1,
            grid=(),
            in_specs=[in_vmem, in_vmem],
            out_specs=[in_vmem] * clips,
            scratch_shapes=[pltpu.VMEM((clips * lat_rows, LANES), F32)],
        ),
        out_shape=[jax.ShapeDtypeStruct((lat_rows, LANES), BF16)] * clips,
        compiler_params=params(16),
        name="pack_latents",
    )(clip_group, lat, old)

    def trade(parts):
        return [parts[0]] + [
            lax.ppermute(part, "seq", [(i, i ^ other) for i in range(groups)])
            for other, part in enumerate(parts)
            if other
        ]

    per_step = 3
    packed_act = pl.pallas_call(
        functools.partial(pack_caches, per_step=per_step, clips=clips),
        grid_spec=pltpu.PrefetchScalarGridSpec(
            num_scalar_prefetch=1,
            grid=(per_owner // per_step,),
            in_specs=[
                pl.BlockSpec((per_step, clips, act.shape[2]), lambda step, _: (step, 0, 0))
            ],
            out_specs=[pl.BlockSpec((per_step * tiles, LANES), lambda step, _: (step, 0))] * clips,
            scratch_shapes=[pltpu.VMEM((clips * per_step * tiles, LANES), F32)],
        ),
        out_shape=[jax.ShapeDtypeStruct((per_owner * tiles, LANES), BF16)] * clips,
        compiler_params=params(24),
        name="pack_caches",
    )(clip_group, act)

    def exchange(array, axis):
        return lax.all_to_all(array, axis, split_axis=0, concat_axis=0, tiled=True)

    lat_capacity = (band_max + 4 + owners - 1) // owners
    slice_rows = (lat_capacity * 12 + 15) // 16 * 16
    band_lat = pl.pallas_call(
        functools.partial(
            slice_latents, owners=owners, units=units, capacity=lat_capacity, per_owner=per_owner
        ),
        grid_spec=pltpu.PrefetchScalarGridSpec(
            num_scalar_prefetch=1,
            grid=(),
            in_specs=[in_vmem] * clips,
            out_specs=in_vmem,
            scratch_shapes=[pltpu.VMEM((units * 12 + slice_rows, LANES), F32)],
        ),
        out_shape=jax.ShapeDtypeStruct((owners, slice_rows, LANES), BF16),
        compiler_params=params(16),
        name="slice_latents",
    )(band_rows, *trade(packed_lat))
    band_lat = exchange(band_lat, "dec")
    band_act = pl.pallas_call(
        functools.partial(
            slice_caches, owners=owners, units=units, capacity=act_capacity, tiles=tiles
        ),
        grid_spec=pltpu.PrefetchScalarGridSpec(
            num_scalar_prefetch=1,
            grid=(),
            in_specs=[any_space] * clips,
            out_specs=any_space,
            scratch_shapes=[
                pltpu.VMEM((units * tiles, LANES), BF16),
                pltpu.SemaphoreType.DMA((clips,)),
                pltpu.SemaphoreType.DMA((owners,)),
            ],
        ),
        out_shape=jax.ShapeDtypeStruct((owners, act_capacity * tiles, LANES), BF16),
        compiler_params=params(16),
        name="slice_caches",
    )(band_rows, *trade(packed_act))
    band_lat, band_act = lax.optimization_barrier((band_lat, band_act))
    band_act = exchange(band_act, "dec")

    ext = band_max + 4
    late, part, early_mid = pl.pallas_call(
        functools.partial(
            new_frames, owners=owners, units=units, capacity=lat_capacity, height=height,
            block=block, band_max=band_max, channels=channels,
        ),
        grid_spec=pltpu.PrefetchScalarGridSpec(
            num_scalar_prefetch=1,
            grid=(band_max // block,),
            in_specs=[in_vmem, in_vmem, in_vmem, any_space],
            out_specs=[
                pl.BlockSpec((block, 2, COLS, channels), lambda step, _: (step, 1, 0, 0)),
                pl.BlockSpec((block, 2, COLS, channels), lambda step, _: (step, 0, 0, 0)),
                any_space,
            ],
            scratch_shapes=[
                pltpu.VMEM((9 * channels, 3 * channels), BF16),
                pltpu.VMEM((6 * LANES, channels), BF16),
                pltpu.VMEM((2, owners * slice_rows, LANES), F32),
                pltpu.VMEM((ext + 1, F * COLS, 2 * LANES), BF16),
                pltpu.VMEM(((ext + block) * F * COLS, channels), F32),
                pltpu.VMEM((ext + 1, F, COLS, channels), BF16),
                pltpu.SemaphoreType.DMA((27,)),
                pltpu.SemaphoreType.DMA,
            ],
        ),
        out_shape=[
            jax.ShapeDtypeStruct((band_max, F, COLS, channels), BF16),
            jax.ShapeDtypeStruct((band_max, 2, COLS, channels), F32),
            jax.ShapeDtypeStruct((6 * channels, 3 * channels), BF16),
        ],
        compiler_params=params(50, dimension_semantics=("arbitrary",)),
        cost_estimate=pl.CostEstimate(
            flops=2 * band_max * 9 * COLS * 9 * channels * channels,
            bytes_accessed=16 * 1024 * 1024,
            transcendentals=0,
        ),
        name="new_frames",
    )(band_rows, band_lat, w_in, norm_gain.reshape(1, channels), w_mid)

    slots = owners * act_capacity
    decoded = pl.pallas_call(
        functools.partial(
            cached_frames, owners=owners, units=units, capacity=act_capacity, height=height,
            block=block, channels=channels,
        ),
        grid_spec=pltpu.PrefetchScalarGridSpec(
            num_scalar_prefetch=1,
            grid=(band_max // block,),
            in_specs=[
                any_space,
                pl.BlockSpec((block, 2, COLS, channels), lambda step, _: (step, 0, 0, 0)),
                any_space,
                any_space,
            ],
            out_specs=pl.BlockSpec(
                (block, 2, COLS, channels), lambda step, _: (step, 0, 0, 0)
            ),
            scratch_shapes=[
                pltpu.VMEM((6 * channels, 3 * channels), BF16),
                pltpu.VMEM((slots + 1, tiles, LANES), BF16),
                pltpu.SemaphoreType.DMA,
                pltpu.SemaphoreType.DMA,
            ],
        ),
        out_shape=jax.ShapeDtypeStruct((band_max, F, COLS, channels), BF16),
        input_output_aliases={4: 0},
        compiler_params=params(24, dimension_semantics=("arbitrary",)),
        cost_estimate=pl.CostEstimate(
            flops=2 * band_max * 3 * COLS * 9 * channels * channels,
            bytes_accessed=16 * 1024 * 1024,
            transcendentals=0,
        ),
        name="cached_frames",
    )(band_rows, band_act.reshape(slots, tiles, LANES), part, early_mid, late)
    return decoded.reshape((1, 1) + decoded.shape)


def solution(mesh):
    placed = (
        P("seq", None, None, "dec", None),
        P("seq", None, None, "dec", None),
        P("seq", None, None, "dec", None),
        P(),
        P(),
        P(),
        P(),
        P(),
    )
    return jax.shard_map(
        shards,
        mesh=mesh,
        in_specs=placed,
        out_specs=P("seq", "dec", None, None, None, None),
        check_vma=False,
    )
```

```python
import functools

import jax
import jax.numpy as jnp
from jax import lax
from jax.experimental import pallas as pl
from jax.experimental.pallas import tpu as pltpu
from jax.sharding import PartitionSpec as P

F = 4
CT = 2
COLS = 16
LANES = 128
EPSILON = 1e-06
F32 = jnp.float32
BF16 = jnp.bfloat16


def band_start(bands, group, owner, owners):
    total = jnp.int32(0)
    for other in range(owners):
        total = total + jnp.where(other < owner, bands[group, other], 0)
    return total


def first_unit(start, margin, source, owners, units, capacity):
    unit = (start - margin - source + owners - 1 + 2 * owners) // owners - 2
    return jnp.clip(unit, 0, units - capacity)


def clip_of(groups_ref, shard, group, clips):
    found = jnp.int32(0)
    for clip in range(clips):
        found = found + jnp.where(groups_ref[shard, clip] == group, clip, 0)
    return found


def pack_latents(groups_ref, lat_in, old_in, *refs, per_owner, clips):
    *outs, lat_ref, old_ref, scratch, sems = refs
    shard = lax.axis_index("seq")
    copies = [
        pltpu.make_async_copy(lat_in, lat_ref, sems.at[0]),
        pltpu.make_async_copy(old_in, old_ref, sems.at[1]),
    ]
    for copy in copies:
        copy.start()
    for copy in copies:
        copy.wait()
    rows = outs[0].shape[0]
    for row in range(per_owner):
        for frame in range(CT + F):
            for half in range(2):
                if frame < CT:
                    tile = frame * 2 + half
                    value = old_ref[row, :, tile * LANES : (tile + 1) * LANES]
                else:
                    tile = (frame - CT) * 2 + half
                    value = lat_ref[row, :, tile * LANES : (tile + 1) * LANES]
                at = row * 12 + half * (CT + F) + frame
                scratch[pl.ds(at, clips, stride=rows), :] = value.astype(F32)
    for other in range(clips):
        clip = clip_of(groups_ref, shard, shard ^ other, clips)
        outs[other][...] = scratch[pl.ds(pl.multiple_of(clip * rows, 8), rows), :].astype(BF16)


def pack_caches(groups_ref, act_ref, *refs, per_step, clips):
    *outs, scratch = refs
    shard = lax.axis_index("seq")
    tiles = act_ref.shape[2] // LANES
    depth = tiles // (CT * COLS)
    size = per_step * tiles
    for row in range(per_step):
        for frame in range(CT):
            for col in range(COLS):
                for part in range(depth):
                    tile = (frame * COLS + col) * depth + part
                    at = row * tiles + (frame * depth + part) * COLS + col
                    value = act_ref[row, :, tile * LANES : (tile + 1) * LANES]
                    scratch[pl.ds(at, clips, stride=size), :] = value.astype(F32)
    for other in range(clips):
        clip = clip_of(groups_ref, shard, shard ^ other, clips)
        outs[other][...] = scratch[pl.ds(pl.multiple_of(clip * size, 8), size), :].astype(BF16)


def slice_latents(bands, *refs, owners, units, capacity, per_owner):
    *ins, out_ref, scratch = refs
    group = lax.axis_index("seq")
    source = lax.axis_index("dec")
    rows = out_ref.shape[1]
    size = per_owner * 12
    for other, in_ref in enumerate(ins):
        scratch[pl.ds((group ^ other) * size, size), :] = in_ref[:size, :].astype(F32)
    value = pltpu.roll(scratch[: units * 12, :], 64, 1)
    lane = lax.broadcasted_iota(jnp.int32, value.shape, 1)
    for width in (32, 16):
        up, down = pltpu.roll(value, width, 1), pltpu.roll(value, LANES - width, 1)
        value = jnp.where(lane & width == 0, down, up)
    scratch[: units * 12, :] = value
    for owner in range(owners):
        start = band_start(bands, group, owner, owners)
        unit = first_unit(start, 2, source, owners, units, capacity)
        out_ref[owner] = scratch[pl.ds(unit * 12, rows), :].astype(BF16)


def slice_caches(bands, *refs, owners, units, capacity, tiles):
    *ins, out_ref, scratch, in_sems, sems = refs
    group = lax.axis_index("seq")
    source = lax.axis_index("dec")
    size = ins[0].shape[0]
    copies = []
    for other, in_ref in enumerate(ins):
        into = pl.ds(pl.multiple_of((group ^ other) * size, 16), size)
        copies.append(pltpu.make_async_copy(in_ref, scratch.at[into], in_sems.at[other]))
    for copy in copies:
        copy.start()
    for copy in copies:
        copy.wait()
    copies = []
    for owner in range(owners):
        start = band_start(bands, group, owner, owners)
        unit = first_unit(start, 1, source, owners, units, capacity)
        copies.append(
            pltpu.make_async_copy(
                scratch.at[pl.ds(pl.multiple_of(unit * tiles, 16), capacity * tiles)],
                out_ref.at[owner],
                sems.at[owner],
            )
        )
    for copy in copies:
        copy.start()
    for copy in copies:
        copy.wait()


def shift_columns(sums, width):
    rows = sums.shape[0]
    col = lax.rem(lax.broadcasted_iota(jnp.int32, (rows, width), 0), COLS)
    left = pltpu.roll(sums[:, :width], 1, 0)
    right = pltpu.roll(sums[:, 2 * width :], rows - 1, 0)
    total = sums[:, width : 2 * width] + jnp.where(col > 0, left, 0.0)
    return total + jnp.where(col < COLS - 1, right, 0.0)


def weight_copies(mid_ref, weights, sems, channels):
    copies = []
    for tap in range(27):
        into = weights.at[
            pl.ds(tap // 3 * channels, channels), pl.ds(tap % 3 * channels, channels)
        ]
        copies.append(pltpu.make_async_copy(mid_ref.at[tap], into, sems.at[tap]))
    return copies


def new_frames(
    bands, lat_ref, win_ref, gain_ref, mid_ref, out_ref, part_ref, weights,
    table, xs, windows_a, windows_b, first_a, first_b, act_a, act_b, late, sems, out_sems,
    *, owners, units, capacity, height, block, band_max, channels,
):
    group = lax.axis_index("seq")
    owner = lax.axis_index("dec")
    live = bands[group, owner]
    start = band_start(bands, group, owner, owners)
    edge = lax.rem(height - lax.rem(start - 1 + height, height), height)
    blocks = band_max // block
    size = F * COLS
    per_source = lat_ref.shape[1]
    copies = weight_copies(mid_ref, weights, sems, channels)
    for copy in copies:
        copy.start()
    table[...] = jnp.zeros(table.shape, BF16)
    for time_tap in range(3):
        for row_tap in range(3):
            for col_tap in range(3):
                into = row_tap * 2 * LANES + (0, 64, LANES)[time_tap]
                into += ((0, 112, 96), (0, -16, -32), (0, 112, 96))[time_tap][col_tap]
                table[pl.ds(into, 16), :] = win_ref[time_tap * 9 + row_tap * 3 + col_tap]
    for source in range(owners):
        value = lat_ref[source].astype(F32)
        xs[0, pl.ds(source * per_source, per_source), :] = value
        xs[1, pl.ds(source * per_source, per_source), :] = pltpu.roll(value, 64, 1)
    window_zero, act_zero = block + 4, block + 2
    for windows in (windows_a, windows_b):
        windows[window_zero] = jnp.zeros(windows.shape[1:], BF16)
    for act in (act_a, act_b):
        act[act_zero] = jnp.zeros((F, COLS, channels), BF16)
    gain = gain_ref[...]

    def clip_edges(at):
        is_first = (at == edge) | (at == edge + height)
        is_last = (at == edge - 1) | (at == edge - 1 + height)
        return is_first, is_last

    def fill(row, windows, into):
        lane = lax.broadcasted_iota(jnp.int32, (8, LANES), 1)
        col = lax.broadcasted_iota(jnp.int32, (8, LANES), 0)
        low = (lane < 16) | (lane >= 96)
        left_end = (col == 0) & ((lane & 63) < 16)
        right_end = (col == 7) & ((lane & 63) >= 32) & ((lane & 63) < 48)
        stack_row = jnp.clip(start - 2 + row, 0, units * owners - 1)
        source = lax.rem(stack_row, owners)
        unit = first_unit(start, 2, source, owners, units, capacity)
        slot = jnp.clip(lax.div(stack_row, owners) - unit, 0, capacity - 1)
        base = source * per_source + slot * 12
        rolled = [{}, {}]
        for frame in range(CT + F):
            for half in range(2):
                at_row = pl.ds(base + half * (CT + F) + frame, 1)
                for turn in range(2):
                    if turn == 1 and not 1 <= frame <= F:
                        continue
                    value = jnp.broadcast_to(xs[turn, at_row, :], (8, LANES))
                    rolled[turn][half, frame] = pltpu.roll(value, 0, 1, stride=16, stride_axis=0)
        for frame in range(F):
            pair = [
                jnp.where(low, rolled[0][half, frame], rolled[1][half, frame + 1])
                for half in range(2)
            ]
            last = [rolled[0][half, frame + 2] for half in range(2)]
            for lanes, (left, right) in enumerate((pair, last)):
                near = jnp.where(left_end, 0.0, jnp.where(right_end, right, left))
                far = jnp.where(right_end, 0.0, jnp.where(left_end, left, right))
                windows[
                    into,
                    frame * COLS : (frame + 1) * COLS,
                    lanes * LANES : (lanes + 1) * LANES,
                ] = jnp.concatenate([near, far], axis=0).astype(BF16)

    def produce(row, count, into, windows, first, act):
        for at in range(count + 2):
            fill(row + at, windows, at)
        pieces = [[], [], []]
        for at in range(count):
            is_first, is_last = clip_edges(row + at)
            pieces[0].append(windows[jnp.where(is_first, window_zero, at)])
            pieces[1].append(windows[at + 1])
            pieces[2].append(windows[jnp.where(is_last, window_zero, at + 2)])
        slab = jnp.concatenate([jnp.concatenate(part, axis=0) for part in pieces], axis=1)
        sums = jnp.dot(slab, table[...], preferred_element_type=F32)
        first[into * size : (into + count) * size, :] = sums
        for at in range(count):
            value = sums[at * size : (at + 1) * size]
            mean_square = jnp.mean(value * value, axis=-1, keepdims=True)
            value = value * lax.rsqrt(mean_square + EPSILON) * gain
            value = value / (1.0 + jnp.exp(-value))
            act[into + at] = value.astype(BF16).reshape(F, COLS, channels)

    def copy_out(number):
        rows = pl.ds(number * block, block)
        return pltpu.make_async_copy(
            late.at[rows], out_ref.at[rows, pl.ds(2, 2)], out_sems.at[number]
        )

    def convolve(number, first, act):
        begin = number * block
        source_rows = [[], [], []]
        for row in range(block):
            is_first, is_last = clip_edges(begin + row + 1)
            source_rows[0].append(jnp.where(is_first, act_zero, row))
            source_rows[1].append(row + 1)
            source_rows[2].append(jnp.where(is_last, act_zero, row + 2))

        def finish(frames, weight_from, frame_from, count):
            pieces = []
            for frame in frames:
                for row_tap in range(3):
                    parts = [
                        act[at, frame : frame + count].reshape(count * COLS, channels)
                        for at in source_rows[row_tap]
                    ]
                    pieces.append(jnp.concatenate(parts, axis=0))
            slab = jnp.concatenate(pieces, axis=1)
            sums = jnp.dot(slab, weights[weight_from:, :], preferred_element_type=F32)
            total = shift_columns(sums, channels)
            parts = []
            for row in range(block):
                at = (row + 1) * size + frame_from * COLS
                parts.append(first[at : at + count * COLS, :])
            return total + jnp.concatenate(parts, axis=0)

        taps = 3 * channels
        rows = pl.ds(begin, block)
        value = finish([0, 1, 2], 0, 2, 2)
        at_row = lax.broadcasted_iota(jnp.int32, value.shape, 0) // (2 * COLS)
        value = jnp.where(at_row < live - begin, value, 0.0)
        late[rows] = value.astype(BF16).reshape(block, 2, COLS, channels)
        part_ref[rows, 1] = finish([0, 1], taps, 1, 1).reshape(block, COLS, channels)
        part_ref[rows, 0] = finish([0], 2 * taps, 0, 1).reshape(block, COLS, channels)

    def step(number, first, act, next_windows, next_first, next_act):
        convolve(number, first, act)
        for row in range(2):
            next_act[row] = act[block + row]
        next_first[: 2 * size, :] = first[block * size :, :]
        produce((number + 1) * block + 2, block, 2, next_windows, next_first, next_act)
        copy_out(number).start()

    produce(0, block + 2, 0, windows_a, first_a, act_a)
    for copy in copies:
        copy.wait()
    used = lax.div(live + block - 1, block)

    def two_steps(pair, carry):
        step(2 * pair, first_a, act_a, windows_b, first_b, act_b)

        @pl.when(2 * pair + 1 < used)
        def _():
            step(2 * pair + 1, first_b, act_b, windows_a, first_a, act_a)

        return carry

    lax.fori_loop(0, lax.div(used + 1, 2), two_steps, 0)

    def clear(number, carry):
        late[pl.ds(number * block, block)] = jnp.zeros((block, 2, COLS, channels), BF16)
        copy_out(number).start()
        return carry

    lax.fori_loop(used, blocks, clear, 0)
    for number in range(blocks):
        copy_out(number).wait()


def cached_frames(
    bands, cache, part_ref, weights, late_ref, out_ref, early, out_sems,
    *, owners, units, capacity, height, block, band_max, channels,
):
    del late_ref
    group = lax.axis_index("seq")
    owner = lax.axis_index("dec")
    live = bands[group, owner]
    start = band_start(bands, group, owner, owners)
    depth = channels // LANES
    blocks = band_max // block
    edge = lax.rem(height - lax.rem(start - 1 + height, height), height)

    def slot_of(at):
        row = jnp.clip(start - 1 + at, 0, units * owners - 1)
        source = lax.rem(row, owners)
        unit = first_unit(start, 1, source, owners, units, capacity)
        return source * capacity + jnp.clip(lax.div(row, owners) - unit, 0, capacity - 1)

    def copy_out(number):
        rows = pl.ds(number * block, block)
        return pltpu.make_async_copy(
            early.at[rows], out_ref.at[rows, pl.ds(0, 2)], out_sems.at[number]
        )

    def convolve(number, carry):
        begin = number * block
        edges, source_rows = [[], [], []], [[], [], []]
        for row in range(block):
            at = begin + row + 1
            edges[0].append((at == edge) | (at == edge + height))
            edges[1].append(None)
            edges[2].append((at == edge - 1) | (at == edge - 1 + height))
            for row_tap in range(3):
                source_rows[row_tap].append(slot_of(at + row_tap - 1))

        def slab(frames):
            pieces = []
            for frame in frames:
                for row_tap in range(3):
                    for part in range(depth):
                        from_tile = (frame * depth + part) * COLS
                        parts = []
                        for at, outside in zip(source_rows[row_tap], edges[row_tap]):
                            value = cache[at, from_tile : from_tile + COLS, :]
                            if outside is not None:
                                value = jnp.where(outside, jnp.zeros_like(value), value)
                            parts.append(value)
                        pieces.append(jnp.concatenate(parts, axis=0))
            return jnp.concatenate(pieces, axis=1)

        at_row = lax.broadcasted_iota(jnp.int32, (block * COLS, channels), 0) // COLS
        taps = 3 * channels
        rows = pl.ds(begin, block)
        for frame, frames in ((0, (0, 1)), (1, (1,))):
            sums = jnp.dot(
                slab(frames), weights[: len(frames) * taps, :], preferred_element_type=F32
            )
            total = shift_columns(sums, channels) + part_ref[rows, frame].reshape(
                block * COLS, channels
            )
            total = jnp.where(at_row < live - begin, total, 0.0)
            early[rows, frame] = total.astype(BF16).reshape(block, COLS, channels)
        copy_out(number).start()
        return carry

    used = lax.div(live + block - 1, block)
    lax.fori_loop(0, used, convolve, 0)

    def clear(number, carry):
        early[pl.ds(number * block, block)] = jnp.zeros((block, 2, COLS, channels), BF16)
        copy_out(number).start()
        return carry

    lax.fori_loop(used, blocks, clear, 0)
    for number in range(blocks):
        copy_out(number).wait()


def params(mebibytes, **extra):
    return pltpu.CompilerParams(vmem_limit_bytes=mebibytes * 1024 * 1024, **extra)


def shards(latents, cache_lat, cache_act, w_in, w_mid, norm_gain, clip_group, band_rows):
    groups = lax.axis_size("seq")
    owners = lax.axis_size("dec")
    clips = latents.shape[1]
    per_owner = latents.shape[2]
    channels = w_mid.shape[2]
    units = groups * per_owner
    height = per_owner * owners
    stack_rows = groups * height
    band_max = 2 * stack_rows // owners
    act_capacity = (band_max + 2 + owners - 1) // owners
    block = 16 if band_max % 16 == 0 else 8
    any_space = pl.BlockSpec(memory_space=pl.ANY)
    in_vmem = pl.BlockSpec(memory_space=pltpu.VMEM)

    def rows_first(array):
        return jnp.transpose(array[0, :, :, 0, :], (1, 0, 2))

    lat, old, act = rows_first(latents), rows_first(cache_lat), rows_first(cache_act)
    tiles = act.shape[2] // LANES
    lat_rows = (per_owner * 12 + 15) // 16 * 16
    packed_lat = pl.pallas_call(
        functools.partial(pack_latents, per_owner=per_owner, clips=clips),
        grid_spec=pltpu.PrefetchScalarGridSpec(
            num_scalar_prefetch=1,
            grid=(),
            in_specs=[any_space, any_space],
            out_specs=[in_vmem] * clips,
            scratch_shapes=[
                pltpu.VMEM(lat.shape, BF16),
                pltpu.VMEM(old.shape, BF16),
                pltpu.VMEM((clips * lat_rows, LANES), F32),
                pltpu.SemaphoreType.DMA((2,)),
            ],
        ),
        out_shape=[jax.ShapeDtypeStruct((lat_rows, LANES), BF16)] * clips,
        compiler_params=params(56),
        name="pack_latents",
    )(clip_group, lat, old)

    def trade(parts):
        return [parts[0]] + [
            lax.ppermute(part, "seq", [(i, i ^ other) for i in range(groups)])
            for other, part in enumerate(parts)
            if other
        ]

    per_step = 3
    packed_act = pl.pallas_call(
        functools.partial(pack_caches, per_step=per_step, clips=clips),
        grid_spec=pltpu.PrefetchScalarGridSpec(
            num_scalar_prefetch=1,
            grid=(per_owner // per_step,),
            in_specs=[
                pl.BlockSpec((per_step, clips, act.shape[2]), lambda step, _: (step, 0, 0))
            ],
            out_specs=[pl.BlockSpec((per_step * tiles, LANES), lambda step, _: (step, 0))] * clips,
            scratch_shapes=[pltpu.VMEM((clips * per_step * tiles, LANES), F32)],
        ),
        out_shape=[jax.ShapeDtypeStruct((per_owner * tiles, LANES), BF16)] * clips,
        compiler_params=params(56),
        name="pack_caches",
    )(clip_group, act)

    def exchange(array, axis):
        return lax.all_to_all(array, axis, split_axis=0, concat_axis=0, tiled=True)

    traded_lat, packed_act = lax.optimization_barrier((trade(packed_lat), packed_act))
    lat_capacity = (band_max + 4 + owners - 1) // owners
    slice_rows = (lat_capacity * 12 + 15) // 16 * 16
    band_lat = pl.pallas_call(
        functools.partial(
            slice_latents, owners=owners, units=units, capacity=lat_capacity, per_owner=per_owner
        ),
        grid_spec=pltpu.PrefetchScalarGridSpec(
            num_scalar_prefetch=1,
            grid=(),
            in_specs=[in_vmem] * clips,
            out_specs=in_vmem,
            scratch_shapes=[pltpu.VMEM((units * 12 + slice_rows, LANES), F32)],
        ),
        out_shape=jax.ShapeDtypeStruct((owners, slice_rows, LANES), BF16),
        compiler_params=params(56),
        name="slice_latents",
    )(band_rows, *traded_lat)
    band_lat = exchange(band_lat, "dec")
    band_act = pl.pallas_call(
        functools.partial(
            slice_caches, owners=owners, units=units, capacity=act_capacity, tiles=tiles
        ),
        grid_spec=pltpu.PrefetchScalarGridSpec(
            num_scalar_prefetch=1,
            grid=(),
            in_specs=[any_space] * clips,
            out_specs=any_space,
            scratch_shapes=[
                pltpu.VMEM((units * tiles, LANES), BF16),
                pltpu.SemaphoreType.DMA((clips,)),
                pltpu.SemaphoreType.DMA((owners,)),
            ],
        ),
        out_shape=jax.ShapeDtypeStruct((owners, act_capacity * tiles, LANES), BF16),
        compiler_params=params(56),
        name="slice_caches",
    )(band_rows, *trade(packed_act))
    band_lat, band_act = lax.optimization_barrier((band_lat, band_act))
    band_act = exchange(band_act, "dec")

    late, part, weights = pl.pallas_call(
        functools.partial(
            new_frames, owners=owners, units=units, capacity=lat_capacity, height=height,
            block=block, band_max=band_max, channels=channels,
        ),
        grid_spec=pltpu.PrefetchScalarGridSpec(
            num_scalar_prefetch=1,
            grid=(),
            in_specs=[in_vmem, in_vmem, in_vmem, any_space],
            out_specs=[any_space, in_vmem, in_vmem],
            scratch_shapes=[
                pltpu.VMEM((6 * LANES, channels), BF16),
                pltpu.VMEM((2, owners * slice_rows, LANES), F32),
                pltpu.VMEM((block + 5, F * COLS, 2 * LANES), BF16),
                pltpu.VMEM((block + 5, F * COLS, 2 * LANES), BF16),
                pltpu.VMEM(((block + 2) * F * COLS, channels), F32),
                pltpu.VMEM(((block + 2) * F * COLS, channels), F32),
                pltpu.VMEM((block + 3, F, COLS, channels), BF16),
                pltpu.VMEM((block + 3, F, COLS, channels), BF16),
                pltpu.VMEM((band_max, 2, COLS, channels), BF16),
                pltpu.SemaphoreType.DMA((27,)),
                pltpu.SemaphoreType.DMA((band_max // block,)),
            ],
        ),
        out_shape=[
            jax.ShapeDtypeStruct((band_max, F, COLS, channels), BF16),
            jax.ShapeDtypeStruct((band_max, 2, COLS, channels), F32),
            jax.ShapeDtypeStruct((9 * channels, 3 * channels), BF16),
        ],
        compiler_params=params(36),
        cost_estimate=pl.CostEstimate(
            flops=2 * band_max * 9 * COLS * 9 * channels * channels,
            bytes_accessed=16 * 1024 * 1024,
            transcendentals=0,
        ),
        name="new_frames",
    )(band_rows, band_lat, w_in, norm_gain.reshape(1, channels), w_mid)

    slots = owners * act_capacity
    decoded = pl.pallas_call(
        functools.partial(
            cached_frames, owners=owners, units=units, capacity=act_capacity, height=height,
            block=block, band_max=band_max, channels=channels,
        ),
        grid_spec=pltpu.PrefetchScalarGridSpec(
            num_scalar_prefetch=1,
            grid=(),
            in_specs=[in_vmem, in_vmem, in_vmem, any_space],
            out_specs=any_space,
            scratch_shapes=[
                pltpu.VMEM((band_max, 2, COLS, channels), BF16),
                pltpu.SemaphoreType.DMA((band_max // block,)),
            ],
        ),
        out_shape=jax.ShapeDtypeStruct((band_max, F, COLS, channels), BF16),
        input_output_aliases={4: 0},
        compiler_params=params(36),
        cost_estimate=pl.CostEstimate(
            flops=2 * band_max * 3 * COLS * 9 * channels * channels,
            bytes_accessed=16 * 1024 * 1024,
            transcendentals=0,
        ),
        name="cached_frames",
    )(band_rows, band_act.reshape(slots, tiles, LANES), part, weights, late)
    return decoded.reshape((1, 1) + decoded.shape)


def solution(mesh):
    placed = (
        P("seq", None, None, "dec", None),
        P("seq", None, None, "dec", None),
        P("seq", None, None, "dec", None),
        P(),
        P(),
        P(),
        P(),
        P(),
    )
    return jax.shard_map(
        shards,
        mesh=mesh,
        in_specs=placed,
        out_specs=P("seq", "dec", None, None, None, None),
        check_vma=False,
    )
```

```python
import functools

import jax
import jax.numpy as jnp
from jax import lax
from jax.experimental import pallas as pl
from jax.experimental.pallas import tpu as pltpu
from jax.sharding import PartitionSpec as P

F = 4
CT = 2
COLS = 16
LANES = 128
EPSILON = 1e-06
F32 = jnp.float32
BF16 = jnp.bfloat16


def band_start(bands, group, owner, owners):
    total = jnp.int32(0)
    for other in range(owners):
        total = total + jnp.where(other < owner, bands[group, other], 0)
    return total


def first_unit(start, margin, source, owners, units, capacity):
    unit = (start - margin - source + owners - 1 + 2 * owners) // owners - 2
    return jnp.clip(unit, 0, units - capacity)


def clip_of(groups_ref, shard, group, clips):
    found = jnp.int32(0)
    for clip in range(clips):
        found = found + jnp.where(groups_ref[shard, clip] == group, clip, 0)
    return found


def pack_clips(groups_ref, lat_in, old_in, act_in, *refs, per_owner, per_step, clips):
    *outs, lat_ref, old_ref, act_ref, lat_scratch, act_scratch, sems = refs
    shard = lax.axis_index("seq")
    copies = [
        pltpu.make_async_copy(lat_in, lat_ref, sems.at[0]),
        pltpu.make_async_copy(old_in, old_ref, sems.at[1]),
    ]
    steps = per_owner // per_step
    for step in range(steps):
        rows = pl.ds(step * per_step, per_step)
        copies.append(
            pltpu.make_async_copy(act_in.at[rows], act_ref.at[rows], sems.at[2 + step])
        )
    for copy in copies:
        copy.start()
    chosen = [clip_of(groups_ref, shard, shard ^ other, clips) for other in range(clips)]
    tiles = act_ref.shape[2] // LANES
    depth = tiles // (CT * COLS)
    size = per_step * tiles
    lat_rows = outs[0].shape[0] - per_owner * tiles
    copies[0].wait()
    copies[1].wait()
    for row in range(per_owner):
        for frame in range(CT + F):
            for half in range(2):
                if frame < CT:
                    tile = frame * 2 + half
                    value = old_ref[row, :, tile * LANES : (tile + 1) * LANES]
                else:
                    tile = (frame - CT) * 2 + half
                    value = lat_ref[row, :, tile * LANES : (tile + 1) * LANES]
                at = row * 12 + half * (CT + F) + frame
                lat_scratch[pl.ds(at, clips, stride=lat_rows), :] = value.astype(F32)
    for out, clip in zip(outs, chosen):
        rows = pl.ds(pl.multiple_of(clip * lat_rows, 8), lat_rows)
        out[per_owner * tiles :, :] = lat_scratch[rows, :].astype(BF16)
    for step in range(steps):
        copies[2 + step].wait()
        for row in range(per_step):
            for frame in range(CT):
                for col in range(COLS):
                    for part in range(depth):
                        tile = (frame * COLS + col) * depth + part
                        at = row * tiles + (frame * depth + part) * COLS + col
                        value = act_ref[
                            step * per_step + row, :, tile * LANES : (tile + 1) * LANES
                        ]
                        act_scratch[step % 2, pl.ds(at, clips, stride=size), :] = value.astype(F32)
        for out, clip in zip(outs, chosen):
            rows = pl.ds(pl.multiple_of(clip * size, 8), size)
            out[step * size : (step + 1) * size, :] = act_scratch[step % 2, rows, :].astype(BF16)


def slice_latents(bands, *refs, owners, units, capacity, per_owner, cache_rows):
    *ins, out_ref, scratch = refs
    group = lax.axis_index("seq")
    source = lax.axis_index("dec")
    rows = out_ref.shape[1]
    size = per_owner * 12
    for other, in_ref in enumerate(ins):
        value = in_ref[cache_rows : cache_rows + size, :].astype(F32)
        scratch[pl.ds((group ^ other) * size, size), :] = value
    value = pltpu.roll(scratch[: units * 12, :], 64, 1)
    lane = lax.broadcasted_iota(jnp.int32, value.shape, 1)
    for width in (32, 16):
        up, down = pltpu.roll(value, width, 1), pltpu.roll(value, LANES - width, 1)
        value = jnp.where(lane & width == 0, down, up)
    scratch[: units * 12, :] = value
    for owner in range(owners):
        start = band_start(bands, group, owner, owners)
        unit = first_unit(start, 2, source, owners, units, capacity)
        out_ref[owner] = scratch[pl.ds(unit * 12, rows), :].astype(BF16)


def slice_caches(bands, *refs, owners, units, capacity, tiles):
    *ins, out_ref, scratch, in_sems, sems = refs
    group = lax.axis_index("seq")
    source = lax.axis_index("dec")
    size = scratch.shape[0] // len(ins)
    copies = []
    for other, in_ref in enumerate(ins):
        into = scratch.at[pl.ds(pl.multiple_of((group ^ other) * size, 16), size)]
        copies.append(pltpu.make_async_copy(in_ref.at[pl.ds(0, size)], into, in_sems.at[other]))
    for copy in copies:
        copy.start()
    for copy in copies:
        copy.wait()
    copies = []
    for owner in range(owners):
        start = band_start(bands, group, owner, owners)
        unit = first_unit(start, 1, source, owners, units, capacity)
        copies.append(
            pltpu.make_async_copy(
                scratch.at[pl.ds(pl.multiple_of(unit * tiles, 16), capacity * tiles)],
                out_ref.at[owner],
                sems.at[owner],
            )
        )
    for copy in copies:
        copy.start()
    for copy in copies:
        copy.wait()


def shift_columns(sums, width):
    rows = sums.shape[0]
    col = lax.rem(lax.broadcasted_iota(jnp.int32, (rows, width), 0), COLS)
    left = pltpu.roll(sums[:, :width], 1, 0)
    right = pltpu.roll(sums[:, 2 * width :], rows - 1, 0)
    total = sums[:, width : 2 * width] + jnp.where(col > 0, left, 0.0)
    return total + jnp.where(col < COLS - 1, right, 0.0)


def weight_copies(mid_ref, weights, sems, channels):
    copies = []
    for tap in range(27):
        into = weights.at[
            pl.ds(tap // 3 * channels, channels), pl.ds(tap % 3 * channels, channels)
        ]
        copies.append(pltpu.make_async_copy(mid_ref.at[tap], into, sems.at[tap]))
    return copies


def new_frames(
    bands, lat_ref, win_ref, gain_ref, mid_ref, out_ref, part_out, early_ref, weights,
    table, xs, windows_a, windows_b, first_a, first_b, act_a, act_b, late, part_ref,
    sems, out_sems, part_sems, early_sem,
    *, owners, units, capacity, height, block, band_max, channels,
):
    group = lax.axis_index("seq")
    owner = lax.axis_index("dec")
    live = bands[group, owner]
    start = band_start(bands, group, owner, owners)
    edge = lax.rem(height - lax.rem(start - 1 + height, height), height)
    blocks = band_max // block
    size = F * COLS
    per_source = lat_ref.shape[1]
    copies = weight_copies(mid_ref, weights, sems, channels)
    for copy in copies:
        copy.start()
    table[...] = jnp.zeros(table.shape, BF16)
    for time_tap in range(3):
        for row_tap in range(3):
            for col_tap in range(3):
                into = row_tap * 2 * LANES + (0, 64, LANES)[time_tap]
                into += ((0, 112, 96), (0, -16, -32), (0, 112, 96))[time_tap][col_tap]
                table[pl.ds(into, 16), :] = win_ref[time_tap * 9 + row_tap * 3 + col_tap]
    for source in range(owners):
        value = lat_ref[source].astype(F32)
        xs[0, pl.ds(source * per_source, per_source), :] = value
        xs[1, pl.ds(source * per_source, per_source), :] = pltpu.roll(value, 64, 1)
    window_zero, act_zero = block + 4, block + 2
    for windows in (windows_a, windows_b):
        windows[window_zero] = jnp.zeros(windows.shape[1:], BF16)
    for act in (act_a, act_b):
        act[act_zero] = jnp.zeros((F, COLS, channels), BF16)
    gain = gain_ref[...]

    def clip_edges(at):
        is_first = (at == edge) | (at == edge + height)
        is_last = (at == edge - 1) | (at == edge - 1 + height)
        return is_first, is_last

    def fill(row, windows, into):
        lane = lax.broadcasted_iota(jnp.int32, (8, LANES), 1)
        col = lax.broadcasted_iota(jnp.int32, (8, LANES), 0)
        low = (lane < 16) | (lane >= 96)
        left_end = (col == 0) & ((lane & 63) < 16)
        right_end = (col == 7) & ((lane & 63) >= 32) & ((lane & 63) < 48)
        stack_row = jnp.clip(start - 2 + row, 0, units * owners - 1)
        source = lax.rem(stack_row, owners)
        unit = first_unit(start, 2, source, owners, units, capacity)
        slot = jnp.clip(lax.div(stack_row, owners) - unit, 0, capacity - 1)
        base = source * per_source + slot * 12
        rolled = [{}, {}]
        for frame in range(CT + F):
            for half in range(2):
                at_row = pl.ds(base + half * (CT + F) + frame, 1)
                for turn in range(2):
                    if turn == 1 and not 1 <= frame <= F:
                        continue
                    value = jnp.broadcast_to(xs[turn, at_row, :], (8, LANES))
                    rolled[turn][half, frame] = pltpu.roll(value, 0, 1, stride=16, stride_axis=0)
        for frame in range(F):
            pair = [
                jnp.where(low, rolled[0][half, frame], rolled[1][half, frame + 1])
                for half in range(2)
            ]
            last = [rolled[0][half, frame + 2] for half in range(2)]
            for lanes, (left, right) in enumerate((pair, last)):
                near = jnp.where(left_end, 0.0, jnp.where(right_end, right, left))
                far = jnp.where(right_end, 0.0, jnp.where(left_end, left, right))
                windows[
                    into,
                    frame * COLS : (frame + 1) * COLS,
                    lanes * LANES : (lanes + 1) * LANES,
                ] = jnp.concatenate([near, far], axis=0).astype(BF16)

    def produce(row, count, into, windows, first, act):
        for at in range(count + 2):
            fill(row + at, windows, at)
        pieces = [[], [], []]
        for at in range(count):
            is_first, is_last = clip_edges(row + at)
            pieces[0].append(windows[jnp.where(is_first, window_zero, at)])
            pieces[1].append(windows[at + 1])
            pieces[2].append(windows[jnp.where(is_last, window_zero, at + 2)])
        slab = jnp.concatenate([jnp.concatenate(part, axis=0) for part in pieces], axis=1)
        sums = jnp.dot(slab, table[...], preferred_element_type=F32)
        first[into * size : (into + count) * size, :] = sums
        for at in range(count):
            value = sums[at * size : (at + 1) * size]
            mean_square = jnp.mean(value * value, axis=-1, keepdims=True)
            value = value * lax.rsqrt(mean_square + EPSILON) * gain
            value = value / (1.0 + jnp.exp(-value))
            act[into + at] = value.astype(BF16).reshape(F, COLS, channels)

    def copy_out(number):
        rows = pl.ds(number * block, block)
        return pltpu.make_async_copy(
            late.at[rows], out_ref.at[rows, pl.ds(2, 2)], out_sems.at[number]
        )

    def part_copy(number):
        rows = pl.ds(number * block, block)
        return pltpu.make_async_copy(part_ref.at[rows], part_out.at[rows], part_sems.at[number])

    early = pltpu.make_async_copy(weights.at[pl.ds(0, 6 * channels)], early_ref, early_sem)

    def convolve(number, first, act):
        begin = number * block
        source_rows = [[], [], []]
        for row in range(block):
            is_first, is_last = clip_edges(begin + row + 1)
            source_rows[0].append(jnp.where(is_first, act_zero, row))
            source_rows[1].append(row + 1)
            source_rows[2].append(jnp.where(is_last, act_zero, row + 2))

        def finish(frames, weight_from, frame_from, count):
            pieces = []
            for frame in frames:
                for row_tap in range(3):
                    parts = [
                        act[at, frame : frame + count].reshape(count * COLS, channels)
                        for at in source_rows[row_tap]
                    ]
                    pieces.append(jnp.concatenate(parts, axis=0))
            slab = jnp.concatenate(pieces, axis=1)
            sums = jnp.dot(slab, weights[weight_from:, :], preferred_element_type=F32)
            total = shift_columns(sums, channels)
            parts = []
            for row in range(block):
                at = (row + 1) * size + frame_from * COLS
                parts.append(first[at : at + count * COLS, :])
            return total + jnp.concatenate(parts, axis=0)

        taps = 3 * channels
        rows = pl.ds(begin, block)
        value = finish([0, 1, 2], 0, 2, 2)
        at_row = lax.broadcasted_iota(jnp.int32, value.shape, 0) // (2 * COLS)
        value = jnp.where(at_row < live - begin, value, 0.0)
        late[rows] = value.astype(BF16).reshape(block, 2, COLS, channels)
        part_ref[rows, 1] = finish([0, 1], taps, 1, 1).reshape(block, COLS, channels)
        part_ref[rows, 0] = finish([0], 2 * taps, 0, 1).reshape(block, COLS, channels)

    def step(number, first, act, next_windows, next_first, next_act):
        convolve(number, first, act)
        for row in range(2):
            next_act[row] = act[block + row]
        next_first[: 2 * size, :] = first[block * size :, :]
        produce((number + 1) * block + 2, block, 2, next_windows, next_first, next_act)
        copy_out(number).start()
        part_copy(number).start()

    produce(0, block + 2, 0, windows_a, first_a, act_a)
    for copy in copies:
        copy.wait()
    early.start()
    used = lax.div(live + block - 1, block)

    def two_steps(pair, carry):
        step(2 * pair, first_a, act_a, windows_b, first_b, act_b)

        @pl.when(2 * pair + 1 < used)
        def _():
            step(2 * pair + 1, first_b, act_b, windows_a, first_a, act_a)

        return carry

    lax.fori_loop(0, lax.div(used + 1, 2), two_steps, 0)

    def clear(number, carry):
        late[pl.ds(number * block, block)] = jnp.zeros((block, 2, COLS, channels), BF16)
        copy_out(number).start()
        return carry

    def finish_part(number, carry):
        part_copy(number).wait()
        return carry

    lax.fori_loop(used, blocks, clear, 0)
    lax.fori_loop(0, used, finish_part, 0)
    early.wait()
    for number in range(blocks):
        copy_out(number).wait()


def cached_frames(
    bands, cache, part_in, early_ref, late_ref, out_ref,
    weights, part_ref, early, out_sems, part_sems, early_sem,
    *, owners, units, capacity, height, block, band_max, channels,
):
    del late_ref
    group = lax.axis_index("seq")
    owner = lax.axis_index("dec")
    live = bands[group, owner]
    start = band_start(bands, group, owner, owners)
    depth = channels // LANES
    blocks = band_max // block
    edge = lax.rem(height - lax.rem(start - 1 + height, height), height)

    def slot_of(at):
        row = jnp.clip(start - 1 + at, 0, units * owners - 1)
        source = lax.rem(row, owners)
        unit = first_unit(start, 1, source, owners, units, capacity)
        return source * capacity + jnp.clip(lax.div(row, owners) - unit, 0, capacity - 1)

    def copy_out(number):
        rows = pl.ds(number * block, block)
        return pltpu.make_async_copy(
            early.at[rows], out_ref.at[rows, pl.ds(0, 2)], out_sems.at[number]
        )

    def part_copy(number):
        rows = pl.ds(number * block, block)
        return pltpu.make_async_copy(part_in.at[rows], part_ref.at[rows], part_sems.at[number])

    load = pltpu.make_async_copy(early_ref, weights, early_sem)
    load.start()
    used = lax.div(live + block - 1, block)

    def load_part(number, carry):
        part_copy(number).start()
        return carry

    part_copy(0).start()
    load.wait()
    lax.fori_loop(1, used, load_part, 0)

    def convolve(number, carry):
        part_copy(number).wait()
        begin = number * block
        edges, source_rows = [[], [], []], [[], [], []]
        for row in range(block):
            at = begin + row + 1
            edges[0].append((at == edge) | (at == edge + height))
            edges[1].append(None)
            edges[2].append((at == edge - 1) | (at == edge - 1 + height))
            for row_tap in range(3):
                source_rows[row_tap].append(slot_of(at + row_tap - 1))

        def slab(frames):
            pieces = []
            for frame in frames:
                for row_tap in range(3):
                    for part in range(depth):
                        from_tile = (frame * depth + part) * COLS
                        parts = []
                        for at, outside in zip(source_rows[row_tap], edges[row_tap]):
                            value = cache[at, from_tile : from_tile + COLS, :]
                            if outside is not None:
                                value = jnp.where(outside, jnp.zeros_like(value), value)
                            parts.append(value)
                        pieces.append(jnp.concatenate(parts, axis=0))
            return jnp.concatenate(pieces, axis=1)

        at_row = lax.broadcasted_iota(jnp.int32, (block * COLS, channels), 0) // COLS
        taps = 3 * channels
        rows = pl.ds(begin, block)
        for frame, frames in ((0, (0, 1)), (1, (1,))):
            sums = jnp.dot(
                slab(frames), weights[: len(frames) * taps, :], preferred_element_type=F32
            )
            total = shift_columns(sums, channels) + part_ref[rows, frame].reshape(
                block * COLS, channels
            )
            total = jnp.where(at_row < live - begin, total, 0.0)
            early[rows, frame] = total.astype(BF16).reshape(block, COLS, channels)
        copy_out(number).start()
        return carry

    lax.fori_loop(0, used, convolve, 0)

    def clear(number, carry):
        early[pl.ds(number * block, block)] = jnp.zeros((block, 2, COLS, channels), BF16)
        copy_out(number).start()
        return carry

    lax.fori_loop(used, blocks, clear, 0)
    for number in range(blocks):
        copy_out(number).wait()


def params(mebibytes, **extra):
    return pltpu.CompilerParams(vmem_limit_bytes=mebibytes * 1024 * 1024, **extra)


def shards(latents, cache_lat, cache_act, w_in, w_mid, norm_gain, clip_group, band_rows):
    groups = lax.axis_size("seq")
    owners = lax.axis_size("dec")
    clips = latents.shape[1]
    per_owner = latents.shape[2]
    channels = w_mid.shape[2]
    units = groups * per_owner
    height = per_owner * owners
    stack_rows = groups * height
    band_max = 2 * stack_rows // owners
    act_capacity = (band_max + 2 + owners - 1) // owners
    block = 8
    any_space = pl.BlockSpec(memory_space=pl.ANY)
    in_vmem = pl.BlockSpec(memory_space=pltpu.VMEM)
    in_hbm = pl.BlockSpec(memory_space=pltpu.HBM)

    def rows_first(array):
        return jnp.transpose(array[0, :, :, 0, :], (1, 0, 2))

    lat, old, act = rows_first(latents), rows_first(cache_lat), rows_first(cache_act)
    tiles = act.shape[2] // LANES
    lat_rows = (per_owner * 12 + 15) // 16 * 16
    per_step = 3
    cache_rows = per_owner * tiles
    packed = pl.pallas_call(
        functools.partial(
            pack_clips, per_owner=per_owner, per_step=per_step, clips=clips
        ),
        grid_spec=pltpu.PrefetchScalarGridSpec(
            num_scalar_prefetch=1,
            grid=(),
            in_specs=[in_hbm, in_hbm, in_hbm],
            out_specs=[in_vmem] * clips,
            scratch_shapes=[
                pltpu.VMEM(lat.shape, BF16),
                pltpu.VMEM(old.shape, BF16),
                pltpu.VMEM(act.shape, BF16),
                pltpu.VMEM((clips * lat_rows, LANES), F32),
                pltpu.VMEM((2, clips * per_step * tiles, LANES), F32),
                pltpu.SemaphoreType.DMA((2 + per_owner // per_step,)),
            ],
        ),
        out_shape=[jax.ShapeDtypeStruct((cache_rows + lat_rows, LANES), BF16)] * clips,
        compiler_params=params(48),
        name="pack_clips",
    )(clip_group, lat, old, act)

    def trade(parts):
        return [parts[0]] + [
            lax.ppermute(part, "seq", [(i, i ^ other) for i in range(groups)])
            for other, part in enumerate(parts)
            if other
        ]

    def exchange(array, axis):
        return lax.all_to_all(array, axis, split_axis=0, concat_axis=0, tiled=True)

    traded = trade(packed)
    lat_capacity = (band_max + 4 + owners - 1) // owners
    slice_rows = (lat_capacity * 12 + 15) // 16 * 16
    band_lat = pl.pallas_call(
        functools.partial(
            slice_latents, owners=owners, units=units, capacity=lat_capacity, per_owner=per_owner,
            cache_rows=cache_rows,
        ),
        grid_spec=pltpu.PrefetchScalarGridSpec(
            num_scalar_prefetch=1,
            grid=(),
            in_specs=[in_vmem] * clips,
            out_specs=in_vmem,
            scratch_shapes=[pltpu.VMEM((units * 12 + slice_rows, LANES), F32)],
        ),
        out_shape=jax.ShapeDtypeStruct((owners, slice_rows, LANES), BF16),
        compiler_params=params(24),
        name="slice_latents",
    )(band_rows, *traded)
    band_lat = exchange(band_lat, "dec")
    band_act = pl.pallas_call(
        functools.partial(
            slice_caches, owners=owners, units=units, capacity=act_capacity, tiles=tiles
        ),
        grid_spec=pltpu.PrefetchScalarGridSpec(
            num_scalar_prefetch=1,
            grid=(),
            in_specs=[any_space] * clips,
            out_specs=any_space,
            scratch_shapes=[
                pltpu.VMEM((units * tiles, LANES), BF16),
                pltpu.SemaphoreType.DMA((clips,)),
                pltpu.SemaphoreType.DMA((owners,)),
            ],
        ),
        out_shape=jax.ShapeDtypeStruct((owners, act_capacity * tiles, LANES), BF16),
        compiler_params=params(24),
        name="slice_caches",
    )(band_rows, *traded)
    band_lat, band_act = lax.optimization_barrier((band_lat, band_act))
    band_act = exchange(band_act, "dec")

    late, part, early_mid = pl.pallas_call(
        functools.partial(
            new_frames, owners=owners, units=units, capacity=lat_capacity, height=height,
            block=block, band_max=band_max, channels=channels,
        ),
        grid_spec=pltpu.PrefetchScalarGridSpec(
            num_scalar_prefetch=1,
            grid=(),
            in_specs=[in_vmem, in_vmem, in_vmem, in_hbm],
            out_specs=[in_hbm, in_hbm, in_hbm],
            scratch_shapes=[
                pltpu.VMEM((9 * channels, 3 * channels), BF16),
                pltpu.VMEM((6 * LANES, channels), BF16),
                pltpu.VMEM((2, owners * slice_rows, LANES), F32),
                pltpu.VMEM((block + 5, F * COLS, 2 * LANES), BF16),
                pltpu.VMEM((block + 5, F * COLS, 2 * LANES), BF16),
                pltpu.VMEM(((block + 2) * F * COLS, channels), F32),
                pltpu.VMEM(((block + 2) * F * COLS, channels), F32),
                pltpu.VMEM((block + 3, F, COLS, channels), BF16),
                pltpu.VMEM((block + 3, F, COLS, channels), BF16),
                pltpu.VMEM((band_max, 2, COLS, channels), BF16),
                pltpu.VMEM((band_max, 2, COLS, channels), F32),
                pltpu.SemaphoreType.DMA((27,)),
                pltpu.SemaphoreType.DMA((band_max // block,)),
                pltpu.SemaphoreType.DMA((band_max // block,)),
                pltpu.SemaphoreType.DMA,
            ],
        ),
        out_shape=[
            jax.ShapeDtypeStruct((band_max, F, COLS, channels), BF16),
            jax.ShapeDtypeStruct((band_max, 2, COLS, channels), F32),
            jax.ShapeDtypeStruct((6 * channels, 3 * channels), BF16),
        ],
        compiler_params=params(44),
        cost_estimate=pl.CostEstimate(
            flops=2 * band_max * 9 * COLS * 9 * channels * channels,
            bytes_accessed=16 * 1024 * 1024,
            transcendentals=0,
        ),
        name="new_frames",
    )(band_rows, band_lat, w_in, norm_gain.reshape(1, channels), w_mid)

    slots = owners * act_capacity
    decoded = pl.pallas_call(
        functools.partial(
            cached_frames, owners=owners, units=units, capacity=act_capacity, height=height,
            block=block, band_max=band_max, channels=channels,
        ),
        grid_spec=pltpu.PrefetchScalarGridSpec(
            num_scalar_prefetch=1,
            grid=(),
            in_specs=[in_vmem, in_hbm, in_hbm, in_hbm],
            out_specs=in_hbm,
            scratch_shapes=[
                pltpu.VMEM((6 * channels, 3 * channels), BF16),
                pltpu.VMEM((band_max, 2, COLS, channels), F32),
                pltpu.VMEM((band_max, 2, COLS, channels), BF16),
                pltpu.SemaphoreType.DMA((band_max // block,)),
                pltpu.SemaphoreType.DMA((band_max // block,)),
                pltpu.SemaphoreType.DMA,
            ],
        ),
        out_shape=jax.ShapeDtypeStruct((band_max, F, COLS, channels), BF16),
        input_output_aliases={4: 0},
        compiler_params=params(36),
        cost_estimate=pl.CostEstimate(
            flops=2 * band_max * 3 * COLS * 9 * channels * channels,
            bytes_accessed=16 * 1024 * 1024,
            transcendentals=0,
        ),
        name="cached_frames",
    )(band_rows, band_act.reshape(slots, tiles, LANES), part, early_mid, late)
    return decoded.reshape((1, 1) + decoded.shape)


def solution(mesh):
    placed = (
        P("seq", None, None, "dec", None),
        P("seq", None, None, "dec", None),
        P("seq", None, None, "dec", None),
        P(),
        P(),
        P(),
        P(),
        P(),
    )
    return jax.shard_map(
        shards,
        mesh=mesh,
        in_specs=placed,
        out_specs=P("seq", "dec", None, None, None, None),
        check_vma=False,
    )
```

```python
import functools

import jax
import jax.numpy as jnp
from jax import lax
from jax.experimental import pallas as pl
from jax.experimental.pallas import tpu as pltpu
from jax.sharding import PartitionSpec as P

F = 4
CT = 2
COLS = 16
LANES = 128
EPSILON = 1e-06
F32 = jnp.float32
BF16 = jnp.bfloat16


def band_start(bands, group, owner, owners):
    total = jnp.int32(0)
    for other in range(owners):
        total = total + jnp.where(other < owner, bands[group, other], 0)
    return total


def first_unit(start, margin, source, owners, units, capacity):
    unit = (start - margin - source + owners - 1 + 2 * owners) // owners - 2
    return jnp.clip(unit, 0, units - capacity)


def clip_of(groups_ref, shard, group, clips):
    found = jnp.int32(0)
    for clip in range(clips):
        found = found + jnp.where(groups_ref[shard, clip] == group, clip, 0)
    return found


def pack_clips(groups_ref, lat_in, old_in, act_in, *refs, per_owner, per_step, clips):
    lat_outs, act_outs = refs[:clips], refs[clips : 2 * clips]
    lat_ref, old_ref, act_ref, lat_scratch, act_scratch, sems = refs[2 * clips :]
    shard = lax.axis_index("seq")
    copies = [
        pltpu.make_async_copy(lat_in, lat_ref, sems.at[0]),
        pltpu.make_async_copy(old_in, old_ref, sems.at[1]),
    ]
    steps = per_owner // per_step
    for step in range(steps):
        rows = pl.ds(step * per_step, per_step)
        copies.append(
            pltpu.make_async_copy(act_in.at[rows], act_ref.at[rows], sems.at[2 + step])
        )
    for copy in copies:
        copy.start()
    chosen = [clip_of(groups_ref, shard, shard ^ other, clips) for other in range(clips)]
    tiles = act_ref.shape[2] // LANES
    depth = tiles // (CT * COLS)
    size = per_step * tiles
    lat_rows = lat_outs[0].shape[0]
    copies[0].wait()
    copies[1].wait()
    for row in range(per_owner):
        for frame in range(CT + F):
            for half in range(2):
                if frame < CT:
                    tile = frame * 2 + half
                    value = old_ref[row, :, tile * LANES : (tile + 1) * LANES]
                else:
                    tile = (frame - CT) * 2 + half
                    value = lat_ref[row, :, tile * LANES : (tile + 1) * LANES]
                at = row * 12 + half * (CT + F) + frame
                lat_scratch[pl.ds(at, clips, stride=lat_rows), :] = value.astype(F32)
    for out, clip in zip(lat_outs, chosen):
        rows = pl.ds(pl.multiple_of(clip * lat_rows, 8), lat_rows)
        out[...] = lat_scratch[rows, :].astype(BF16)
    for step in range(steps):
        copies[2 + step].wait()
        for row in range(per_step):
            for frame in range(CT):
                for col in range(COLS):
                    for part in range(depth):
                        tile = (frame * COLS + col) * depth + part
                        at = row * tiles + (frame * depth + part) * COLS + col
                        value = act_ref[
                            step * per_step + row, :, tile * LANES : (tile + 1) * LANES
                        ]
                        act_scratch[step % 2, pl.ds(at, clips, stride=size), :] = value.astype(F32)
        for out, clip in zip(act_outs, chosen):
            rows = pl.ds(pl.multiple_of(clip * size, 8), size)
            out[step * size : (step + 1) * size, :] = act_scratch[step % 2, rows, :].astype(BF16)


def slice_latents(bands, *refs, owners, units, capacity, per_owner):
    *ins, out_ref, scratch = refs
    group = lax.axis_index("seq")
    source = lax.axis_index("dec")
    rows = out_ref.shape[1]
    size = per_owner * 12
    for other, in_ref in enumerate(ins):
        value = in_ref[:size, :].astype(F32)
        scratch[pl.ds((group ^ other) * size, size), :] = value
    value = pltpu.roll(scratch[: units * 12, :], 64, 1)
    lane = lax.broadcasted_iota(jnp.int32, value.shape, 1)
    for width in (32, 16):
        up, down = pltpu.roll(value, width, 1), pltpu.roll(value, LANES - width, 1)
        value = jnp.where(lane & width == 0, down, up)
    scratch[: units * 12, :] = value
    for owner in range(owners):
        start = band_start(bands, group, owner, owners)
        unit = first_unit(start, 2, source, owners, units, capacity)
        out_ref[owner] = scratch[pl.ds(unit * 12, rows), :].astype(BF16)


def slice_caches(bands, *refs, owners, units, capacity, tiles):
    *ins, out_ref, scratch, in_sems, sems = refs
    group = lax.axis_index("seq")
    source = lax.axis_index("dec")
    size = scratch.shape[0] // len(ins)
    copies = []
    for other, in_ref in enumerate(ins):
        into = scratch.at[pl.ds(pl.multiple_of((group ^ other) * size, 16), size)]
        copies.append(pltpu.make_async_copy(in_ref.at[pl.ds(0, size)], into, in_sems.at[other]))
    for copy in copies:
        copy.start()
    for copy in copies:
        copy.wait()
    copies = []
    for owner in range(owners):
        start = band_start(bands, group, owner, owners)
        unit = first_unit(start, 1, source, owners, units, capacity)
        copies.append(
            pltpu.make_async_copy(
                scratch.at[pl.ds(pl.multiple_of(unit * tiles, 16), capacity * tiles)],
                out_ref.at[owner],
                sems.at[owner],
            )
        )
    for copy in copies:
        copy.start()
    for copy in copies:
        copy.wait()


def shift_columns(sums, width):
    rows = sums.shape[0]
    col = lax.rem(lax.broadcasted_iota(jnp.int32, (rows, width), 0), COLS)
    left = pltpu.roll(sums[:, :width], 1, 0)
    right = pltpu.roll(sums[:, 2 * width :], rows - 1, 0)
    total = sums[:, width : 2 * width] + jnp.where(col > 0, left, 0.0)
    return total + jnp.where(col < COLS - 1, right, 0.0)


def widen_weights(mid_ref, _, out_ref):
    channels = mid_ref.shape[1]
    for tap in range(3):
        out_ref[:, tap * channels : (tap + 1) * channels] = mid_ref[tap]


def new_frames(
    bands, lat_ref, win_ref, gain_ref, mid_ref, out_ref, part_out,
    weights, table, xs, windows_a, windows_b, first_a, first_b, act_a, act_b, late, part_ref,
    sem, out_sems, part_sems,
    *, owners, units, capacity, height, block, band_max, channels,
):
    group = lax.axis_index("seq")
    owner = lax.axis_index("dec")
    live = bands[group, owner]
    start = band_start(bands, group, owner, owners)
    edge = lax.rem(height - lax.rem(start - 1 + height, height), height)
    blocks = band_max // block
    size = F * COLS
    per_source = lat_ref.shape[1]
    load = pltpu.make_async_copy(mid_ref, weights, sem)
    load.start()
    table[...] = jnp.zeros(table.shape, BF16)
    for time_tap in range(3):
        for row_tap in range(3):
            for col_tap in range(3):
                into = row_tap * 2 * LANES + (0, 64, LANES)[time_tap]
                into += ((0, 112, 96), (0, -16, -32), (0, 112, 96))[time_tap][col_tap]
                table[pl.ds(into, 16), :] = win_ref[time_tap * 9 + row_tap * 3 + col_tap]
    for source in range(owners):
        value = lat_ref[source].astype(F32)
        xs[0, pl.ds(source * per_source, per_source), :] = value
        xs[1, pl.ds(source * per_source, per_source), :] = pltpu.roll(value, 64, 1)
    window_zero, act_zero = block + 4, block + 2
    for windows in (windows_a, windows_b):
        windows[window_zero] = jnp.zeros(windows.shape[1:], BF16)
    for act in (act_a, act_b):
        act[act_zero] = jnp.zeros((F, COLS, channels), BF16)
    gain = gain_ref[...]

    def clip_edges(at):
        is_first = (at == edge) | (at == edge + height)
        is_last = (at == edge - 1) | (at == edge - 1 + height)
        return is_first, is_last

    def fill(row, windows, into):
        lane = lax.broadcasted_iota(jnp.int32, (8, LANES), 1)
        col = lax.broadcasted_iota(jnp.int32, (8, LANES), 0)
        low = (lane < 16) | (lane >= 96)
        left_end = (col == 0) & ((lane & 63) < 16)
        right_end = (col == 7) & ((lane & 63) >= 32) & ((lane & 63) < 48)
        stack_row = jnp.clip(start - 2 + row, 0, units * owners - 1)
        source = lax.rem(stack_row, owners)
        unit = first_unit(start, 2, source, owners, units, capacity)
        slot = jnp.clip(lax.div(stack_row, owners) - unit, 0, capacity - 1)
        base = source * per_source + slot * 12
        rolled = [{}, {}]
        for frame in range(CT + F):
            for half in range(2):
                at_row = pl.ds(base + half * (CT + F) + frame, 1)
                for turn in range(2):
                    if turn == 1 and not 1 <= frame <= F:
                        continue
                    value = jnp.broadcast_to(xs[turn, at_row, :], (8, LANES))
                    rolled[turn][half, frame] = pltpu.roll(value, 0, 1, stride=16, stride_axis=0)
        for frame in range(F):
            pair = [
                jnp.where(low, rolled[0][half, frame], rolled[1][half, frame + 1])
                for half in range(2)
            ]
            last = [rolled[0][half, frame + 2] for half in range(2)]
            for lanes, (left, right) in enumerate((pair, last)):
                near = jnp.where(left_end, 0.0, jnp.where(right_end, right, left))
                far = jnp.where(right_end, 0.0, jnp.where(left_end, left, right))
                windows[
                    into,
                    frame * COLS : (frame + 1) * COLS,
                    lanes * LANES : (lanes + 1) * LANES,
                ] = jnp.concatenate([near, far], axis=0).astype(BF16)

    def fill_block(row, count, windows):
        for at in range(count + 2):
            fill(row + at, windows, at)

    def convolve_first(row, count, windows):
        pieces = [[], [], []]
        for at in range(count):
            is_first, is_last = clip_edges(row + at)
            pieces[0].append(windows[jnp.where(is_first, window_zero, at)])
            pieces[1].append(windows[at + 1])
            pieces[2].append(windows[jnp.where(is_last, window_zero, at + 2)])
        slab = jnp.concatenate([jnp.concatenate(part, axis=0) for part in pieces], axis=1)
        return jnp.dot(slab, table[...], preferred_element_type=F32)

    def activate(sums, count, into, first, act):
        first[into * size : (into + count) * size, :] = sums
        for at in range(count):
            value = sums[at * size : (at + 1) * size]
            mean_square = jnp.mean(value * value, axis=-1, keepdims=True)
            value = value * lax.rsqrt(mean_square + EPSILON) * gain
            value = value / (1.0 + jnp.exp(-value))
            act[into + at] = value.astype(BF16).reshape(F, COLS, channels)

    def copy_out(number):
        rows = pl.ds(number * block, block)
        return pltpu.make_async_copy(
            late.at[rows], out_ref.at[rows, pl.ds(2, 2)], out_sems.at[number]
        )

    def part_copy(number):
        rows = pl.ds(number * block, block)
        return pltpu.make_async_copy(part_ref.at[rows], part_out.at[rows], part_sems.at[number])

    def convolve(number, first, act):
        begin = number * block
        source_rows = [[], [], []]
        for row in range(block):
            is_first, is_last = clip_edges(begin + row + 1)
            source_rows[0].append(jnp.where(is_first, act_zero, row))
            source_rows[1].append(row + 1)
            source_rows[2].append(jnp.where(is_last, act_zero, row + 2))

        def finish(frames, weight_from, frame_from, count):
            pieces = []
            for frame in frames:
                for row_tap in range(3):
                    parts = [
                        act[at, frame : frame + count].reshape(count * COLS, channels)
                        for at in source_rows[row_tap]
                    ]
                    pieces.append(jnp.concatenate(parts, axis=0))
            slab = jnp.concatenate(pieces, axis=1)
            sums = jnp.dot(slab, weights[weight_from:, :], preferred_element_type=F32)
            total = shift_columns(sums, channels)
            parts = []
            for row in range(block):
                at = (row + 1) * size + frame_from * COLS
                parts.append(first[at : at + count * COLS, :])
            return total + jnp.concatenate(parts, axis=0)

        taps = 3 * channels
        rows = pl.ds(begin, block)
        value = finish([0, 1, 2], 0, 2, 2)
        at_row = lax.broadcasted_iota(jnp.int32, value.shape, 0) // (2 * COLS)
        value = jnp.where(at_row < live - begin, value, 0.0)
        late[rows] = value.astype(BF16).reshape(block, 2, COLS, channels)
        part_ref[rows, 1] = finish([0, 1], taps, 1, 1).reshape(block, COLS, channels)
        part_ref[rows, 0] = finish([0], 2 * taps, 0, 1).reshape(block, COLS, channels)

    def step(number, windows, first, act, next_windows, next_first, next_act):
        sums = convolve_first((number + 1) * block + 2, block, windows)
        for row in range(2):
            next_act[row] = act[block + row]
        next_first[: 2 * size, :] = first[block * size :, :]
        activate(sums, block, 2, next_first, next_act)
        convolve(number, first, act)
        fill_block((number + 2) * block + 2, block, next_windows)
        copy_out(number).start()
        part_copy(number).start()

    fill_block(0, block + 2, windows_b)
    activate(convolve_first(0, block + 2, windows_b), block + 2, 0, first_a, act_a)
    fill_block(block + 2, block, windows_a)
    load.wait()
    used = lax.div(live + block - 1, block)

    def two_steps(pair, carry):
        step(2 * pair, windows_a, first_a, act_a, windows_b, first_b, act_b)

        @pl.when(2 * pair + 1 < used)
        def _():
            step(2 * pair + 1, windows_b, first_b, act_b, windows_a, first_a, act_a)

        return carry

    lax.fori_loop(0, lax.div(used + 1, 2), two_steps, 0)

    def clear(number, carry):
        late[pl.ds(number * block, block)] = jnp.zeros((block, 2, COLS, channels), BF16)
        copy_out(number).start()
        return carry

    def finish_part(number, carry):
        part_copy(number).wait()
        return carry

    lax.fori_loop(used, blocks, clear, 0)
    lax.fori_loop(0, used, finish_part, 0)
    for number in range(blocks):
        copy_out(number).wait()


def cached_frames(
    bands, cache, part_in, early_ref, late_ref, out_ref,
    weights, part_ref, early, out_sems, part_sems, early_sem,
    *, owners, units, capacity, height, block, band_max, channels,
):
    del late_ref
    group = lax.axis_index("seq")
    owner = lax.axis_index("dec")
    live = bands[group, owner]
    start = band_start(bands, group, owner, owners)
    depth = channels // LANES
    blocks = band_max // block
    edge = lax.rem(height - lax.rem(start - 1 + height, height), height)

    def slot_of(at):
        row = jnp.clip(start - 1 + at, 0, units * owners - 1)
        source = lax.rem(row, owners)
        unit = first_unit(start, 1, source, owners, units, capacity)
        return source * capacity + jnp.clip(lax.div(row, owners) - unit, 0, capacity - 1)

    def copy_out(number):
        rows = pl.ds(number * block, block)
        return pltpu.make_async_copy(
            early.at[rows], out_ref.at[rows, pl.ds(0, 2)], out_sems.at[number]
        )

    def part_copy(number):
        rows = pl.ds(number * block, block)
        return pltpu.make_async_copy(part_in.at[rows], part_ref.at[rows], part_sems.at[number])

    load = pltpu.make_async_copy(early_ref.at[pl.ds(0, 6 * channels)], weights, early_sem)
    load.start()
    used = lax.div(live + block - 1, block)

    def load_part(number, carry):
        part_copy(number).start()
        return carry

    part_copy(0).start()
    load.wait()
    lax.fori_loop(1, used, load_part, 0)

    def convolve(number, carry):
        part_copy(number).wait()
        begin = number * block
        edges, source_rows = [[], [], []], [[], [], []]
        for row in range(block):
            at = begin + row + 1
            edges[0].append((at == edge) | (at == edge + height))
            edges[1].append(None)
            edges[2].append((at == edge - 1) | (at == edge - 1 + height))
            for row_tap in range(3):
                source_rows[row_tap].append(slot_of(at + row_tap - 1))

        def slab(frames):
            pieces = []
            for frame in frames:
                for row_tap in range(3):
                    for part in range(depth):
                        from_tile = (frame * depth + part) * COLS
                        parts = []
                        for at, outside in zip(source_rows[row_tap], edges[row_tap]):
                            value = cache[at, from_tile : from_tile + COLS, :]
                            if outside is not None:
                                value = jnp.where(outside, jnp.zeros_like(value), value)
                            parts.append(value)
                        pieces.append(jnp.concatenate(parts, axis=0))
            return jnp.concatenate(pieces, axis=1)

        at_row = lax.broadcasted_iota(jnp.int32, (block * COLS, channels), 0) // COLS
        taps = 3 * channels
        rows = pl.ds(begin, block)
        for frame, frames in ((0, (0, 1)), (1, (1,))):
            sums = jnp.dot(
                slab(frames), weights[: len(frames) * taps, :], preferred_element_type=F32
            )
            total = shift_columns(sums, channels) + part_ref[rows, frame].reshape(
                block * COLS, channels
            )
            total = jnp.where(at_row < live - begin, total, 0.0)
            early[rows, frame] = total.astype(BF16).reshape(block, COLS, channels)
        copy_out(number).start()
        return carry

    lax.fori_loop(0, used, convolve, 0)

    def clear(number, carry):
        early[pl.ds(number * block, block)] = jnp.zeros((block, 2, COLS, channels), BF16)
        copy_out(number).start()
        return carry

    lax.fori_loop(used, blocks, clear, 0)
    for number in range(blocks):
        copy_out(number).wait()


def params(mebibytes, **extra):
    return pltpu.CompilerParams(vmem_limit_bytes=mebibytes * 1024 * 1024, **extra)


def shards(latents, cache_lat, cache_act, w_in, w_mid, norm_gain, clip_group, band_rows):
    groups = lax.axis_size("seq")
    owners = lax.axis_size("dec")
    clips = latents.shape[1]
    per_owner = latents.shape[2]
    channels = w_mid.shape[2]
    units = groups * per_owner
    height = per_owner * owners
    stack_rows = groups * height
    band_max = 2 * stack_rows // owners
    act_capacity = (band_max + 2 + owners - 1) // owners
    block = next(size for size in (16, 8) if band_max % size == 0)
    cached_block = next(size for size in (32, 16, 8) if band_max % size == 0)
    any_space = pl.BlockSpec(memory_space=pl.ANY)
    in_vmem = pl.BlockSpec(memory_space=pltpu.VMEM)
    in_hbm = pl.BlockSpec(memory_space=pltpu.HBM)

    def rows_first(array):
        return jnp.transpose(array[0, :, :, 0, :], (1, 0, 2))

    lat, old, act = rows_first(latents), rows_first(cache_lat), rows_first(cache_act)
    tiles = act.shape[2] // LANES
    lat_rows = (per_owner * 12 + 15) // 16 * 16
    per_step = 3
    packed = pl.pallas_call(
        functools.partial(
            pack_clips, per_owner=per_owner, per_step=per_step, clips=clips
        ),
        grid_spec=pltpu.PrefetchScalarGridSpec(
            num_scalar_prefetch=1,
            grid=(),
            in_specs=[in_hbm, in_hbm, in_hbm],
            out_specs=[in_vmem] * (2 * clips),
            scratch_shapes=[
                pltpu.VMEM(lat.shape, BF16),
                pltpu.VMEM(old.shape, BF16),
                pltpu.VMEM(act.shape, BF16),
                pltpu.VMEM((clips * lat_rows, LANES), F32),
                pltpu.VMEM((2, clips * per_step * tiles, LANES), F32),
                pltpu.SemaphoreType.DMA((2 + per_owner // per_step,)),
            ],
        ),
        out_shape=[jax.ShapeDtypeStruct((lat_rows, LANES), BF16)] * clips
        + [jax.ShapeDtypeStruct((per_owner * tiles, LANES), BF16)] * clips,
        compiler_params=params(56),
        name="pack_clips",
    )(clip_group, lat, old, act)

    after_pack = packed[0]
    wide_mid = pl.pallas_call(
        widen_weights,
        grid=(9,),
        in_specs=[
            pl.BlockSpec((3, channels, channels), lambda step: (step, 0, 0)),
            any_space,
        ],
        out_specs=pl.BlockSpec((channels, 3 * channels), lambda step: (step, 0)),
        out_shape=jax.ShapeDtypeStruct((9 * channels, 3 * channels), BF16),
        compiler_params=params(40, dimension_semantics=("arbitrary",)),
        cost_estimate=pl.CostEstimate(
            flops=0, bytes_accessed=4 * 27 * channels * channels, transcendentals=0
        ),
        name="widen_weights",
    )(w_mid, after_pack)

    def trade(parts):
        return [parts[0]] + [
            lax.ppermute(part, "seq", [(i, i ^ other) for i in range(groups)])
            for other, part in enumerate(parts)
            if other
        ]

    def exchange(array, axis):
        return lax.all_to_all(array, axis, split_axis=0, concat_axis=0, tiled=True)

    lat_capacity = (band_max + 4 + owners - 1) // owners
    slice_rows = (lat_capacity * 12 + 15) // 16 * 16
    band_lat = pl.pallas_call(
        functools.partial(
            slice_latents, owners=owners, units=units, capacity=lat_capacity, per_owner=per_owner,
        ),
        grid_spec=pltpu.PrefetchScalarGridSpec(
            num_scalar_prefetch=1,
            grid=(),
            in_specs=[in_vmem] * clips,
            out_specs=in_vmem,
            scratch_shapes=[pltpu.VMEM((units * 12 + slice_rows, LANES), F32)],
        ),
        out_shape=jax.ShapeDtypeStruct((owners, slice_rows, LANES), BF16),
        compiler_params=params(24),
        name="slice_latents",
    )(band_rows, *trade(packed[:clips]))
    band_lat = exchange(band_lat, "dec")
    band_act = pl.pallas_call(
        functools.partial(
            slice_caches, owners=owners, units=units, capacity=act_capacity, tiles=tiles
        ),
        grid_spec=pltpu.PrefetchScalarGridSpec(
            num_scalar_prefetch=1,
            grid=(),
            in_specs=[any_space] * clips,
            out_specs=any_space,
            scratch_shapes=[
                pltpu.VMEM((units * tiles, LANES), BF16),
                pltpu.SemaphoreType.DMA((clips,)),
                pltpu.SemaphoreType.DMA((owners,)),
            ],
        ),
        out_shape=jax.ShapeDtypeStruct((owners, act_capacity * tiles, LANES), BF16),
        compiler_params=params(24),
        name="slice_caches",
    )(band_rows, *trade(packed[clips:]))
    band_lat, band_act = lax.optimization_barrier((band_lat, band_act))
    band_act = exchange(band_act, "dec")

    late, part = pl.pallas_call(
        functools.partial(
            new_frames, owners=owners, units=units, capacity=lat_capacity, height=height,
            block=block, band_max=band_max, channels=channels,
        ),
        grid_spec=pltpu.PrefetchScalarGridSpec(
            num_scalar_prefetch=1,
            grid=(),
            in_specs=[in_vmem, in_vmem, in_vmem, in_hbm],
            out_specs=[in_hbm, in_hbm],
            scratch_shapes=[
                pltpu.VMEM((9 * channels, 3 * channels), BF16),
                pltpu.VMEM((6 * LANES, channels), BF16),
                pltpu.VMEM((2, owners * slice_rows, LANES), F32),
                pltpu.VMEM((block + 5, F * COLS, 2 * LANES), BF16),
                pltpu.VMEM((block + 5, F * COLS, 2 * LANES), BF16),
                pltpu.VMEM(((block + 2) * F * COLS, channels), F32),
                pltpu.VMEM(((block + 2) * F * COLS, channels), F32),
                pltpu.VMEM((block + 3, F, COLS, channels), BF16),
                pltpu.VMEM((block + 3, F, COLS, channels), BF16),
                pltpu.VMEM((band_max, 2, COLS, channels), BF16),
                pltpu.VMEM((band_max, 2, COLS, channels), F32),
                pltpu.SemaphoreType.DMA,
                pltpu.SemaphoreType.DMA((band_max // block,)),
                pltpu.SemaphoreType.DMA((band_max // block,)),
            ],
        ),
        out_shape=[
            jax.ShapeDtypeStruct((band_max, F, COLS, channels), BF16),
            jax.ShapeDtypeStruct((band_max, 2, COLS, channels), F32),
        ],
        compiler_params=params(44),
        cost_estimate=pl.CostEstimate(
            flops=2 * band_max * 9 * COLS * 9 * channels * channels,
            bytes_accessed=16 * 1024 * 1024,
            transcendentals=0,
        ),
        name="new_frames",
    )(band_rows, band_lat, w_in, norm_gain.reshape(1, channels), wide_mid)

    slots = owners * act_capacity
    decoded = pl.pallas_call(
        functools.partial(
            cached_frames, owners=owners, units=units, capacity=act_capacity, height=height,
            block=cached_block, band_max=band_max, channels=channels,
        ),
        grid_spec=pltpu.PrefetchScalarGridSpec(
            num_scalar_prefetch=1,
            grid=(),
            in_specs=[in_vmem, in_hbm, in_hbm, in_hbm],
            out_specs=in_hbm,
            scratch_shapes=[
                pltpu.VMEM((6 * channels, 3 * channels), BF16),
                pltpu.VMEM((band_max, 2, COLS, channels), F32),
                pltpu.VMEM((band_max, 2, COLS, channels), BF16),
                pltpu.SemaphoreType.DMA((band_max // cached_block,)),
                pltpu.SemaphoreType.DMA((band_max // cached_block,)),
                pltpu.SemaphoreType.DMA,
            ],
        ),
        out_shape=jax.ShapeDtypeStruct((band_max, F, COLS, channels), BF16),
        input_output_aliases={4: 0},
        compiler_params=params(56),
        cost_estimate=pl.CostEstimate(
            flops=2 * band_max * 3 * COLS * 9 * channels * channels,
            bytes_accessed=16 * 1024 * 1024,
            transcendentals=0,
        ),
        name="cached_frames",
    )(band_rows, band_act.reshape(slots, tiles, LANES), part, wide_mid, late)
    return decoded.reshape((1, 1) + decoded.shape)


def solution(mesh):
    placed = (
        P("seq", None, None, "dec", None),
        P("seq", None, None, "dec", None),
        P("seq", None, None, "dec", None),
        P(),
        P(),
        P(),
        P(),
        P(),
    )
    return jax.shard_map(
        shards,
        mesh=mesh,
        in_specs=placed,
        out_specs=P("seq", "dec", None, None, None, None),
        check_vma=False,
    )
```

```python
import functools

import jax
import jax.numpy as jnp
from jax import lax
from jax.experimental import pallas as pl
from jax.experimental.pallas import tpu as pltpu
from jax.sharding import PartitionSpec as P

F = 4
CT = 2
COLS = 16
LANES = 128
EPSILON = 1e-06
F32 = jnp.float32
BF16 = jnp.bfloat16


def band_start(bands, group, owner, owners):
    total = jnp.int32(0)
    for other in range(owners):
        total = total + jnp.where(other < owner, bands[group, other], 0)
    return total


def first_unit(start, margin, source, owners, units, capacity):
    unit = (start - margin - source + owners - 1 + 2 * owners) // owners - 2
    return jnp.clip(unit, 0, units - capacity)


def clip_of(groups_ref, shard, group, clips):
    found = jnp.int32(0)
    for clip in range(clips):
        found = found + jnp.where(groups_ref[shard, clip] == group, clip, 0)
    return found


def pack_clips(groups_ref, lat_in, old_in, act_in, *refs, per_owner, per_step, clips):
    lat_outs, act_outs = refs[:clips], refs[clips : 2 * clips]
    lat_ref, old_ref, act_ref, lat_scratch, act_scratch, sems = refs[2 * clips :]
    shard = lax.axis_index("seq")
    copies = [
        pltpu.make_async_copy(lat_in, lat_ref, sems.at[0]),
        pltpu.make_async_copy(old_in, old_ref, sems.at[1]),
    ]
    steps = per_owner // per_step
    for step in range(steps):
        rows = pl.ds(step * per_step, per_step)
        copies.append(
            pltpu.make_async_copy(act_in.at[rows], act_ref.at[rows], sems.at[2 + step])
        )
    for copy in copies:
        copy.start()
    chosen = [clip_of(groups_ref, shard, shard ^ other, clips) for other in range(clips)]
    tiles = act_ref.shape[2] // LANES
    depth = tiles // (CT * COLS)
    size = per_step * tiles
    lat_rows = lat_outs[0].shape[0]
    copies[0].wait()
    copies[1].wait()
    for row in range(per_owner):
        for frame in range(CT + F):
            for half in range(2):
                if frame < CT:
                    tile = frame * 2 + half
                    value = old_ref[row, :, tile * LANES : (tile + 1) * LANES]
                else:
                    tile = (frame - CT) * 2 + half
                    value = lat_ref[row, :, tile * LANES : (tile + 1) * LANES]
                at = row * 12 + half * (CT + F) + frame
                lat_scratch[pl.ds(at, clips, stride=lat_rows), :] = value.astype(F32)
    for out, clip in zip(lat_outs, chosen):
        rows = pl.ds(pl.multiple_of(clip * lat_rows, 8), lat_rows)
        out[...] = lat_scratch[rows, :].astype(BF16)
    for step in range(steps):
        copies[2 + step].wait()
        for row in range(per_step):
            for frame in range(CT):
                for col in range(COLS):
                    for part in range(depth):
                        tile = (frame * COLS + col) * depth + part
                        at = row * tiles + (frame * depth + part) * COLS + col
                        value = act_ref[
                            step * per_step + row, :, tile * LANES : (tile + 1) * LANES
                        ]
                        act_scratch[step % 2, pl.ds(at, clips, stride=size), :] = value.astype(F32)
        for out, clip in zip(act_outs, chosen):
            rows = pl.ds(pl.multiple_of(clip * size, 8), size)
            out[step * size : (step + 1) * size, :] = act_scratch[step % 2, rows, :].astype(BF16)


def slice_latents(bands, *refs, owners, units, capacity, per_owner, groups):
    ins, outs, scratch = refs[:groups], refs[groups:-1], refs[-1]
    group = lax.axis_index("seq")
    source = lax.axis_index("dec")
    rows = outs[0].shape[0]
    size = per_owner * 12
    for other, in_ref in enumerate(ins):
        value = in_ref[:size, :].astype(F32)
        scratch[pl.ds((group ^ other) * size, size), :] = value
    value = pltpu.roll(scratch[: units * 12, :], 64, 1)
    lane = lax.broadcasted_iota(jnp.int32, value.shape, 1)
    for width in (32, 16):
        up, down = pltpu.roll(value, width, 1), pltpu.roll(value, LANES - width, 1)
        value = jnp.where(lane & width == 0, down, up)
    scratch[: units * 12, :] = value
    for other, out_ref in enumerate(outs):
        start = band_start(bands, group, source ^ other, owners)
        unit = first_unit(start, 2, source, owners, units, capacity)
        out_ref[...] = scratch[pl.ds(unit * 12, rows), :].astype(BF16)


def slice_caches(bands, *refs, owners, units, capacity, tiles, groups):
    ins, outs, (scratch, in_sems, sems) = refs[:groups], refs[groups:-3], refs[-3:]
    group = lax.axis_index("seq")
    source = lax.axis_index("dec")
    size = scratch.shape[0] // groups
    copies = []
    for other, in_ref in enumerate(ins):
        into = scratch.at[pl.ds(pl.multiple_of((group ^ other) * size, 16), size)]
        copies.append(pltpu.make_async_copy(in_ref, into, in_sems.at[other]))
    for copy in copies:
        copy.start()
    for copy in copies:
        copy.wait()
    copies = []
    for other, out_ref in enumerate(outs):
        start = band_start(bands, group, source ^ other, owners)
        unit = first_unit(start, 1, source, owners, units, capacity)
        rows = pl.ds(pl.multiple_of(unit * tiles, 16), capacity * tiles)
        copies.append(pltpu.make_async_copy(scratch.at[rows], out_ref, sems.at[other]))
    for copy in copies:
        copy.start()
    for copy in copies:
        copy.wait()


def shift_columns(sums, width):
    rows = sums.shape[0]
    col = lax.rem(lax.broadcasted_iota(jnp.int32, (rows, width), 0), COLS)
    left = pltpu.roll(sums[:, :width], 1, 0)
    right = pltpu.roll(sums[:, 2 * width :], rows - 1, 0)
    total = sums[:, width : 2 * width] + jnp.where(col > 0, left, 0.0)
    return total + jnp.where(col < COLS - 1, right, 0.0)


def widen_weights(mid_ref, _, out_ref, sems):
    channels = mid_ref.shape[1]
    copies = []
    for tap in range(27):
        into = out_ref.at[
            pl.ds(tap // 3 * channels, channels), pl.ds(tap % 3 * channels, channels)
        ]
        copies.append(pltpu.make_async_copy(mid_ref.at[tap], into, sems.at[tap]))
    for copy in copies:
        copy.start()
    for copy in copies:
        copy.wait()


def new_frames(
    bands, win_ref, gain_ref, weights, *refs,
    owners, units, capacity, height, block, band_max, channels,
):
    group = lax.axis_index("seq")
    owner = lax.axis_index("dec")
    lat_refs, refs = refs[:owners], refs[owners:]
    out_ref, part_ref, table, xs, windows_a, windows_b, first_a, first_b, act_a, act_b, late = refs[:-1]
    out_sems = refs[-1]
    live = bands[group, owner]
    start = band_start(bands, group, owner, owners)
    edge = lax.rem(height - lax.rem(start - 1 + height, height), height)
    blocks = band_max // block
    size = F * COLS
    per_source = lat_refs[0].shape[0]
    table[...] = jnp.zeros(table.shape, BF16)
    for time_tap in range(3):
        for row_tap in range(3):
            for col_tap in range(3):
                into = row_tap * 2 * LANES + (0, 64, LANES)[time_tap]
                into += ((0, 112, 96), (0, -16, -32), (0, 112, 96))[time_tap][col_tap]
                table[pl.ds(into, 16), :] = win_ref[time_tap * 9 + row_tap * 3 + col_tap]
    for other, lat_ref in enumerate(lat_refs):
        value = lat_ref[...].astype(F32)
        rows = pl.ds(pl.multiple_of((owner ^ other) * per_source, 8), per_source)
        xs[0, rows, :] = value
        xs[1, rows, :] = pltpu.roll(value, 64, 1)
    window_zero, act_zero = block + 4, block + 2
    for windows in (windows_a, windows_b):
        windows[window_zero] = jnp.zeros(windows.shape[1:], BF16)
    for act in (act_a, act_b):
        act[act_zero] = jnp.zeros((F, COLS, channels), BF16)
    half_gain = 0.5 * gain_ref[...]

    def clip_edges(at):
        is_first = (at == edge) | (at == edge + height)
        is_last = (at == edge - 1) | (at == edge - 1 + height)
        return is_first, is_last

    def fill(row, windows, into):
        lane = lax.broadcasted_iota(jnp.int32, (8, LANES), 1)
        col = lax.broadcasted_iota(jnp.int32, (8, LANES), 0)
        low = (lane < 16) | (lane >= 96)
        left_end = (col == 0) & ((lane & 63) < 16)
        right_end = (col == 7) & ((lane & 63) >= 32) & ((lane & 63) < 48)
        stack_row = jnp.clip(start - 2 + row, 0, units * owners - 1)
        source = lax.rem(stack_row, owners)
        unit = first_unit(start, 2, source, owners, units, capacity)
        slot = jnp.clip(lax.div(stack_row, owners) - unit, 0, capacity - 1)
        base = source * per_source + slot * 12
        rolled = [{}, {}]
        for frame in range(CT + F):
            for half in range(2):
                at_row = pl.ds(base + half * (CT + F) + frame, 1)
                for turn in range(2):
                    if turn == 1 and not 1 <= frame <= F:
                        continue
                    value = jnp.broadcast_to(xs[turn, at_row, :], (8, LANES))
                    rolled[turn][half, frame] = pltpu.roll(value, 0, 1, stride=16, stride_axis=0)
        for frame in range(F):
            pair = [
                jnp.where(low, rolled[0][half, frame], rolled[1][half, frame + 1])
                for half in range(2)
            ]
            last = [rolled[0][half, frame + 2] for half in range(2)]
            for lanes, (left, right) in enumerate((pair, last)):
                near = jnp.where(left_end, 0.0, jnp.where(right_end, right, left))
                far = jnp.where(right_end, 0.0, jnp.where(left_end, left, right))
                windows[
                    into,
                    frame * COLS : (frame + 1) * COLS,
                    lanes * LANES : (lanes + 1) * LANES,
                ] = jnp.concatenate([near, far], axis=0).astype(BF16)

    def fill_block(row, count, windows):
        for at in range(count + 2):
            fill(row + at, windows, at)

    def convolve_first(row, count, windows):
        pieces = [[], [], []]
        for at in range(count):
            is_first, is_last = clip_edges(row + at)
            pieces[0].append(windows[jnp.where(is_first, window_zero, at)])
            pieces[1].append(windows[at + 1])
            pieces[2].append(windows[jnp.where(is_last, window_zero, at + 2)])
        slab = jnp.concatenate([jnp.concatenate(part, axis=0) for part in pieces], axis=1)
        return jnp.dot(slab, table[...], preferred_element_type=F32)

    def activate(sums, count, into, first, act):
        first[into * size : (into + count) * size, :] = sums
        for at in range(count):
            value = sums[at * size : (at + 1) * size]
            mean_square = jnp.mean(value * value, axis=-1, keepdims=True)
            half = value * lax.rsqrt(mean_square + EPSILON) * half_gain
            value = half + half * jnp.tanh(half)
            act[into + at] = value.astype(BF16).reshape(F, COLS, channels)

    def copy_out(number):
        rows = pl.ds(number * block, block)
        return pltpu.make_async_copy(
            late.at[rows], out_ref.at[rows, pl.ds(2, 2)], out_sems.at[number]
        )

    def convolve(number, first, act):
        begin = number * block
        source_rows = [[], [], []]
        for row in range(block):
            is_first, is_last = clip_edges(begin + row + 1)
            source_rows[0].append(jnp.where(is_first, act_zero, row))
            source_rows[1].append(row + 1)
            source_rows[2].append(jnp.where(is_last, act_zero, row + 2))

        def finish(frames, weight_from, frame_from, count):
            pieces = []
            for frame in frames:
                for row_tap in range(3):
                    parts = [
                        act[at, frame : frame + count].reshape(count * COLS, channels)
                        for at in source_rows[row_tap]
                    ]
                    pieces.append(jnp.concatenate(parts, axis=0))
            slab = jnp.concatenate(pieces, axis=1)
            sums = jnp.dot(slab, weights[weight_from:, :], preferred_element_type=F32)
            total = shift_columns(sums, channels)
            parts = []
            for row in range(block):
                at = (row + 1) * size + frame_from * COLS
                parts.append(first[at : at + count * COLS, :])
            return total + jnp.concatenate(parts, axis=0)

        taps = 3 * channels
        rows = pl.ds(begin, block)
        value = finish([0, 1, 2], 0, 2, 2)
        at_row = lax.broadcasted_iota(jnp.int32, value.shape, 0) // (2 * COLS)
        value = jnp.where(at_row < live - begin, value, 0.0)
        late[rows] = value.astype(BF16).reshape(block, 2, COLS, channels)
        part_ref[rows, 1] = finish([0, 1], taps, 1, 1).reshape(block, COLS, channels)
        part_ref[rows, 0] = finish([0], 2 * taps, 0, 1).reshape(block, COLS, channels)

    def step(number, windows, first, act, next_windows, next_first, next_act):
        sums = convolve_first((number + 1) * block + 2, block, windows)
        for row in range(2):
            next_act[row] = act[block + row]
        next_first[: 2 * size, :] = first[block * size :, :]
        activate(sums, block, 2, next_first, next_act)
        convolve(number, first, act)
        fill_block((number + 2) * block + 2, block, next_windows)
        copy_out(number).start()

    fill_block(0, block + 2, windows_b)
    activate(convolve_first(0, block + 2, windows_b), block + 2, 0, first_a, act_a)
    fill_block(block + 2, block, windows_a)
    used = lax.div(live + block - 1, block)

    def two_steps(pair, carry):
        step(2 * pair, windows_a, first_a, act_a, windows_b, first_b, act_b)

        @pl.when(2 * pair + 1 < used)
        def _():
            step(2 * pair + 1, windows_b, first_b, act_b, windows_a, first_a, act_a)

        return carry

    lax.fori_loop(0, lax.div(used + 1, 2), two_steps, 0)

    def clear(number, carry):
        late[pl.ds(number * block, block)] = jnp.zeros((block, 2, COLS, channels), BF16)
        copy_out(number).start()
        return carry

    lax.fori_loop(used, blocks, clear, 0)
    for number in range(blocks):
        copy_out(number).wait()


def cached_frames(
    bands, part_ref, weights, late_ref, *refs,
    owners, units, capacity, height, block, band_max, channels,
):
    del late_ref
    parts, (out_ref, cache, early, out_sems, cache_sems) = refs[:owners], refs[owners:]
    group = lax.axis_index("seq")
    owner = lax.axis_index("dec")
    live = bands[group, owner]
    start = band_start(bands, group, owner, owners)
    depth = channels // LANES
    blocks = band_max // block
    edge = lax.rem(height - lax.rem(start - 1 + height, height), height)

    def slot_of(at):
        row = jnp.clip(start - 1 + at, 0, units * owners - 1)
        source = lax.rem(row, owners)
        unit = first_unit(start, 1, source, owners, units, capacity)
        return source * capacity + jnp.clip(lax.div(row, owners) - unit, 0, capacity - 1)

    def copy_out(number):
        rows = pl.ds(number * block, block)
        return pltpu.make_async_copy(
            early.at[rows], out_ref.at[rows, pl.ds(0, 2)], out_sems.at[number]
        )

    copies = []
    for other, part in enumerate(parts):
        into = cache.at[pl.ds((owner ^ other) * capacity, capacity)]
        copies.append(pltpu.make_async_copy(part, into, cache_sems.at[other]))
    for copy in copies:
        copy.start()
    slots = owners * capacity
    cache[slots] = jnp.zeros(cache.shape[1:], BF16)
    for copy in copies:
        copy.wait()
    used = lax.div(live + block - 1, block)

    def convolve(number, carry):
        begin = number * block
        source_rows = [[], [], []]
        for row in range(block):
            at = begin + row + 1
            is_first = (at == edge) | (at == edge + height)
            is_last = (at == edge - 1) | (at == edge - 1 + height)
            source_rows[0].append(jnp.where(is_first, slots, slot_of(at - 1)))
            source_rows[1].append(slot_of(at))
            source_rows[2].append(jnp.where(is_last, slots, slot_of(at + 1)))

        def slab(frames):
            pieces = []
            for frame in frames:
                for row_tap in range(3):
                    for part in range(depth):
                        tile = pl.ds((frame * depth + part) * COLS, COLS)
                        values = [cache[at, tile, :] for at in source_rows[row_tap]]
                        pieces.append(jnp.concatenate(values, axis=0))
            return jnp.concatenate(pieces, axis=1)

        at_row = lax.broadcasted_iota(jnp.int32, (block * COLS, channels), 0) // COLS
        taps = 3 * channels
        rows = pl.ds(begin, block)
        for frame, frames in ((0, (0, 1)), (1, (1,))):
            sums = jnp.dot(
                slab(frames), weights[: len(frames) * taps, :], preferred_element_type=F32
            )
            total = shift_columns(sums, channels) + part_ref[rows, frame].reshape(
                block * COLS, channels
            )
            total = jnp.where(at_row < live - begin, total, 0.0)
            early[rows, frame] = total.astype(BF16).reshape(block, COLS, channels)
        copy_out(number).start()
        return carry

    lax.fori_loop(0, used, convolve, 0)

    def clear(number, carry):
        early[pl.ds(number * block, block)] = jnp.zeros((block, 2, COLS, channels), BF16)
        copy_out(number).start()
        return carry

    lax.fori_loop(used, blocks, clear, 0)
    for number in range(blocks):
        copy_out(number).wait()


def params(mebibytes, **extra):
    return pltpu.CompilerParams(vmem_limit_bytes=mebibytes * 1024 * 1024, **extra)


def shards(latents, cache_lat, cache_act, w_in, w_mid, norm_gain, clip_group, band_rows):
    groups = lax.axis_size("seq")
    owners = lax.axis_size("dec")
    clips = latents.shape[1]
    per_owner = latents.shape[2]
    channels = w_mid.shape[2]
    units = groups * per_owner
    height = per_owner * owners
    stack_rows = groups * height
    band_max = 2 * stack_rows // owners
    act_capacity = (band_max + 2 + owners - 1) // owners
    block = next(size for size in (16, 8) if band_max % size == 0)
    any_space = pl.BlockSpec(memory_space=pl.ANY)
    in_vmem = pl.BlockSpec(memory_space=pltpu.VMEM)
    in_hbm = pl.BlockSpec(memory_space=pltpu.HBM)

    def rows_first(array):
        return jnp.transpose(array[0, :, :, 0, :], (1, 0, 2))

    lat, old, act = rows_first(latents), rows_first(cache_lat), rows_first(cache_act)
    tiles = act.shape[2] // LANES
    lat_rows = (per_owner * 12 + 15) // 16 * 16
    per_step = 3
    packed = pl.pallas_call(
        functools.partial(
            pack_clips, per_owner=per_owner, per_step=per_step, clips=clips
        ),
        grid_spec=pltpu.PrefetchScalarGridSpec(
            num_scalar_prefetch=1,
            grid=(),
            in_specs=[in_hbm, in_hbm, in_hbm],
            out_specs=[in_vmem] * (2 * clips),
            scratch_shapes=[
                pltpu.VMEM(lat.shape, BF16),
                pltpu.VMEM(old.shape, BF16),
                pltpu.VMEM(act.shape, BF16),
                pltpu.VMEM((clips * lat_rows, LANES), F32),
                pltpu.VMEM((2, clips * per_step * tiles, LANES), F32),
                pltpu.SemaphoreType.DMA((2 + per_owner // per_step,)),
            ],
        ),
        out_shape=[jax.ShapeDtypeStruct((lat_rows, LANES), BF16)] * clips
        + [jax.ShapeDtypeStruct((per_owner * tiles, LANES), BF16)] * clips,
        compiler_params=params(56),
        name="pack_clips",
    )(clip_group, lat, old, act)

    def trade(parts, axis):
        count = lax.axis_size(axis)
        return [parts[0]] + [
            lax.ppermute(part, axis, [(i, i ^ other) for i in range(count)])
            for other, part in enumerate(parts)
            if other
        ]

    traded_act = trade(packed[clips:], "seq")
    traded_lat = trade(packed[:clips], "seq")
    wide_mid = pl.pallas_call(
        widen_weights,
        in_specs=[in_hbm, any_space],
        out_specs=in_vmem,
        scratch_shapes=[pltpu.SemaphoreType.DMA((27,))],
        out_shape=jax.ShapeDtypeStruct((9 * channels, 3 * channels), BF16),
        compiler_params=params(16),
        cost_estimate=pl.CostEstimate(
            flops=0, bytes_accessed=4 * 27 * channels * channels, transcendentals=0
        ),
        name="widen_weights",
    )(w_mid, packed[0])
    lat_capacity = (band_max + 4 + owners - 1) // owners
    slice_rows = (lat_capacity * 12 + 15) // 16 * 16
    band_lat = pl.pallas_call(
        functools.partial(
            slice_latents, owners=owners, units=units, capacity=lat_capacity, per_owner=per_owner,
            groups=groups,
        ),
        grid_spec=pltpu.PrefetchScalarGridSpec(
            num_scalar_prefetch=1,
            grid=(),
            in_specs=[in_vmem] * clips,
            out_specs=[in_vmem] * owners,
            scratch_shapes=[pltpu.VMEM((units * 12 + slice_rows, LANES), F32)],
        ),
        out_shape=[jax.ShapeDtypeStruct((slice_rows, LANES), BF16)] * owners,
        compiler_params=params(16),
        name="slice_latents",
    )(band_rows, *traded_lat)
    band_lat = trade(band_lat, "dec")
    band_act = pl.pallas_call(
        functools.partial(
            slice_caches, owners=owners, units=units, capacity=act_capacity, tiles=tiles,
            groups=groups,
        ),
        grid_spec=pltpu.PrefetchScalarGridSpec(
            num_scalar_prefetch=1,
            grid=(),
            in_specs=[any_space] * clips,
            out_specs=[in_vmem] * owners,
            scratch_shapes=[
                pltpu.VMEM((units * tiles, LANES), BF16),
                pltpu.SemaphoreType.DMA((clips,)),
                pltpu.SemaphoreType.DMA((owners,)),
            ],
        ),
        out_shape=[jax.ShapeDtypeStruct((act_capacity * tiles, LANES), BF16)] * owners,
        compiler_params=params(16),
        name="slice_caches",
    )(band_rows, *traded_act)
    band_lat, band_act = lax.optimization_barrier((band_lat, band_act))
    band_act = trade(band_act, "dec")

    late, part = pl.pallas_call(
        functools.partial(
            new_frames, owners=owners, units=units, capacity=lat_capacity, height=height,
            block=block, band_max=band_max, channels=channels,
        ),
        grid_spec=pltpu.PrefetchScalarGridSpec(
            num_scalar_prefetch=1,
            grid=(),
            in_specs=[in_vmem] * (3 + owners),
            out_specs=[in_hbm, in_vmem],
            scratch_shapes=[
                pltpu.VMEM((6 * LANES, channels), BF16),
                pltpu.VMEM((2, owners * slice_rows, LANES), F32),
                pltpu.VMEM((block + 5, F * COLS, 2 * LANES), BF16),
                pltpu.VMEM((block + 5, F * COLS, 2 * LANES), BF16),
                pltpu.VMEM(((block + 2) * F * COLS, channels), F32),
                pltpu.VMEM(((block + 2) * F * COLS, channels), F32),
                pltpu.VMEM((block + 3, F, COLS, channels), BF16),
                pltpu.VMEM((block + 3, F, COLS, channels), BF16),
                pltpu.VMEM((band_max, 2, COLS, channels), BF16),
                pltpu.SemaphoreType.DMA((band_max // block,)),
            ],
        ),
        out_shape=[
            jax.ShapeDtypeStruct((band_max, F, COLS, channels), BF16),
            jax.ShapeDtypeStruct((band_max, 2, COLS, channels), F32),
        ],
        compiler_params=params(36),
        cost_estimate=pl.CostEstimate(
            flops=2 * band_max * 9 * COLS * 9 * channels * channels,
            bytes_accessed=16 * 1024 * 1024,
            transcendentals=0,
        ),
        name="new_frames",
    )(band_rows, w_in, norm_gain.reshape(1, channels), wide_mid, *band_lat)

    slots = owners * act_capacity
    band_act = [rows.reshape(act_capacity, tiles, LANES) for rows in band_act]
    decoded = pl.pallas_call(
        functools.partial(
            cached_frames, owners=owners, units=units, capacity=act_capacity, height=height,
            block=block, band_max=band_max, channels=channels,
        ),
        grid_spec=pltpu.PrefetchScalarGridSpec(
            num_scalar_prefetch=1,
            grid=(),
            in_specs=[in_vmem, in_vmem, in_hbm] + [any_space] * owners,
            out_specs=in_hbm,
            scratch_shapes=[
                pltpu.VMEM((slots + 1, tiles, LANES), BF16),
                pltpu.VMEM((band_max, 2, COLS, channels), BF16),
                pltpu.SemaphoreType.DMA((band_max // block,)),
                pltpu.SemaphoreType.DMA((owners,)),
            ],
        ),
        out_shape=jax.ShapeDtypeStruct((band_max, F, COLS, channels), BF16),
        input_output_aliases={3: 0},
        compiler_params=params(24),
        cost_estimate=pl.CostEstimate(
            flops=2 * band_max * 3 * COLS * 9 * channels * channels,
            bytes_accessed=16 * 1024 * 1024,
            transcendentals=0,
        ),
        name="cached_frames",
    )(band_rows, part, wide_mid, late, *band_act)
    return decoded.reshape((1, 1) + decoded.shape)


def solution(mesh):
    placed = (
        P("seq", None, None, "dec", None),
        P("seq", None, None, "dec", None),
        P("seq", None, None, "dec", None),
        P(),
        P(),
        P(),
        P(),
        P(),
    )
    return jax.shard_map(
        shards,
        mesh=mesh,
        in_specs=placed,
        out_specs=P("seq", "dec", None, None, None, None),
        check_vma=False,
    )
```

```python
import functools

import jax
import jax.numpy as jnp
from jax import lax
from jax.experimental import pallas as pl
from jax.experimental.pallas import tpu as pltpu
from jax.sharding import PartitionSpec as P

F = 4
CT = 2
COLS = 16
LANES = 128
EPSILON = 1e-06
F32 = jnp.float32
BF16 = jnp.bfloat16


def band_start(bands, group, owner, owners):
    total = jnp.int32(0)
    for other in range(owners):
        total = total + jnp.where(other < owner, bands[group, other], 0)
    return total


def first_unit(start, margin, source, owners, units, capacity):
    unit = (start - margin - source + owners - 1 + 2 * owners) // owners - 2
    return jnp.clip(unit, 0, units - capacity)


def clip_of(groups_ref, shard, group, clips):
    found = jnp.int32(0)
    for clip in range(clips):
        found = found + jnp.where(groups_ref[shard, clip] == group, clip, 0)
    return found


def pack_clips(groups_ref, lat_in, old_in, act_in, *refs, per_owner, per_step, clips):
    lat_outs, act_outs = refs[:clips], refs[clips : 2 * clips]
    lat_ref, old_ref, act_ref, lat_scratch, act_scratch, sems = refs[2 * clips :]
    shard = lax.axis_index("seq")
    copies = [
        pltpu.make_async_copy(lat_in, lat_ref, sems.at[0]),
        pltpu.make_async_copy(old_in, old_ref, sems.at[1]),
    ]
    steps = per_owner // per_step
    for step in range(steps):
        rows = pl.ds(step * per_step, per_step)
        copies.append(
            pltpu.make_async_copy(act_in.at[rows], act_ref.at[rows], sems.at[2 + step])
        )
    for copy in copies:
        copy.start()
    chosen = [clip_of(groups_ref, shard, shard ^ other, clips) for other in range(clips)]
    tiles = act_ref.shape[2] // LANES
    depth = tiles // (CT * COLS)
    size = per_step * tiles
    lat_rows = lat_outs[0].shape[0]
    copies[0].wait()
    copies[1].wait()
    for row in range(per_owner):
        for frame in range(CT + F):
            for half in range(2):
                if frame < CT:
                    tile = frame * 2 + half
                    value = old_ref[row, :, tile * LANES : (tile + 1) * LANES]
                else:
                    tile = (frame - CT) * 2 + half
                    value = lat_ref[row, :, tile * LANES : (tile + 1) * LANES]
                at = row * 12 + half * (CT + F) + frame
                lat_scratch[pl.ds(at, clips, stride=lat_rows), :] = value.astype(F32)
    for out, clip in zip(lat_outs, chosen):
        rows = pl.ds(pl.multiple_of(clip * lat_rows, 8), lat_rows)
        out[...] = lat_scratch[rows, :].astype(BF16)
    for step in range(steps):
        copies[2 + step].wait()
        for row in range(per_step):
            for frame in range(CT):
                for col in range(COLS):
                    for part in range(depth):
                        tile = (frame * COLS + col) * depth + part
                        at = row * tiles + (frame * depth + part) * COLS + col
                        value = act_ref[
                            step * per_step + row, :, tile * LANES : (tile + 1) * LANES
                        ]
                        act_scratch[step % 2, pl.ds(at, clips, stride=size), :] = value.astype(F32)
        for out, clip in zip(act_outs, chosen):
            rows = pl.ds(pl.multiple_of(clip * size, 8), size)
            out[step * size : (step + 1) * size, :] = act_scratch[step % 2, rows, :].astype(BF16)


def slice_latents(bands, *refs, owners, units, capacity, per_owner, groups):
    ins, outs, scratch = refs[:groups], refs[groups:-1], refs[-1]
    group = lax.axis_index("seq")
    source = lax.axis_index("dec")
    rows = outs[0].shape[0]
    size = per_owner * 12
    for other, in_ref in enumerate(ins):
        value = in_ref[:size, :].astype(F32)
        scratch[pl.ds((group ^ other) * size, size), :] = value
    value = pltpu.roll(scratch[: units * 12, :], 64, 1)
    lane = lax.broadcasted_iota(jnp.int32, value.shape, 1)
    for width in (32, 16):
        up, down = pltpu.roll(value, width, 1), pltpu.roll(value, LANES - width, 1)
        value = jnp.where(lane & width == 0, down, up)
    scratch[: units * 12, :] = value
    for other, out_ref in enumerate(outs):
        start = band_start(bands, group, source ^ other, owners)
        unit = first_unit(start, 2, source, owners, units, capacity)
        out_ref[...] = scratch[pl.ds(unit * 12, rows), :].astype(BF16)


def slice_caches(bands, *refs, owners, units, capacity, tiles, groups):
    ins, outs, (scratch, in_sems, sems) = refs[:groups], refs[groups:-3], refs[-3:]
    group = lax.axis_index("seq")
    source = lax.axis_index("dec")
    size = scratch.shape[0] // groups
    copies = []
    for other, in_ref in enumerate(ins):
        into = scratch.at[pl.ds(pl.multiple_of((group ^ other) * size, 16), size)]
        copies.append(pltpu.make_async_copy(in_ref, into, in_sems.at[other]))
    for copy in copies:
        copy.start()
    for copy in copies:
        copy.wait()
    copies = []
    for other, out_ref in enumerate(outs):
        start = band_start(bands, group, source ^ other, owners)
        unit = first_unit(start, 1, source, owners, units, capacity)
        rows = pl.ds(pl.multiple_of(unit * tiles, 16), capacity * tiles)
        copies.append(pltpu.make_async_copy(scratch.at[rows], out_ref, sems.at[other]))
    for copy in copies:
        copy.start()
    for copy in copies:
        copy.wait()


def shift_columns(sums, width):
    rows = sums.shape[0]
    col = lax.rem(lax.broadcasted_iota(jnp.int32, (rows, width), 0), COLS)
    left = pltpu.roll(sums[:, :width], 1, 0)
    right = pltpu.roll(sums[:, 2 * width :], rows - 1, 0)
    total = sums[:, width : 2 * width] + jnp.where(col > 0, left, 0.0)
    return total + jnp.where(col < COLS - 1, right, 0.0)


def weight_copies(mid_ref, weights, sems, channels):
    copies = []
    for tap in range(27):
        into = weights.at[
            pl.ds(tap // 3 * channels, channels), pl.ds(tap % 3 * channels, channels)
        ]
        copies.append(pltpu.make_async_copy(mid_ref.at[tap], into, sems.at[tap]))
    return copies


def new_frames(
    bands, win_ref, gain_ref, mid_ref, *refs,
    owners, units, capacity, height, block, band_max, channels,
):
    group = lax.axis_index("seq")
    owner = lax.axis_index("dec")
    lat_refs, refs = refs[:owners], refs[owners:]
    out_ref, part_ref, weights, table, xs, windows_a, windows_b, first_a, first_b = refs[:9]
    act_a, act_b, late, out_sems, sems = refs[9:]
    copies = weight_copies(mid_ref, weights, sems, channels)
    for copy in copies:
        copy.start()
    live = bands[group, owner]
    start = band_start(bands, group, owner, owners)
    edge = lax.rem(height - lax.rem(start - 1 + height, height), height)
    blocks = band_max // block
    size = F * COLS
    per_source = lat_refs[0].shape[0]
    table[...] = jnp.zeros(table.shape, BF16)
    for time_tap in range(3):
        for row_tap in range(3):
            for col_tap in range(3):
                into = row_tap * 2 * LANES + (0, 64, LANES)[time_tap]
                into += ((0, 112, 96), (0, -16, -32), (0, 112, 96))[time_tap][col_tap]
                table[pl.ds(into, 16), :] = win_ref[time_tap * 9 + row_tap * 3 + col_tap]
    for other, lat_ref in enumerate(lat_refs):
        value = lat_ref[...].astype(F32)
        rows = pl.ds(pl.multiple_of((owner ^ other) * per_source, 8), per_source)
        xs[0, rows, :] = value
        xs[1, rows, :] = pltpu.roll(value, 64, 1)
    window_zero, act_zero = block + 4, block + 2
    for windows in (windows_a, windows_b):
        windows[window_zero] = jnp.zeros(windows.shape[1:], BF16)
    for act in (act_a, act_b):
        act[act_zero] = jnp.zeros((F, COLS, channels), BF16)
    half_gain = 0.5 * gain_ref[...]

    def clip_edges(at):
        is_first = (at == edge) | (at == edge + height)
        is_last = (at == edge - 1) | (at == edge - 1 + height)
        return is_first, is_last

    def fill(row, windows, into):
        lane = lax.broadcasted_iota(jnp.int32, (8, LANES), 1)
        col = lax.broadcasted_iota(jnp.int32, (8, LANES), 0)
        low = (lane < 16) | (lane >= 96)
        left_end = (col == 0) & ((lane & 63) < 16)
        right_end = (col == 7) & ((lane & 63) >= 32) & ((lane & 63) < 48)
        stack_row = jnp.clip(start - 2 + row, 0, units * owners - 1)
        source = lax.rem(stack_row, owners)
        unit = first_unit(start, 2, source, owners, units, capacity)
        slot = jnp.clip(lax.div(stack_row, owners) - unit, 0, capacity - 1)
        base = source * per_source + slot * 12
        rolled = [{}, {}]
        for frame in range(CT + F):
            for half in range(2):
                at_row = pl.ds(base + half * (CT + F) + frame, 1)
                for turn in range(2):
                    if turn == 1 and not 1 <= frame <= F:
                        continue
                    value = jnp.broadcast_to(xs[turn, at_row, :], (8, LANES))
                    rolled[turn][half, frame] = pltpu.roll(value, 0, 1, stride=16, stride_axis=0)
        for frame in range(F):
            pair = [
                jnp.where(low, rolled[0][half, frame], rolled[1][half, frame + 1])
                for half in range(2)
            ]
            last = [rolled[0][half, frame + 2] for half in range(2)]
            for lanes, (left, right) in enumerate((pair, last)):
                near = jnp.where(left_end, 0.0, jnp.where(right_end, right, left))
                far = jnp.where(right_end, 0.0, jnp.where(left_end, left, right))
                windows[
                    into,
                    frame * COLS : (frame + 1) * COLS,
                    lanes * LANES : (lanes + 1) * LANES,
                ] = jnp.concatenate([near, far], axis=0).astype(BF16)

    def fill_block(row, count, windows):
        for at in range(count + 2):
            fill(row + at, windows, at)

    def convolve_first(row, count, windows):
        pieces = [[], [], []]
        for at in range(count):
            is_first, is_last = clip_edges(row + at)
            pieces[0].append(windows[jnp.where(is_first, window_zero, at)])
            pieces[1].append(windows[at + 1])
            pieces[2].append(windows[jnp.where(is_last, window_zero, at + 2)])
        slab = jnp.concatenate([jnp.concatenate(part, axis=0) for part in pieces], axis=1)
        return jnp.dot(slab, table[...], preferred_element_type=F32)

    def activate(sums, count, into, first, act):
        first[into * size : (into + count) * size, :] = sums
        for at in range(count):
            value = sums[at * size : (at + 1) * size]
            mean_square = jnp.mean(value * value, axis=-1, keepdims=True)
            half = value * lax.rsqrt(mean_square + EPSILON) * half_gain
            value = half + half * jnp.tanh(half)
            act[into + at] = value.astype(BF16).reshape(F, COLS, channels)

    def copy_out(number):
        rows = pl.ds(number * block, block)
        return pltpu.make_async_copy(
            late.at[rows], out_ref.at[rows, pl.ds(2, 2)], out_sems.at[number]
        )

    def convolve(number, first, act):
        begin = number * block
        source_rows = [[], [], []]
        for row in range(block):
            is_first, is_last = clip_edges(begin + row + 1)
            source_rows[0].append(jnp.where(is_first, act_zero, row))
            source_rows[1].append(row + 1)
            source_rows[2].append(jnp.where(is_last, act_zero, row + 2))

        def finish(frames, weight_from, frame_from, count):
            pieces = []
            for frame in frames:
                for row_tap in range(3):
                    parts = [
                        act[at, frame : frame + count].reshape(count * COLS, channels)
                        for at in source_rows[row_tap]
                    ]
                    pieces.append(jnp.concatenate(parts, axis=0))
            slab = jnp.concatenate(pieces, axis=1)
            sums = jnp.dot(slab, weights[weight_from:, :], preferred_element_type=F32)
            total = shift_columns(sums, channels)
            parts = []
            for row in range(block):
                at = (row + 1) * size + frame_from * COLS
                parts.append(first[at : at + count * COLS, :])
            return total + jnp.concatenate(parts, axis=0)

        taps = 3 * channels
        rows = pl.ds(begin, block)
        value = finish([0, 1, 2], 0, 2, 2)
        at_row = lax.broadcasted_iota(jnp.int32, value.shape, 0) // (2 * COLS)
        value = jnp.where(at_row < live - begin, value, 0.0)
        late[rows] = value.astype(BF16).reshape(block, 2, COLS, channels)
        part_ref[rows, 1] = finish([0, 1], taps, 1, 1).reshape(block, COLS, channels)
        part_ref[rows, 0] = finish([0], 2 * taps, 0, 1).reshape(block, COLS, channels)

    def step(number, windows, first, act, next_windows, next_first, next_act):
        sums = convolve_first((number + 1) * block + 2, block, windows)
        for row in range(2):
            next_act[row] = act[block + row]
        next_first[: 2 * size, :] = first[block * size :, :]
        activate(sums, block, 2, next_first, next_act)
        convolve(number, first, act)
        fill_block((number + 2) * block + 2, block, next_windows)
        copy_out(number).start()

    fill_block(0, block + 2, windows_b)
    activate(convolve_first(0, block + 2, windows_b), block + 2, 0, first_a, act_a)
    fill_block(block + 2, block, windows_a)
    for copy in copies:
        copy.wait()
    used = lax.div(live + block - 1, block)

    def two_steps(pair, carry):
        step(2 * pair, windows_a, first_a, act_a, windows_b, first_b, act_b)

        @pl.when(2 * pair + 1 < used)
        def _():
            step(2 * pair + 1, windows_b, first_b, act_b, windows_a, first_a, act_a)

        return carry

    lax.fori_loop(0, lax.div(used + 1, 2), two_steps, 0)

    def clear(number, carry):
        late[pl.ds(number * block, block)] = jnp.zeros((block, 2, COLS, channels), BF16)
        copy_out(number).start()
        return carry

    lax.fori_loop(used, blocks, clear, 0)
    for number in range(blocks):
        copy_out(number).wait()


def cached_frames(
    bands, part_ref, weights, late_ref, *refs,
    owners, units, capacity, height, block, band_max, channels,
):
    del late_ref
    parts, (out_ref, cache, early, out_sems, cache_sems) = refs[:owners], refs[owners:]
    group = lax.axis_index("seq")
    owner = lax.axis_index("dec")
    live = bands[group, owner]
    start = band_start(bands, group, owner, owners)
    depth = channels // LANES
    blocks = band_max // block
    edge = lax.rem(height - lax.rem(start - 1 + height, height), height)

    def slot_of(at):
        row = jnp.clip(start - 1 + at, 0, units * owners - 1)
        source = lax.rem(row, owners)
        unit = first_unit(start, 1, source, owners, units, capacity)
        return source * capacity + jnp.clip(lax.div(row, owners) - unit, 0, capacity - 1)

    def copy_out(number):
        rows = pl.ds(number * block, block)
        return pltpu.make_async_copy(
            early.at[rows], out_ref.at[rows, pl.ds(0, 2)], out_sems.at[number]
        )

    copies = []
    for other, part in enumerate(parts):
        into = cache.at[pl.ds((owner ^ other) * capacity, capacity)]
        copies.append(pltpu.make_async_copy(part, into, cache_sems.at[other]))
    for copy in copies:
        copy.start()
    slots = owners * capacity
    cache[slots] = jnp.zeros(cache.shape[1:], BF16)
    for copy in copies:
        copy.wait()
    used = lax.div(live + block - 1, block)

    def convolve(number, carry):
        begin = number * block
        source_rows = [[], [], []]
        for row in range(block):
            at = begin + row + 1
            is_first = (at == edge) | (at == edge + height)
            is_last = (at == edge - 1) | (at == edge - 1 + height)
            source_rows[0].append(jnp.where(is_first, slots, slot_of(at - 1)))
            source_rows[1].append(slot_of(at))
            source_rows[2].append(jnp.where(is_last, slots, slot_of(at + 1)))

        def slab(frames):
            pieces = []
            for frame in frames:
                for row_tap in range(3):
                    for part in range(depth):
                        tile = pl.ds((frame * depth + part) * COLS, COLS)
                        values = [cache[at, tile, :] for at in source_rows[row_tap]]
                        pieces.append(jnp.concatenate(values, axis=0))
            return jnp.concatenate(pieces, axis=1)

        at_row = lax.broadcasted_iota(jnp.int32, (block * COLS, channels), 0) // COLS
        taps = 3 * channels
        rows = pl.ds(begin, block)
        for frame, frames in ((0, (0, 1)), (1, (1,))):
            sums = jnp.dot(
                slab(frames), weights[: len(frames) * taps, :], preferred_element_type=F32
            )
            total = shift_columns(sums, channels) + part_ref[rows, frame].reshape(
                block * COLS, channels
            )
            total = jnp.where(at_row < live - begin, total, 0.0)
            early[rows, frame] = total.astype(BF16).reshape(block, COLS, channels)
        copy_out(number).start()
        return carry

    lax.fori_loop(0, used, convolve, 0)

    def clear(number, carry):
        early[pl.ds(number * block, block)] = jnp.zeros((block, 2, COLS, channels), BF16)
        copy_out(number).start()
        return carry

    lax.fori_loop(used, blocks, clear, 0)
    for number in range(blocks):
        copy_out(number).wait()


def params(mebibytes, **extra):
    return pltpu.CompilerParams(vmem_limit_bytes=mebibytes * 1024 * 1024, **extra)


def shards(latents, cache_lat, cache_act, w_in, w_mid, norm_gain, clip_group, band_rows):
    groups = lax.axis_size("seq")
    owners = lax.axis_size("dec")
    clips = latents.shape[1]
    per_owner = latents.shape[2]
    channels = w_mid.shape[2]
    units = groups * per_owner
    height = per_owner * owners
    stack_rows = groups * height
    band_max = 2 * stack_rows // owners
    act_capacity = (band_max + 2 + owners - 1) // owners
    block = next(size for size in (16, 8) if band_max % size == 0)
    any_space = pl.BlockSpec(memory_space=pl.ANY)
    in_vmem = pl.BlockSpec(memory_space=pltpu.VMEM)
    in_hbm = pl.BlockSpec(memory_space=pltpu.HBM)

    def rows_first(array):
        return jnp.transpose(array[0, :, :, 0, :], (1, 0, 2))

    lat, old, act = rows_first(latents), rows_first(cache_lat), rows_first(cache_act)
    tiles = act.shape[2] // LANES
    lat_rows = (per_owner * 12 + 15) // 16 * 16
    per_step = 3
    packed = pl.pallas_call(
        functools.partial(
            pack_clips, per_owner=per_owner, per_step=per_step, clips=clips
        ),
        grid_spec=pltpu.PrefetchScalarGridSpec(
            num_scalar_prefetch=1,
            grid=(),
            in_specs=[in_hbm, in_hbm, in_hbm],
            out_specs=[in_vmem] * (2 * clips),
            scratch_shapes=[
                pltpu.VMEM(lat.shape, BF16),
                pltpu.VMEM(old.shape, BF16),
                pltpu.VMEM(act.shape, BF16),
                pltpu.VMEM((clips * lat_rows, LANES), F32),
                pltpu.VMEM((2, clips * per_step * tiles, LANES), F32),
                pltpu.SemaphoreType.DMA((2 + per_owner // per_step,)),
            ],
        ),
        out_shape=[jax.ShapeDtypeStruct((lat_rows, LANES), BF16)] * clips
        + [jax.ShapeDtypeStruct((per_owner * tiles, LANES), BF16)] * clips,
        compiler_params=params(56),
        name="pack_clips",
    )(clip_group, lat, old, act)

    def trade(parts, axis):
        count = lax.axis_size(axis)
        return [parts[0]] + [
            lax.ppermute(part, axis, [(i, i ^ other) for i in range(count)])
            for other, part in enumerate(parts)
            if other
        ]

    traded_lat, packed_act = lax.optimization_barrier(
        (trade(packed[:clips], "seq"), packed[clips:])
    )
    traded_act = trade(packed_act, "seq")
    lat_capacity = (band_max + 4 + owners - 1) // owners
    slice_rows = (lat_capacity * 12 + 15) // 16 * 16
    band_lat = pl.pallas_call(
        functools.partial(
            slice_latents, owners=owners, units=units, capacity=lat_capacity, per_owner=per_owner,
            groups=groups,
        ),
        grid_spec=pltpu.PrefetchScalarGridSpec(
            num_scalar_prefetch=1,
            grid=(),
            in_specs=[in_vmem] * clips,
            out_specs=[in_vmem] * owners,
            scratch_shapes=[pltpu.VMEM((units * 12 + slice_rows, LANES), F32)],
        ),
        out_shape=[jax.ShapeDtypeStruct((slice_rows, LANES), BF16)] * owners,
        compiler_params=params(16),
        name="slice_latents",
    )(band_rows, *traded_lat)
    band_lat = trade(band_lat, "dec")
    band_act = pl.pallas_call(
        functools.partial(
            slice_caches, owners=owners, units=units, capacity=act_capacity, tiles=tiles,
            groups=groups,
        ),
        grid_spec=pltpu.PrefetchScalarGridSpec(
            num_scalar_prefetch=1,
            grid=(),
            in_specs=[any_space] * clips,
            out_specs=[in_vmem] * owners,
            scratch_shapes=[
                pltpu.VMEM((units * tiles, LANES), BF16),
                pltpu.SemaphoreType.DMA((clips,)),
                pltpu.SemaphoreType.DMA((owners,)),
            ],
        ),
        out_shape=[jax.ShapeDtypeStruct((act_capacity * tiles, LANES), BF16)] * owners,
        compiler_params=params(16),
        name="slice_caches",
    )(band_rows, *traded_act)
    band_lat, band_act = lax.optimization_barrier((band_lat, band_act))
    band_act = trade(band_act, "dec")

    late, part, wide_mid = pl.pallas_call(
        functools.partial(
            new_frames, owners=owners, units=units, capacity=lat_capacity, height=height,
            block=block, band_max=band_max, channels=channels,
        ),
        grid_spec=pltpu.PrefetchScalarGridSpec(
            num_scalar_prefetch=1,
            grid=(),
            in_specs=[in_vmem, in_vmem, in_hbm] + [in_vmem] * owners,
            out_specs=[in_hbm, in_vmem, in_vmem],
            scratch_shapes=[
                pltpu.VMEM((6 * LANES, channels), BF16),
                pltpu.VMEM((2, owners * slice_rows, LANES), F32),
                pltpu.VMEM((block + 5, F * COLS, 2 * LANES), BF16),
                pltpu.VMEM((block + 5, F * COLS, 2 * LANES), BF16),
                pltpu.VMEM(((block + 2) * F * COLS, channels), F32),
                pltpu.VMEM(((block + 2) * F * COLS, channels), F32),
                pltpu.VMEM((block + 3, F, COLS, channels), BF16),
                pltpu.VMEM((block + 3, F, COLS, channels), BF16),
                pltpu.VMEM((band_max, 2, COLS, channels), BF16),
                pltpu.SemaphoreType.DMA((band_max // block,)),
                pltpu.SemaphoreType.DMA((27,)),
            ],
        ),
        out_shape=[
            jax.ShapeDtypeStruct((band_max, F, COLS, channels), BF16),
            jax.ShapeDtypeStruct((band_max, 2, COLS, channels), F32),
            jax.ShapeDtypeStruct((9 * channels, 3 * channels), BF16),
        ],
        compiler_params=params(36),
        cost_estimate=pl.CostEstimate(
            flops=2 * band_max * 9 * COLS * 9 * channels * channels,
            bytes_accessed=16 * 1024 * 1024,
            transcendentals=0,
        ),
        name="new_frames",
    )(band_rows, w_in, norm_gain.reshape(1, channels), w_mid, *band_lat)

    slots = owners * act_capacity
    band_act = [rows.reshape(act_capacity, tiles, LANES) for rows in band_act]
    decoded = pl.pallas_call(
        functools.partial(
            cached_frames, owners=owners, units=units, capacity=act_capacity, height=height,
            block=block, band_max=band_max, channels=channels,
        ),
        grid_spec=pltpu.PrefetchScalarGridSpec(
            num_scalar_prefetch=1,
            grid=(),
            in_specs=[in_vmem, in_vmem, in_hbm] + [any_space] * owners,
            out_specs=in_hbm,
            scratch_shapes=[
                pltpu.VMEM((slots + 1, tiles, LANES), BF16),
                pltpu.VMEM((band_max, 2, COLS, channels), BF16),
                pltpu.SemaphoreType.DMA((band_max // block,)),
                pltpu.SemaphoreType.DMA((owners,)),
            ],
        ),
        out_shape=jax.ShapeDtypeStruct((band_max, F, COLS, channels), BF16),
        input_output_aliases={3: 0},
        compiler_params=params(24),
        cost_estimate=pl.CostEstimate(
            flops=2 * band_max * 3 * COLS * 9 * channels * channels,
            bytes_accessed=16 * 1024 * 1024,
            transcendentals=0,
        ),
        name="cached_frames",
    )(band_rows, part, wide_mid, late, *band_act)
    return decoded.reshape((1, 1) + decoded.shape)


def solution(mesh):
    placed = (
        P("seq", None, None, "dec", None),
        P("seq", None, None, "dec", None),
        P("seq", None, None, "dec", None),
        P(),
        P(),
        P(),
        P(),
        P(),
    )
    return jax.shard_map(
        shards,
        mesh=mesh,
        in_specs=placed,
        out_specs=P("seq", "dec", None, None, None, None),
        check_vma=False,
    )
```

```python
import functools

import jax
import jax.numpy as jnp
from jax import lax
from jax.experimental import pallas as pl
from jax.experimental.pallas import tpu as pltpu
from jax.sharding import PartitionSpec as P

F = 4
CT = 2
COLS = 16
LANES = 128
EPSILON = 1e-06
F32 = jnp.float32
BF16 = jnp.bfloat16


def band_start(bands, group, owner, owners):
    total = jnp.int32(0)
    for other in range(owners):
        total = total + jnp.where(other < owner, bands[group, other], 0)
    return total


def first_unit(start, margin, source, owners, units, capacity):
    unit = (start - margin - source + owners - 1 + 2 * owners) // owners - 2
    return jnp.clip(unit, 0, units - capacity)


def clip_of(groups_ref, shard, group, clips):
    found = jnp.int32(0)
    for clip in range(clips):
        found = found + jnp.where(groups_ref[shard, clip] == group, clip, 0)
    return found


def pack_clips(groups_ref, lat_in, old_in, act_in, *refs, per_owner, per_step, clips):
    *outs, lat_ref, old_ref, act_ref, lat_scratch, act_scratch, sems = refs
    shard = lax.axis_index("seq")
    copies = [
        pltpu.make_async_copy(lat_in, lat_ref, sems.at[0]),
        pltpu.make_async_copy(old_in, old_ref, sems.at[1]),
    ]
    steps = per_owner // per_step
    for step in range(steps):
        rows = pl.ds(step * per_step, per_step)
        copies.append(
            pltpu.make_async_copy(act_in.at[rows], act_ref.at[rows], sems.at[2 + step])
        )
    for copy in copies:
        copy.start()
    chosen = [clip_of(groups_ref, shard, shard ^ other, clips) for other in range(clips)]
    tiles = act_ref.shape[2] // LANES
    depth = tiles // (CT * COLS)
    size = per_step * tiles
    lat_rows = outs[0].shape[0] - per_owner * tiles
    copies[0].wait()
    copies[1].wait()
    for row in range(per_owner):
        for frame in range(CT + F):
            for half in range(2):
                if frame < CT:
                    tile = frame * 2 + half
                    value = old_ref[row, :, tile * LANES : (tile + 1) * LANES]
                else:
                    tile = (frame - CT) * 2 + half
                    value = lat_ref[row, :, tile * LANES : (tile + 1) * LANES]
                at = row * 12 + half * (CT + F) + frame
                lat_scratch[pl.ds(at, clips, stride=lat_rows), :] = value.astype(F32)
    for out, clip in zip(outs, chosen):
        rows = pl.ds(pl.multiple_of(clip * lat_rows, 8), lat_rows)
        out[per_owner * tiles :, :] = lat_scratch[rows, :].astype(BF16)
    for step in range(steps):
        copies[2 + step].wait()
        for row in range(per_step):
            for frame in range(CT):
                for col in range(COLS):
                    for part in range(depth):
                        tile = (frame * COLS + col) * depth + part
                        at = row * tiles + (frame * depth + part) * COLS + col
                        value = act_ref[
                            step * per_step + row, :, tile * LANES : (tile + 1) * LANES
                        ]
                        act_scratch[step % 2, pl.ds(at, clips, stride=size), :] = value.astype(F32)
        for out, clip in zip(outs, chosen):
            rows = pl.ds(pl.multiple_of(clip * size, 8), size)
            out[step * size : (step + 1) * size, :] = act_scratch[step % 2, rows, :].astype(BF16)


def slice_bands(
    bands, _, *refs, owners, units, lat_capacity, act_capacity, per_owner, tiles, groups
):
    ins, lat_outs, act_outs = refs[:groups], refs[groups : groups + owners], refs[groups + owners : -4]
    lat_scratch, scratch, in_sems, sems = refs[-4:]
    group = lax.axis_index("seq")
    source = lax.axis_index("dec")
    size = per_owner * tiles
    copies = []
    for other, in_ref in enumerate(ins):
        into = scratch.at[pl.ds(pl.multiple_of((group ^ other) * size, 16), size)]
        copies.append(pltpu.make_async_copy(in_ref.at[pl.ds(0, size)], into, in_sems.at[other]))
    for copy in copies:
        copy.start()
    rows = lat_outs[0].shape[0]
    lat_size = per_owner * 12
    for other, in_ref in enumerate(ins):
        value = in_ref[size : size + lat_size, :].astype(F32)
        lat_scratch[pl.ds((group ^ other) * lat_size, lat_size), :] = value
    value = pltpu.roll(lat_scratch[: units * 12, :], 64, 1)
    lane = lax.broadcasted_iota(jnp.int32, value.shape, 1)
    for width in (32, 16):
        up, down = pltpu.roll(value, width, 1), pltpu.roll(value, LANES - width, 1)
        value = jnp.where(lane & width == 0, down, up)
    lat_scratch[: units * 12, :] = value
    starts = [band_start(bands, group, source ^ other, owners) for other in range(owners)]
    for copy in copies:
        copy.wait()
    copies = []
    into = [(act_outs[0], 0), (lat_outs[1], 0), (act_outs[1], 0), (act_outs[1], 1)]
    into += [(out, 0) for out in act_outs[2:]]
    length = act_capacity * tiles
    for other, (out_ref, place) in enumerate(into):
        unit = first_unit(starts[other], 1, source, owners, units, act_capacity)
        rows_in = pl.ds(pl.multiple_of(unit * tiles, 16), length)
        rows_out = pl.ds(place * length, length)
        copies.append(
            pltpu.make_async_copy(scratch.at[rows_in], out_ref.at[rows_out], sems.at[other])
        )
    for copy in copies:
        copy.start()
    for other, out_ref in enumerate(lat_outs):
        unit = first_unit(starts[other], 2, source, owners, units, lat_capacity)
        value = lat_scratch[pl.ds(unit * 12, rows), :].astype(BF16)
        out_ref[pl.ds(length if other == 1 else 0, rows), :] = value
    for copy in copies:
        copy.wait()


def shift_columns(sums, width):
    rows = sums.shape[0]
    col = lax.rem(lax.broadcasted_iota(jnp.int32, (rows, width), 0), COLS)
    left = pltpu.roll(sums[:, :width], 1, 0)
    right = pltpu.roll(sums[:, 2 * width :], rows - 1, 0)
    total = sums[:, width : 2 * width] + jnp.where(col > 0, left, 0.0)
    return total + jnp.where(col < COLS - 1, right, 0.0)


def widen_weights(mid_ref, out_ref, mark, sems):
    channels = mid_ref.shape[1]
    mark[...] = jnp.zeros(mark.shape, F32)
    copies = []
    for tap in range(27):
        into = out_ref.at[
            pl.ds(tap // 3 * channels, channels), pl.ds(tap % 3 * channels, channels)
        ]
        copies.append(pltpu.make_async_copy(mid_ref.at[tap], into, sems.at[tap]))
    for copy in copies:
        copy.start()
    for copy in copies:
        copy.wait()


def new_frames(
    bands, win_ref, gain_ref, weights, *refs,
    owners, units, capacity, height, block, band_max, channels, cache_rows,
):
    group = lax.axis_index("seq")
    owner = lax.axis_index("dec")
    lat_refs, refs = refs[:owners], refs[owners:]
    out_ref, part_ref, table, xs, windows_a, windows_b, first_a, first_b = refs[:8]
    act_a, act_b, late, out_sems = refs[8:]
    live = bands[group, owner]
    start = band_start(bands, group, owner, owners)
    edge = lax.rem(height - lax.rem(start - 1 + height, height), height)
    blocks = band_max // block
    size = F * COLS
    per_source = lat_refs[0].shape[0]
    table[...] = jnp.zeros(table.shape, BF16)
    for time_tap in range(3):
        for row_tap in range(3):
            for col_tap in range(3):
                into = row_tap * 2 * LANES + (0, 64, LANES)[time_tap]
                into += ((0, 112, 96), (0, -16, -32), (0, 112, 96))[time_tap][col_tap]
                table[pl.ds(into, 16), :] = win_ref[time_tap * 9 + row_tap * 3 + col_tap]
    for other, lat_ref in enumerate(lat_refs):
        from_row = lat_ref.shape[0] - per_source if other != 1 else cache_rows
        value = lat_ref[pl.ds(from_row, per_source), :].astype(F32)
        rows = pl.ds(pl.multiple_of((owner ^ other) * per_source, 8), per_source)
        xs[0, rows, :] = value
        xs[1, rows, :] = pltpu.roll(value, 64, 1)
    window_zero, act_zero = block + 4, block + 2
    for windows in (windows_a, windows_b):
        windows[window_zero] = jnp.zeros(windows.shape[1:], BF16)
    for act in (act_a, act_b):
        act[act_zero] = jnp.zeros((F, COLS, channels), BF16)
    half_gain = 0.5 * gain_ref[...]

    def clip_edges(at):
        is_first = (at == edge) | (at == edge + height)
        is_last = (at == edge - 1) | (at == edge - 1 + height)
        return is_first, is_last

    def fill(row, windows, into):
        lane = lax.broadcasted_iota(jnp.int32, (8, LANES), 1)
        col = lax.broadcasted_iota(jnp.int32, (8, LANES), 0)
        low = (lane < 16) | (lane >= 96)
        left_end = (col == 0) & ((lane & 63) < 16)
        right_end = (col == 7) & ((lane & 63) >= 32) & ((lane & 63) < 48)
        stack_row = jnp.clip(start - 2 + row, 0, units * owners - 1)
        source = lax.rem(stack_row, owners)
        unit = first_unit(start, 2, source, owners, units, capacity)
        slot = jnp.clip(lax.div(stack_row, owners) - unit, 0, capacity - 1)
        base = source * per_source + slot * 12
        rolled = [{}, {}]
        for frame in range(CT + F):
            for half in range(2):
                at_row = pl.ds(base + half * (CT + F) + frame, 1)
                for turn in range(2):
                    if turn == 1 and not 1 <= frame <= F:
                        continue
                    value = jnp.broadcast_to(xs[turn, at_row, :], (8, LANES))
                    rolled[turn][half, frame] = pltpu.roll(value, 0, 1, stride=16, stride_axis=0)
        for frame in range(F):
            pair = [
                jnp.where(low, rolled[0][half, frame], rolled[1][half, frame + 1])
                for half in range(2)
            ]
            last = [rolled[0][half, frame + 2] for half in range(2)]
            for lanes, (left, right) in enumerate((pair, last)):
                near = jnp.where(left_end, 0.0, jnp.where(right_end, right, left))
                far = jnp.where(right_end, 0.0, jnp.where(left_end, left, right))
                windows[
                    into,
                    frame * COLS : (frame + 1) * COLS,
                    lanes * LANES : (lanes + 1) * LANES,
                ] = jnp.concatenate([near, far], axis=0).astype(BF16)

    def fill_block(row, count, windows):
        for at in range(count + 2):
            fill(row + at, windows, at)

    def convolve_first(row, count, windows):
        pieces = [[], [], []]
        for at in range(count):
            is_first, is_last = clip_edges(row + at)
            pieces[0].append(windows[jnp.where(is_first, window_zero, at)])
            pieces[1].append(windows[at + 1])
            pieces[2].append(windows[jnp.where(is_last, window_zero, at + 2)])
        slab = jnp.concatenate([jnp.concatenate(part, axis=0) for part in pieces], axis=1)
        return jnp.dot(slab, table[...], preferred_element_type=F32)

    def activate(sums, count, into, first, act):
        first[into * size : (into + count) * size, :] = sums
        for at in range(count):
            value = sums[at * size : (at + 1) * size]
            mean_square = jnp.mean(value * value, axis=-1, keepdims=True)
            half = value * lax.rsqrt(mean_square + EPSILON) * half_gain
            value = half + half * jnp.tanh(half)
            act[into + at] = value.astype(BF16).reshape(F, COLS, channels)

    def copy_out(number):
        rows = pl.ds(number * block, block)
        return pltpu.make_async_copy(
            late.at[rows], out_ref.at[rows, pl.ds(2, 2)], out_sems.at[number]
        )

    def convolve(number, first, act):
        begin = number * block
        source_rows = [[], [], []]
        for row in range(block):
            is_first, is_last = clip_edges(begin + row + 1)
            source_rows[0].append(jnp.where(is_first, act_zero, row))
            source_rows[1].append(row + 1)
            source_rows[2].append(jnp.where(is_last, act_zero, row + 2))

        def finish(frames, weight_from, frame_from, count):
            pieces = []
            for frame in frames:
                for row_tap in range(3):
                    parts = [
                        act[at, frame : frame + count].reshape(count * COLS, channels)
                        for at in source_rows[row_tap]
                    ]
                    pieces.append(jnp.concatenate(parts, axis=0))
            slab = jnp.concatenate(pieces, axis=1)
            sums = jnp.dot(slab, weights[weight_from:, :], preferred_element_type=F32)
            total = shift_columns(sums, channels)
            parts = []
            for row in range(block):
                at = (row + 1) * size + frame_from * COLS
                parts.append(first[at : at + count * COLS, :])
            return total + jnp.concatenate(parts, axis=0)

        taps = 3 * channels
        rows = pl.ds(begin, block)
        value = finish([0, 1, 2], 0, 2, 2)
        at_row = lax.broadcasted_iota(jnp.int32, value.shape, 0) // (2 * COLS)
        value = jnp.where(at_row < live - begin, value, 0.0)
        late[rows] = value.astype(BF16).reshape(block, 2, COLS, channels)
        part_ref[rows, 1] = finish([0, 1], taps, 1, 1).reshape(block, COLS, channels)
        part_ref[rows, 0] = finish([0], 2 * taps, 0, 1).reshape(block, COLS, channels)

    def step(number, windows, first, act, next_windows, next_first, next_act):
        sums = convolve_first((number + 1) * block + 2, block, windows)
        for row in range(2):
            next_act[row] = act[block + row]
        next_first[: 2 * size, :] = first[block * size :, :]
        activate(sums, block, 2, next_first, next_act)
        convolve(number, first, act)
        fill_block((number + 2) * block + 2, block, next_windows)
        copy_out(number).start()

    fill_block(0, block + 2, windows_b)
    activate(convolve_first(0, block + 2, windows_b), block + 2, 0, first_a, act_a)
    fill_block(block + 2, block, windows_a)
    used = lax.div(live + block - 1, block)

    def two_steps(pair, carry):
        step(2 * pair, windows_a, first_a, act_a, windows_b, first_b, act_b)

        @pl.when(2 * pair + 1 < used)
        def _():
            step(2 * pair + 1, windows_b, first_b, act_b, windows_a, first_a, act_a)

        return carry

    lax.fori_loop(0, lax.div(used + 1, 2), two_steps, 0)

    def clear(number, carry):
        late[pl.ds(number * block, block)] = jnp.zeros((block, 2, COLS, channels), BF16)
        copy_out(number).start()
        return carry

    lax.fori_loop(used, blocks, clear, 0)
    for number in range(blocks):
        copy_out(number).wait()


def cached_frames(
    bands, part_ref, weights, late_ref, *refs,
    owners, units, capacity, height, block, band_max, channels,
):
    del late_ref
    parts, (out_ref, cache, early, out_sems, cache_sems) = refs[:owners], refs[owners:]
    group = lax.axis_index("seq")
    owner = lax.axis_index("dec")
    live = bands[group, owner]
    start = band_start(bands, group, owner, owners)
    depth = channels // LANES
    blocks = band_max // block
    edge = lax.rem(height - lax.rem(start - 1 + height, height), height)

    def slot_of(at):
        row = jnp.clip(start - 1 + at, 0, units * owners - 1)
        source = lax.rem(row, owners)
        unit = first_unit(start, 1, source, owners, units, capacity)
        return source * capacity + jnp.clip(lax.div(row, owners) - unit, 0, capacity - 1)

    def copy_out(number):
        rows = pl.ds(number * block, block)
        return pltpu.make_async_copy(
            early.at[rows], out_ref.at[rows, pl.ds(0, 2)], out_sems.at[number]
        )

    copies = []
    for other, part in enumerate(parts):
        into = cache.at[pl.ds((owner ^ other) * capacity, capacity)]
        arrived = part.at[pl.ds(0, capacity)]
        copies.append(pltpu.make_async_copy(arrived, into, cache_sems.at[other]))
    for copy in copies:
        copy.start()
    slots = owners * capacity
    cache[slots] = jnp.zeros(cache.shape[1:], BF16)
    for copy in copies:
        copy.wait()
    used = lax.div(live + block - 1, block)

    def convolve(number, carry):
        begin = number * block
        source_rows = [[], [], []]
        for row in range(block):
            at = begin + row + 1
            is_first = (at == edge) | (at == edge + height)
            is_last = (at == edge - 1) | (at == edge - 1 + height)
            source_rows[0].append(jnp.where(is_first, slots, slot_of(at - 1)))
            source_rows[1].append(slot_of(at))
            source_rows[2].append(jnp.where(is_last, slots, slot_of(at + 1)))

        def slab(frames):
            pieces = []
            for frame in frames:
                for row_tap in range(3):
                    for part in range(depth):
                        tile = pl.ds((frame * depth + part) * COLS, COLS)
                        values = [cache[at, tile, :] for at in source_rows[row_tap]]
                        pieces.append(jnp.concatenate(values, axis=0))
            return jnp.concatenate(pieces, axis=1)

        at_row = lax.broadcasted_iota(jnp.int32, (block * COLS, channels), 0) // COLS
        taps = 3 * channels
        rows = pl.ds(begin, block)
        for frame, frames in ((0, (0, 1)), (1, (1,))):
            sums = jnp.dot(
                slab(frames), weights[: len(frames) * taps, :], preferred_element_type=F32
            )
            total = shift_columns(sums, channels) + part_ref[rows, frame].reshape(
                block * COLS, channels
            )
            total = jnp.where(at_row < live - begin, total, 0.0)
            early[rows, frame] = total.astype(BF16).reshape(block, COLS, channels)
        copy_out(number).start()
        return carry

    lax.fori_loop(0, used, convolve, 0)

    def clear(number, carry):
        early[pl.ds(number * block, block)] = jnp.zeros((block, 2, COLS, channels), BF16)
        copy_out(number).start()
        return carry

    lax.fori_loop(used, blocks, clear, 0)
    for number in range(blocks):
        copy_out(number).wait()


def params(mebibytes, **extra):
    return pltpu.CompilerParams(vmem_limit_bytes=mebibytes * 1024 * 1024, **extra)


def shards(latents, cache_lat, cache_act, w_in, w_mid, norm_gain, clip_group, band_rows):
    groups = lax.axis_size("seq")
    owners = lax.axis_size("dec")
    clips = latents.shape[1]
    per_owner = latents.shape[2]
    channels = w_mid.shape[2]
    units = groups * per_owner
    height = per_owner * owners
    stack_rows = groups * height
    band_max = 2 * stack_rows // owners
    act_capacity = (band_max + 2 + owners - 1) // owners
    block = next(size for size in (16, 8) if band_max % size == 0)
    any_space = pl.BlockSpec(memory_space=pl.ANY)
    in_vmem = pl.BlockSpec(memory_space=pltpu.VMEM)
    in_hbm = pl.BlockSpec(memory_space=pltpu.HBM)

    def rows_first(array):
        return jnp.transpose(array[0, :, :, 0, :], (1, 0, 2))

    lat, old, act = rows_first(latents), rows_first(cache_lat), rows_first(cache_act)
    tiles = act.shape[2] // LANES
    lat_rows = (per_owner * 12 + 15) // 16 * 16
    per_step = 3
    packed = pl.pallas_call(
        functools.partial(
            pack_clips, per_owner=per_owner, per_step=per_step, clips=clips
        ),
        grid_spec=pltpu.PrefetchScalarGridSpec(
            num_scalar_prefetch=1,
            grid=(),
            in_specs=[in_hbm, in_hbm, in_hbm],
            out_specs=[in_vmem] * clips,
            scratch_shapes=[
                pltpu.VMEM(lat.shape, BF16),
                pltpu.VMEM(old.shape, BF16),
                pltpu.VMEM(act.shape, BF16),
                pltpu.VMEM((clips * lat_rows, LANES), F32),
                pltpu.VMEM((2, clips * per_step * tiles, LANES), F32),
                pltpu.SemaphoreType.DMA((2 + per_owner // per_step,)),
            ],
        ),
        out_shape=[jax.ShapeDtypeStruct((per_owner * tiles + lat_rows, LANES), BF16)] * clips,
        compiler_params=params(56),
        name="pack_clips",
    )(clip_group, lat, old, act)

    def trade(parts, axis):
        count = lax.axis_size(axis)
        return [parts[0]] + [
            lax.ppermute(part, axis, [(i, i ^ other) for i in range(count)])
            for other, part in enumerate(parts)
            if other
        ]

    traded = trade(packed, "seq")
    wide_mid, mark = pl.pallas_call(
        widen_weights,
        in_specs=[in_hbm],
        out_specs=[in_vmem, in_vmem],
        scratch_shapes=[pltpu.SemaphoreType.DMA((27,))],
        out_shape=[
            jax.ShapeDtypeStruct((9 * channels, 3 * channels), BF16),
            jax.ShapeDtypeStruct((8, LANES), F32),
        ],
        compiler_params=params(16),
        cost_estimate=pl.CostEstimate(
            flops=0, bytes_accessed=4 * 27 * channels * channels, transcendentals=0
        ),
        name="widen_weights",
    )(w_mid)
    lat_capacity = (band_max + 4 + owners - 1) // owners
    slice_rows = (lat_capacity * 12 + 15) // 16 * 16
    slice_both = (act_capacity * tiles + slice_rows + tiles - 1) // tiles * tiles
    slice_act = jax.ShapeDtypeStruct((act_capacity * tiles, LANES), BF16)
    slice_two = jax.ShapeDtypeStruct((2 * act_capacity * tiles, LANES), BF16)
    sliced = pl.pallas_call(
        functools.partial(
            slice_bands, owners=owners, units=units, lat_capacity=lat_capacity,
            act_capacity=act_capacity, per_owner=per_owner, tiles=tiles, groups=groups,
        ),
        grid_spec=pltpu.PrefetchScalarGridSpec(
            num_scalar_prefetch=1,
            grid=(),
            in_specs=[in_vmem] * (1 + clips),
            out_specs=[in_vmem] * (2 * owners - 2),
            scratch_shapes=[
                pltpu.VMEM((units * 12 + slice_rows, LANES), F32),
                pltpu.VMEM((units * tiles, LANES), BF16),
                pltpu.SemaphoreType.DMA((clips,)),
                pltpu.SemaphoreType.DMA((owners,)),
            ],
        ),
        out_shape=[
            jax.ShapeDtypeStruct((slice_both if other == 1 else slice_rows, LANES), BF16)
            for other in range(owners)
        ]
        + [slice_act, slice_two]
        + [slice_act] * (owners - 4),
        compiler_params=params(16),
        name="slice_bands",
    )(band_rows, mark, *traded)
    band_lat, band_act = lax.optimization_barrier(
        (trade(sliced[:owners], "dec"), sliced[owners:])
    )

    def send(part, other):
        return lax.ppermute(part, "dec", [(i, i ^ other) for i in range(owners)])

    own, *band_act = band_act
    far = [send(part, other) for other, part in enumerate(band_act[1:], 4)]
    two = send(band_act[0], 2)

    late, part = pl.pallas_call(
        functools.partial(
            new_frames, owners=owners, units=units, capacity=lat_capacity, height=height,
            block=block, band_max=band_max, channels=channels, cache_rows=act_capacity * tiles,
        ),
        grid_spec=pltpu.PrefetchScalarGridSpec(
            num_scalar_prefetch=1,
            grid=(),
            in_specs=[in_vmem] * (3 + owners),
            out_specs=[in_hbm, in_vmem],
            scratch_shapes=[
                pltpu.VMEM((6 * LANES, channels), BF16),
                pltpu.VMEM((2, owners * slice_rows, LANES), F32),
                pltpu.VMEM((block + 5, F * COLS, 2 * LANES), BF16),
                pltpu.VMEM((block + 5, F * COLS, 2 * LANES), BF16),
                pltpu.VMEM(((block + 2) * F * COLS, channels), F32),
                pltpu.VMEM(((block + 2) * F * COLS, channels), F32),
                pltpu.VMEM((block + 3, F, COLS, channels), BF16),
                pltpu.VMEM((block + 3, F, COLS, channels), BF16),
                pltpu.VMEM((band_max, 2, COLS, channels), BF16),
                pltpu.SemaphoreType.DMA((band_max // block,)),
            ],
        ),
        out_shape=[
            jax.ShapeDtypeStruct((band_max, F, COLS, channels), BF16),
            jax.ShapeDtypeStruct((band_max, 2, COLS, channels), F32),
        ],
        compiler_params=params(36),
        cost_estimate=pl.CostEstimate(
            flops=2 * band_max * 9 * COLS * 9 * channels * channels,
            bytes_accessed=16 * 1024 * 1024,
            transcendentals=0,
        ),
        name="new_frames",
    )(band_rows, w_in, norm_gain.reshape(1, channels), wide_mid, *band_lat)

    slots = owners * act_capacity
    two, part = lax.optimization_barrier((two, part))
    handed = send(two[act_capacity * tiles :], 1)
    band_act = [rows.reshape(-1, tiles, LANES) for rows in (own, band_lat[1], two, handed, *far)]
    decoded = pl.pallas_call(
        functools.partial(
            cached_frames, owners=owners, units=units, capacity=act_capacity, height=height,
            block=block, band_max=band_max, channels=channels,
        ),
        grid_spec=pltpu.PrefetchScalarGridSpec(
            num_scalar_prefetch=1,
            grid=(),
            in_specs=[in_vmem, in_vmem, in_hbm] + [any_space] * owners,
            out_specs=in_hbm,
            scratch_shapes=[
                pltpu.VMEM((slots + 1, tiles, LANES), BF16),
                pltpu.VMEM((band_max, 2, COLS, channels), BF16),
                pltpu.SemaphoreType.DMA((band_max // block,)),
                pltpu.SemaphoreType.DMA((owners,)),
            ],
        ),
        out_shape=jax.ShapeDtypeStruct((band_max, F, COLS, channels), BF16),
        input_output_aliases={3: 0},
        compiler_params=params(24),
        cost_estimate=pl.CostEstimate(
            flops=2 * band_max * 3 * COLS * 9 * channels * channels,
            bytes_accessed=16 * 1024 * 1024,
            transcendentals=0,
        ),
        name="cached_frames",
    )(band_rows, part, wide_mid, late, *band_act)
    return decoded.reshape((1, 1) + decoded.shape)


def solution(mesh):
    placed = (
        P("seq", None, None, "dec", None),
        P("seq", None, None, "dec", None),
        P("seq", None, None, "dec", None),
        P(),
        P(),
        P(),
        P(),
        P(),
    )
    return jax.shard_map(
        shards,
        mesh=mesh,
        in_specs=placed,
        out_specs=P("seq", "dec", None, None, None, None),
        check_vma=False,
    )
```

```python
import functools

import jax
import jax.numpy as jnp
from jax import lax
from jax.experimental import pallas as pl
from jax.experimental.pallas import tpu as pltpu
from jax.sharding import PartitionSpec as P

F = 4
CT = 2
COLS = 16
LANES = 128
EPSILON = 1e-06
F32 = jnp.float32
BF16 = jnp.bfloat16


def band_start(bands, group, owner, owners):
    total = jnp.int32(0)
    for other in range(owners):
        total = total + jnp.where(other < owner, bands[group, other], 0)
    return total


def first_unit(start, margin, source, owners, units, capacity):
    unit = (start - margin - source + owners - 1 + 2 * owners) // owners - 2
    return jnp.clip(unit, 0, units - capacity)


def clip_of(groups_ref, shard, group, clips):
    found = jnp.int32(0)
    for clip in range(clips):
        found = found + jnp.where(groups_ref[shard, clip] == group, clip, 0)
    return found


def pack_clips(groups_ref, lat_in, old_in, act_in, *refs, per_owner, per_step, clips):
    *outs, lat_ref, old_ref, act_ref, lat_scratch, act_scratch, sems = refs
    shard = lax.axis_index("seq")
    copies = [
        pltpu.make_async_copy(lat_in, lat_ref, sems.at[0]),
        pltpu.make_async_copy(old_in, old_ref, sems.at[1]),
    ]
    steps = per_owner // per_step
    for step in range(steps):
        rows = pl.ds(step * per_step, per_step)
        copies.append(
            pltpu.make_async_copy(act_in.at[rows], act_ref.at[rows], sems.at[2 + step])
        )
    for copy in copies:
        copy.start()
    chosen = [clip_of(groups_ref, shard, shard ^ other, clips) for other in range(clips)]
    tiles = act_ref.shape[2] // LANES
    depth = tiles // (CT * COLS)
    size = per_step * tiles
    lat_rows = outs[0].shape[0] - per_owner * tiles
    copies[0].wait()
    copies[1].wait()
    for row in range(per_owner):
        for frame in range(CT + F):
            for half in range(2):
                if frame < CT:
                    tile = frame * 2 + half
                    value = old_ref[row, :, tile * LANES : (tile + 1) * LANES]
                else:
                    tile = (frame - CT) * 2 + half
                    value = lat_ref[row, :, tile * LANES : (tile + 1) * LANES]
                at = row * 12 + half * (CT + F) + frame
                lat_scratch[pl.ds(at, clips, stride=lat_rows), :] = value.astype(F32)
    for out, clip in zip(outs, chosen):
        rows = pl.ds(pl.multiple_of(clip * lat_rows, 8), lat_rows)
        out[per_owner * tiles :, :] = lat_scratch[rows, :].astype(BF16)
    for step in range(steps):
        copies[2 + step].wait()
        for row in range(per_step):
            for frame in range(CT):
                for col in range(COLS):
                    for part in range(depth):
                        tile = (frame * COLS + col) * depth + part
                        at = row * tiles + (frame * depth + part) * COLS + col
                        value = act_ref[
                            step * per_step + row, :, tile * LANES : (tile + 1) * LANES
                        ]
                        act_scratch[step % 2, pl.ds(at, clips, stride=size), :] = value.astype(F32)
        for out, clip in zip(outs, chosen):
            rows = pl.ds(pl.multiple_of(clip * size, 8), size)
            out[step * size : (step + 1) * size, :] = act_scratch[step % 2, rows, :].astype(BF16)


def slice_bands(
    bands, _, *refs, owners, units, lat_capacity, act_capacity, per_owner, tiles, groups
):
    ins, lat_out, act_outs = refs[:groups], refs[groups], refs[groups + 1 : -4]
    lat_scratch, scratch, in_sems, sems = refs[-4:]
    group = lax.axis_index("seq")
    source = lax.axis_index("dec")
    size = per_owner * tiles
    copies = []
    for other, in_ref in enumerate(ins):
        into = scratch.at[pl.ds(pl.multiple_of((group ^ other) * size, 16), size)]
        copies.append(pltpu.make_async_copy(in_ref.at[pl.ds(0, size)], into, in_sems.at[other]))
    for copy in copies:
        copy.start()
    rows = lat_out.shape[1]
    lat_size = per_owner * 12
    for other, in_ref in enumerate(ins):
        value = in_ref[size : size + lat_size, :].astype(F32)
        lat_scratch[pl.ds((group ^ other) * lat_size, lat_size), :] = value
    value = pltpu.roll(lat_scratch[: units * 12, :], 64, 1)
    lane = lax.broadcasted_iota(jnp.int32, value.shape, 1)
    for width in (32, 16):
        up, down = pltpu.roll(value, width, 1), pltpu.roll(value, LANES - width, 1)
        value = jnp.where(lane & width == 0, down, up)
    lat_scratch[: units * 12, :] = value
    starts = [band_start(bands, group, source ^ other, owners) for other in range(owners)]
    for copy in copies:
        copy.wait()
    copies = []
    into = [(act_outs[0], 0), (act_outs[1], 0), (act_outs[2], 0), (act_outs[2], 1)]
    into += [(out, 0) for out in act_outs[3:]]
    length = act_capacity * tiles
    for other, (out_ref, place) in enumerate(into):
        unit = first_unit(starts[other], 1, source, owners, units, act_capacity)
        rows_in = pl.ds(pl.multiple_of(unit * tiles, 16), length)
        rows_out = pl.ds(place * length, length)
        copies.append(
            pltpu.make_async_copy(scratch.at[rows_in], out_ref.at[rows_out], sems.at[other])
        )
    for copy in copies:
        copy.start()
    for other in range(owners):
        unit = first_unit(starts[other], 2, source, owners, units, lat_capacity)
        lat_out[source ^ other] = lat_scratch[pl.ds(unit * 12, rows), :].astype(BF16)
    for copy in copies:
        copy.wait()


def shift_columns(sums, width):
    rows = sums.shape[0]
    col = lax.rem(lax.broadcasted_iota(jnp.int32, (rows, width), 0), COLS)
    left = pltpu.roll(sums[:, :width], 1, 0)
    right = pltpu.roll(sums[:, 2 * width :], rows - 1, 0)
    total = sums[:, width : 2 * width] + jnp.where(col > 0, left, 0.0)
    return total + jnp.where(col < COLS - 1, right, 0.0)


def widen_weights(mid_ref, win_ref, out_ref, table, wide, sems, out_sems):
    channels = mid_ref.shape[1]
    copies, stores = [], []
    for tap in range(27):
        rows = pl.ds(tap // 3 * channels, channels)
        into = wide.at[rows, pl.ds(tap % 3 * channels, channels)]
        copies.append(pltpu.make_async_copy(mid_ref.at[tap], into, sems.at[tap]))
        if tap % 3 == 2:
            stores.append(
                pltpu.make_async_copy(wide.at[rows], out_ref.at[rows], out_sems.at[tap // 3])
            )
    for copy in copies:
        copy.start()
    table[...] = jnp.zeros(table.shape, BF16)
    for time_tap in range(3):
        for row_tap in range(3):
            for col_tap in range(3):
                into = row_tap * 2 * LANES + (0, 64, LANES)[time_tap]
                into += ((0, 112, 96), (0, -16, -32), (0, 112, 96))[time_tap][col_tap]
                table[pl.ds(into, 16), :] = win_ref[time_tap * 9 + row_tap * 3 + col_tap]
    for tap, copy in enumerate(copies):
        copy.wait()
        if tap % 3 == 2:
            stores[tap // 3].start()
    for store in stores:
        store.wait()


def new_frames(
    bands, gain_ref, table, lat_ref, mid_ref, *refs,
    owners, units, capacity, height, block, band_max, channels,
):
    group = lax.axis_index("seq")
    owner = lax.axis_index("dec")
    out_ref, part_ref, weights, xs, windows_a, windows_b, first_a, first_b = refs[:8]
    act_a, act_b, late, out_sems, sem = refs[8:]
    load = pltpu.make_async_copy(mid_ref, weights, sem)
    load.start()
    live = bands[group, owner]
    start = band_start(bands, group, owner, owners)
    edge = lax.rem(height - lax.rem(start - 1 + height, height), height)
    blocks = band_max // block
    size = F * COLS
    per_source = lat_ref.shape[1]
    for source in range(owners):
        xs[pl.ds(source * per_source, per_source), :] = lat_ref[source].astype(F32)
    window_zero, act_zero = block + 4, block + 2
    for windows in (windows_a, windows_b):
        windows[window_zero] = jnp.zeros(windows.shape[1:], BF16)
    for act in (act_a, act_b):
        act[act_zero] = jnp.zeros((F, COLS, channels), BF16)
    half_gain = 0.5 * gain_ref[...]

    def clip_edges(at):
        is_first = (at == edge) | (at == edge + height)
        is_last = (at == edge - 1) | (at == edge - 1 + height)
        return is_first, is_last

    def fill(row, windows, into):
        lane = lax.broadcasted_iota(jnp.int32, (8, LANES), 1)
        col = lax.broadcasted_iota(jnp.int32, (8, LANES), 0)
        low = (lane < 16) | (lane >= 96)
        left_end = (col == 0) & ((lane & 63) < 16)
        right_end = (col == 7) & ((lane & 63) >= 32) & ((lane & 63) < 48)
        stack_row = jnp.clip(start - 2 + row, 0, units * owners - 1)
        source = lax.rem(stack_row, owners)
        unit = first_unit(start, 2, source, owners, units, capacity)
        slot = jnp.clip(lax.div(stack_row, owners) - unit, 0, capacity - 1)
        base = source * per_source + slot * 12
        rolled = [{}, {}]
        for frame in range(CT + F):
            for half in range(2):
                at_row = pl.ds(base + half * (CT + F) + frame, 1)
                value = jnp.broadcast_to(xs[at_row, :], (8, LANES))
                rolled[0][half, frame] = pltpu.roll(value, 0, 1, stride=16, stride_axis=0)
                if 1 <= frame <= F:
                    rolled[1][half, frame] = pltpu.roll(rolled[0][half, frame], 64, 1)
        for frame in range(F):
            pair = [
                jnp.where(low, rolled[0][half, frame], rolled[1][half, frame + 1])
                for half in range(2)
            ]
            last = [rolled[0][half, frame + 2] for half in range(2)]
            for lanes, (left, right) in enumerate((pair, last)):
                near = jnp.where(left_end, 0.0, jnp.where(right_end, right, left))
                far = jnp.where(right_end, 0.0, jnp.where(left_end, left, right))
                windows[
                    into,
                    frame * COLS : (frame + 1) * COLS,
                    lanes * LANES : (lanes + 1) * LANES,
                ] = jnp.concatenate([near, far], axis=0).astype(BF16)

    def fill_block(row, count, windows):
        for at in range(count + 2):
            fill(row + at, windows, at)

    def convolve_first(row, count, windows):
        pieces = [[], [], []]
        for at in range(count):
            is_first, is_last = clip_edges(row + at)
            pieces[0].append(windows[jnp.where(is_first, window_zero, at)])
            pieces[1].append(windows[at + 1])
            pieces[2].append(windows[jnp.where(is_last, window_zero, at + 2)])
        slab = jnp.concatenate([jnp.concatenate(part, axis=0) for part in pieces], axis=1)
        return jnp.dot(slab, table[...], preferred_element_type=F32)

    def activate(sums, count, into, first, act):
        first[into * size : (into + count) * size, :] = sums
        for at in range(count):
            value = sums[at * size : (at + 1) * size]
            mean_square = jnp.mean(value * value, axis=-1, keepdims=True)
            half = value * lax.rsqrt(mean_square + EPSILON) * half_gain
            value = half + half * jnp.tanh(half)
            act[into + at] = value.astype(BF16).reshape(F, COLS, channels)

    def copy_out(number):
        rows = pl.ds(number * block, block)
        return pltpu.make_async_copy(
            late.at[rows], out_ref.at[rows, pl.ds(2, 2)], out_sems.at[number]
        )

    def convolve(number, first, act):
        begin = number * block
        source_rows = [[], [], []]
        for row in range(block):
            is_first, is_last = clip_edges(begin + row + 1)
            source_rows[0].append(jnp.where(is_first, act_zero, row))
            source_rows[1].append(row + 1)
            source_rows[2].append(jnp.where(is_last, act_zero, row + 2))

        def finish(frames, weight_from, frame_from, count):
            pieces = []
            for frame in frames:
                for row_tap in range(3):
                    parts = [
                        act[at, frame : frame + count].reshape(count * COLS, channels)
                        for at in source_rows[row_tap]
                    ]
                    pieces.append(jnp.concatenate(parts, axis=0))
            slab = jnp.concatenate(pieces, axis=1)
            sums = jnp.dot(slab, weights[weight_from:, :], preferred_element_type=F32)
            total = shift_columns(sums, channels)
            parts = []
            for row in range(block):
                at = (row + 1) * size + frame_from * COLS
                parts.append(first[at : at + count * COLS, :])
            return total + jnp.concatenate(parts, axis=0)

        taps = 3 * channels
        rows = pl.ds(begin, block)
        value = finish([0, 1, 2], 0, 2, 2)
        at_row = lax.broadcasted_iota(jnp.int32, value.shape, 0) // (2 * COLS)
        value = jnp.where(at_row < live - begin, value, 0.0)
        late[rows] = value.astype(BF16).reshape(block, 2, COLS, channels)
        part_ref[rows, 1] = finish([0, 1], taps, 1, 1).reshape(block, COLS, channels)
        part_ref[rows, 0] = finish([0], 2 * taps, 0, 1).reshape(block, COLS, channels)

    def step(number, windows, first, act, next_windows, next_first, next_act):
        sums = convolve_first((number + 1) * block + 2, block, windows)
        for row in range(2):
            next_act[row] = act[block + row]
        next_first[: 2 * size, :] = first[block * size :, :]
        activate(sums, block, 2, next_first, next_act)
        convolve(number, first, act)
        fill_block((number + 2) * block + 2, block, next_windows)
        copy_out(number).start()

    fill_block(0, block + 2, windows_b)
    activate(convolve_first(0, block + 2, windows_b), block + 2, 0, first_a, act_a)
    fill_block(block + 2, block, windows_a)
    load.wait()
    used = lax.div(live + block - 1, block)

    def two_steps(pair, carry):
        step(2 * pair, windows_a, first_a, act_a, windows_b, first_b, act_b)

        @pl.when(2 * pair + 1 < used)
        def _():
            step(2 * pair + 1, windows_b, first_b, act_b, windows_a, first_a, act_a)

        return carry

    lax.fori_loop(0, lax.div(used + 1, 2), two_steps, 0)

    def clear(number, carry):
        late[pl.ds(number * block, block)] = jnp.zeros((block, 2, COLS, channels), BF16)
        copy_out(number).start()
        return carry

    lax.fori_loop(used, blocks, clear, 0)
    for number in range(blocks):
        copy_out(number).wait()


def cached_frames(
    bands, part_ref, weights, late_ref, *refs,
    owners, units, capacity, height, block, band_max, channels,
):
    del late_ref
    parts, (out_ref, cache, early, out_sems, cache_sems) = refs[:owners], refs[owners:]
    group = lax.axis_index("seq")
    owner = lax.axis_index("dec")
    live = bands[group, owner]
    start = band_start(bands, group, owner, owners)
    depth = channels // LANES
    blocks = band_max // block
    edge = lax.rem(height - lax.rem(start - 1 + height, height), height)

    def slot_of(at):
        row = jnp.clip(start - 1 + at, 0, units * owners - 1)
        source = lax.rem(row, owners)
        unit = first_unit(start, 1, source, owners, units, capacity)
        return source * capacity + jnp.clip(lax.div(row, owners) - unit, 0, capacity - 1)

    def copy_out(number):
        rows = pl.ds(number * block, block)
        return pltpu.make_async_copy(
            early.at[rows], out_ref.at[rows, pl.ds(0, 2)], out_sems.at[number]
        )

    copies = []
    for other, part in enumerate(parts):
        into = cache.at[pl.ds((owner ^ other) * capacity, capacity)]
        arrived = part.at[pl.ds(0, capacity)]
        copies.append(pltpu.make_async_copy(arrived, into, cache_sems.at[other]))
    for copy in copies:
        copy.start()
    slots = owners * capacity
    cache[slots] = jnp.zeros(cache.shape[1:], BF16)
    for copy in copies:
        copy.wait()
    used = lax.div(live + block - 1, block)

    def convolve(number, carry):
        begin = number * block
        source_rows = [[], [], []]
        for row in range(block):
            at = begin + row + 1
            is_first = (at == edge) | (at == edge + height)
            is_last = (at == edge - 1) | (at == edge - 1 + height)
            source_rows[0].append(jnp.where(is_first, slots, slot_of(at - 1)))
            source_rows[1].append(slot_of(at))
            source_rows[2].append(jnp.where(is_last, slots, slot_of(at + 1)))

        def slab(frames):
            pieces = []
            for frame in frames:
                for row_tap in range(3):
                    for part in range(depth):
                        tile = pl.ds((frame * depth + part) * COLS, COLS)
                        values = [cache[at, tile, :] for at in source_rows[row_tap]]
                        pieces.append(jnp.concatenate(values, axis=0))
            return jnp.concatenate(pieces, axis=1)

        at_row = lax.broadcasted_iota(jnp.int32, (block * COLS, channels), 0) // COLS
        taps = 3 * channels
        rows = pl.ds(begin, block)
        for frame, frames in ((0, (0, 1)), (1, (1,))):
            sums = jnp.dot(
                slab(frames), weights[: len(frames) * taps, :], preferred_element_type=F32
            )
            total = shift_columns(sums, channels) + part_ref[rows, frame].reshape(
                block * COLS, channels
            )
            total = jnp.where(at_row < live - begin, total, 0.0)
            early[rows, frame] = total.astype(BF16).reshape(block, COLS, channels)
        copy_out(number).start()
        return carry

    lax.fori_loop(0, used, convolve, 0)

    def clear(number, carry):
        early[pl.ds(number * block, block)] = jnp.zeros((block, 2, COLS, channels), BF16)
        copy_out(number).start()
        return carry

    lax.fori_loop(used, blocks, clear, 0)
    for number in range(blocks):
        copy_out(number).wait()


def params(mebibytes, **extra):
    return pltpu.CompilerParams(vmem_limit_bytes=mebibytes * 1024 * 1024, **extra)


def shards(latents, cache_lat, cache_act, w_in, w_mid, norm_gain, clip_group, band_rows):
    groups = lax.axis_size("seq")
    owners = lax.axis_size("dec")
    clips = latents.shape[1]
    per_owner = latents.shape[2]
    channels = w_mid.shape[2]
    units = groups * per_owner
    height = per_owner * owners
    stack_rows = groups * height
    band_max = 2 * stack_rows // owners
    act_capacity = (band_max + 2 + owners - 1) // owners
    block = next(size for size in (16, 8) if band_max % size == 0)
    any_space = pl.BlockSpec(memory_space=pl.ANY)
    in_vmem = pl.BlockSpec(memory_space=pltpu.VMEM)
    in_hbm = pl.BlockSpec(memory_space=pltpu.HBM)

    def rows_first(array):
        return jnp.transpose(array[0, :, :, 0, :], (1, 0, 2))

    lat, old, act = rows_first(latents), rows_first(cache_lat), rows_first(cache_act)
    tiles = act.shape[2] // LANES
    lat_rows = (per_owner * 12 + 15) // 16 * 16
    per_step = 3
    packed = pl.pallas_call(
        functools.partial(
            pack_clips, per_owner=per_owner, per_step=per_step, clips=clips
        ),
        grid_spec=pltpu.PrefetchScalarGridSpec(
            num_scalar_prefetch=1,
            grid=(),
            in_specs=[in_hbm, in_hbm, in_hbm],
            out_specs=[in_vmem] * clips,
            scratch_shapes=[
                pltpu.VMEM(lat.shape, BF16),
                pltpu.VMEM(old.shape, BF16),
                pltpu.VMEM(act.shape, BF16),
                pltpu.VMEM((clips * lat_rows, LANES), F32),
                pltpu.VMEM((2, clips * per_step * tiles, LANES), F32),
                pltpu.SemaphoreType.DMA((2 + per_owner // per_step,)),
            ],
        ),
        out_shape=[jax.ShapeDtypeStruct((per_owner * tiles + lat_rows, LANES), BF16)] * clips,
        compiler_params=params(56),
        name="pack_clips",
    )(clip_group, lat, old, act)

    def trade(parts, axis):
        count = lax.axis_size(axis)
        return [parts[0]] + [
            lax.ppermute(part, axis, [(i, i ^ other) for i in range(count)])
            for other, part in enumerate(parts)
            if other
        ]

    traded = trade(packed, "seq")
    wide_mid, table = pl.pallas_call(
        widen_weights,
        in_specs=[in_hbm, in_vmem],
        out_specs=[in_hbm, in_vmem],
        scratch_shapes=[
            pltpu.VMEM((9 * channels, 3 * channels), BF16),
            pltpu.SemaphoreType.DMA((27,)),
            pltpu.SemaphoreType.DMA((9,)),
        ],
        out_shape=[
            jax.ShapeDtypeStruct((9 * channels, 3 * channels), BF16),
            jax.ShapeDtypeStruct((6 * LANES, channels), BF16),
        ],
        compiler_params=params(50),
        cost_estimate=pl.CostEstimate(
            flops=0, bytes_accessed=4 * 27 * channels * channels, transcendentals=0
        ),
        name="widen_weights",
    )(w_mid, w_in)
    lat_capacity = (band_max + 4 + owners - 1) // owners
    slice_rows = (lat_capacity * 12 + 15) // 16 * 16
    slice_act = jax.ShapeDtypeStruct((act_capacity * tiles, LANES), BF16)
    slice_two = jax.ShapeDtypeStruct((2 * act_capacity * tiles, LANES), BF16)
    sliced = pl.pallas_call(
        functools.partial(
            slice_bands, owners=owners, units=units, lat_capacity=lat_capacity,
            act_capacity=act_capacity, per_owner=per_owner, tiles=tiles, groups=groups,
        ),
        grid_spec=pltpu.PrefetchScalarGridSpec(
            num_scalar_prefetch=1,
            grid=(),
            in_specs=[any_space] + [in_vmem] * clips,
            out_specs=[in_vmem] * owners,
            scratch_shapes=[
                pltpu.VMEM((units * 12 + slice_rows, LANES), F32),
                pltpu.VMEM((units * tiles, LANES), BF16),
                pltpu.SemaphoreType.DMA((clips,)),
                pltpu.SemaphoreType.DMA((owners,)),
            ],
        ),
        out_shape=[
            jax.ShapeDtypeStruct((owners, slice_rows, LANES), BF16), slice_act, slice_act, slice_two
        ]
        + [slice_act] * (owners - 4),
        compiler_params=params(16),
        name="slice_bands",
    )(band_rows, table, *traded)
    band_lat, own, beside, two, *far = sliced
    band_lat = lax.all_to_all(band_lat, "dec", split_axis=0, concat_axis=0, tiled=True)

    def send(part, other):
        return lax.ppermute(part, "dec", [(i, i ^ other) for i in range(owners)])

    far = [send(part, other) for other, part in enumerate(far, 4)]
    two = send(two, 2)

    late, part, weights = pl.pallas_call(
        functools.partial(
            new_frames, owners=owners, units=units, capacity=lat_capacity, height=height,
            block=block, band_max=band_max, channels=channels,
        ),
        grid_spec=pltpu.PrefetchScalarGridSpec(
            num_scalar_prefetch=1,
            grid=(),
            in_specs=[in_vmem, in_vmem, in_vmem, in_hbm],
            out_specs=[in_hbm, in_vmem, in_vmem],
            scratch_shapes=[
                pltpu.VMEM((owners * slice_rows, LANES), F32),
                pltpu.VMEM((block + 5, F * COLS, 2 * LANES), BF16),
                pltpu.VMEM((block + 5, F * COLS, 2 * LANES), BF16),
                pltpu.VMEM(((block + 2) * F * COLS, channels), F32),
                pltpu.VMEM(((block + 2) * F * COLS, channels), F32),
                pltpu.VMEM((block + 3, F, COLS, channels), BF16),
                pltpu.VMEM((block + 3, F, COLS, channels), BF16),
                pltpu.VMEM((band_max, 2, COLS, channels), BF16),
                pltpu.SemaphoreType.DMA((band_max // block,)),
                pltpu.SemaphoreType.DMA,
            ],
        ),
        out_shape=[
            jax.ShapeDtypeStruct((band_max, F, COLS, channels), BF16),
            jax.ShapeDtypeStruct((band_max, 2, COLS, channels), F32),
            jax.ShapeDtypeStruct((9 * channels, 3 * channels), BF16),
        ],
        compiler_params=params(36),
        cost_estimate=pl.CostEstimate(
            flops=2 * band_max * 9 * COLS * 9 * channels * channels,
            bytes_accessed=16 * 1024 * 1024,
            transcendentals=0,
        ),
        name="new_frames",
    )(band_rows, norm_gain.reshape(1, channels), table, band_lat, wide_mid)

    slots = owners * act_capacity
    two, beside, part = lax.optimization_barrier((two, beside, part))
    handed = send(two[act_capacity * tiles :], 1)
    beside = send(beside, 1)
    band_act = [rows.reshape(-1, tiles, LANES) for rows in (own, beside, two, handed, *far)]
    decoded = pl.pallas_call(
        functools.partial(
            cached_frames, owners=owners, units=units, capacity=act_capacity, height=height,
            block=block, band_max=band_max, channels=channels,
        ),
        grid_spec=pltpu.PrefetchScalarGridSpec(
            num_scalar_prefetch=1,
            grid=(),
            in_specs=[in_vmem, in_vmem, in_hbm] + [any_space] * owners,
            out_specs=in_hbm,
            scratch_shapes=[
                pltpu.VMEM((slots + 1, tiles, LANES), BF16),
                pltpu.VMEM((band_max, 2, COLS, channels), BF16),
                pltpu.SemaphoreType.DMA((band_max // block,)),
                pltpu.SemaphoreType.DMA((owners,)),
            ],
        ),
        out_shape=jax.ShapeDtypeStruct((band_max, F, COLS, channels), BF16),
        input_output_aliases={3: 0},
        compiler_params=params(24),
        cost_estimate=pl.CostEstimate(
            flops=2 * band_max * 3 * COLS * 9 * channels * channels,
            bytes_accessed=16 * 1024 * 1024,
            transcendentals=0,
        ),
        name="cached_frames",
    )(band_rows, part, weights, late, *band_act)
    return decoded.reshape((1, 1) + decoded.shape)


def solution(mesh):
    placed = (
        P("seq", None, None, "dec", None),
        P("seq", None, None, "dec", None),
        P("seq", None, None, "dec", None),
        P(),
        P(),
        P(),
        P(),
        P(),
    )
    return jax.shard_map(
        shards,
        mesh=mesh,
        in_specs=placed,
        out_specs=P("seq", "dec", None, None, None, None),
        check_vma=False,
    )
```

```python
import functools

import jax
import jax.numpy as jnp
from jax import lax
from jax.experimental import pallas as pl
from jax.experimental.pallas import tpu as pltpu
from jax.sharding import PartitionSpec as P

F = 4
CT = 2
COLS = 16
LANES = 128
EPSILON = 1e-06
F32 = jnp.float32
BF16 = jnp.bfloat16


def band_start(bands, group, owner, owners):
    total = jnp.int32(0)
    for other in range(owners):
        total = total + jnp.where(other < owner, bands[group, other], 0)
    return total


def first_unit(start, margin, source, owners, units, capacity):
    unit = (start - margin - source + owners - 1 + 2 * owners) // owners - 2
    return jnp.clip(unit, 0, units - capacity)


def clip_of(groups_ref, shard, group, clips):
    found = jnp.int32(0)
    for clip in range(clips):
        found = found + jnp.where(groups_ref[shard, clip] == group, clip, 0)
    return found


def pack_clips(groups_ref, lat_in, old_in, act_in, *refs, per_owner, per_step, clips):
    *outs, lat_ref, old_ref, act_ref, lat_scratch, act_scratch, sems = refs
    shard = lax.axis_index("seq")
    copies = [
        pltpu.make_async_copy(lat_in, lat_ref, sems.at[0]),
        pltpu.make_async_copy(old_in, old_ref, sems.at[1]),
    ]
    steps = per_owner // per_step
    for step in range(steps):
        rows = pl.ds(step * per_step, per_step)
        copies.append(
            pltpu.make_async_copy(act_in.at[rows], act_ref.at[rows], sems.at[2 + step])
        )
    for copy in copies:
        copy.start()
    chosen = [clip_of(groups_ref, shard, shard ^ other, clips) for other in range(clips)]
    tiles = act_ref.shape[2] // LANES
    depth = tiles // (CT * COLS)
    size = per_step * tiles
    lat_rows = outs[0].shape[0] - per_owner * tiles
    copies[0].wait()
    copies[1].wait()
    for row in range(per_owner):
        for frame in range(CT + F):
            for half in range(2):
                if frame < CT:
                    tile = frame * 2 + half
                    value = old_ref[row, :, tile * LANES : (tile + 1) * LANES]
                else:
                    tile = (frame - CT) * 2 + half
                    value = lat_ref[row, :, tile * LANES : (tile + 1) * LANES]
                at = row * 12 + half * (CT + F) + frame
                lat_scratch[pl.ds(at, clips, stride=lat_rows), :] = value.astype(F32)
    for out, clip in zip(outs, chosen):
        rows = pl.ds(pl.multiple_of(clip * lat_rows, 8), lat_rows)
        out[per_owner * tiles :, :] = lat_scratch[rows, :].astype(BF16)
    for step in range(steps):
        copies[2 + step].wait()
        for row in range(per_step):
            for frame in range(CT):
                for col in range(COLS):
                    for part in range(depth):
                        tile = (frame * COLS + col) * depth + part
                        at = row * tiles + (frame * depth + part) * COLS + col
                        value = act_ref[
                            step * per_step + row, :, tile * LANES : (tile + 1) * LANES
                        ]
                        act_scratch[step % 2, pl.ds(at, clips, stride=size), :] = value.astype(F32)
        for out, clip in zip(outs, chosen):
            rows = pl.ds(pl.multiple_of(clip * size, 8), size)
            out[step * size : (step + 1) * size, :] = act_scratch[step % 2, rows, :].astype(BF16)


def slice_bands(
    bands, _, *refs, owners, units, lat_capacity, act_capacity, per_owner, tiles, groups
):
    ins, lat_outs, act_outs = refs[:groups], refs[groups : groups + owners], refs[groups + owners : -4]
    lat_scratch, scratch, in_sems, sems = refs[-4:]
    group = lax.axis_index("seq")
    source = lax.axis_index("dec")
    size = per_owner * tiles
    copies = []
    for other, in_ref in enumerate(ins):
        into = scratch.at[pl.ds(pl.multiple_of((group ^ other) * size, 16), size)]
        copies.append(pltpu.make_async_copy(in_ref.at[pl.ds(0, size)], into, in_sems.at[other]))
    for copy in copies:
        copy.start()
    rows = lat_outs[0].shape[0]
    lat_size = per_owner * 12
    for other, in_ref in enumerate(ins):
        value = in_ref[size : size + lat_size, :].astype(F32)
        lat_scratch[pl.ds((group ^ other) * lat_size, lat_size), :] = value
    value = pltpu.roll(lat_scratch[: units * 12, :], 64, 1)
    lane = lax.broadcasted_iota(jnp.int32, value.shape, 1)
    for width in (32, 16):
        up, down = pltpu.roll(value, width, 1), pltpu.roll(value, LANES - width, 1)
        value = jnp.where(lane & width == 0, down, up)
    lat_scratch[: units * 12, :] = value
    starts = [band_start(bands, group, source ^ other, owners) for other in range(owners)]
    for copy in copies:
        copy.wait()
    copies = []
    into = [(act_outs[0], 0), (lat_outs[1], 0), (act_outs[1], 0), (act_outs[1], 1)]
    into += [(out, 0) for out in act_outs[2:]]
    length = act_capacity * tiles
    for other, (out_ref, place) in enumerate(into):
        unit = first_unit(starts[other], 1, source, owners, units, act_capacity)
        rows_in = pl.ds(pl.multiple_of(unit * tiles, 16), length)
        rows_out = pl.ds(place * length, length)
        copies.append(
            pltpu.make_async_copy(scratch.at[rows_in], out_ref.at[rows_out], sems.at[other])
        )
    for copy in copies:
        copy.start()
    for other, out_ref in enumerate(lat_outs):
        unit = first_unit(starts[other], 2, source, owners, units, lat_capacity)
        value = lat_scratch[pl.ds(unit * 12, rows), :].astype(BF16)
        out_ref[pl.ds(length if other == 1 else 0, rows), :] = value
    for copy in copies:
        copy.wait()


def shift_columns(sums, width):
    rows = sums.shape[0]
    col = lax.rem(lax.broadcasted_iota(jnp.int32, (rows, width), 0), COLS)
    left = pltpu.roll(sums[:, :width], 1, 0)
    right = pltpu.roll(sums[:, 2 * width :], rows - 1, 0)
    total = sums[:, width : 2 * width] + jnp.where(col > 0, left, 0.0)
    return total + jnp.where(col < COLS - 1, right, 0.0)


def widen_weights(mid_ref, win_ref, out_ref, table, sems):
    channels = mid_ref.shape[1]
    copies = []
    for tap in range(27):
        into = out_ref.at[
            pl.ds(tap // 3 * channels, channels), pl.ds(tap % 3 * channels, channels)
        ]
        copies.append(pltpu.make_async_copy(mid_ref.at[tap], into, sems.at[tap]))
    for copy in copies:
        copy.start()
    table[...] = jnp.zeros(table.shape, BF16)
    for time_tap in range(3):
        for row_tap in range(3):
            for col_tap in range(3):
                into = row_tap * 2 * LANES + (0, 64, LANES)[time_tap]
                into += ((0, 112, 96), (0, -16, -32), (0, 112, 96))[time_tap][col_tap]
                table[pl.ds(into, 16), :] = win_ref[time_tap * 9 + row_tap * 3 + col_tap]
    for copy in copies:
        copy.wait()


def new_frames(
    bands, table, gain_ref, weights, *refs,
    owners, units, capacity, height, block, band_max, channels, cache_rows,
):
    group = lax.axis_index("seq")
    owner = lax.axis_index("dec")
    lat_refs, refs = refs[:owners], refs[owners:]
    out_ref, part_ref, xs, windows_a, windows_b, first_a, first_b = refs[:7]
    act_a, act_b, late, out_sems = refs[7:]
    live = bands[group, owner]
    start = band_start(bands, group, owner, owners)
    edge = lax.rem(height - lax.rem(start - 1 + height, height), height)
    blocks = band_max // block
    size = F * COLS
    per_source = lat_refs[0].shape[0]
    for other, lat_ref in enumerate(lat_refs):
        from_row = lat_ref.shape[0] - per_source if other != 1 else cache_rows
        value = lat_ref[pl.ds(from_row, per_source), :].astype(F32)
        rows = pl.ds(pl.multiple_of((owner ^ other) * per_source, 8), per_source)
        xs[0, rows, :] = value
        xs[1, rows, :] = pltpu.roll(value, 64, 1)
    window_zero, act_zero = block + 4, block + 2
    for windows in (windows_a, windows_b):
        windows[window_zero] = jnp.zeros(windows.shape[1:], BF16)
    for act in (act_a, act_b):
        act[act_zero] = jnp.zeros((F, COLS, channels), BF16)
    half_gain = 0.5 * gain_ref[...]

    def clip_edges(at):
        is_first = (at == edge) | (at == edge + height)
        is_last = (at == edge - 1) | (at == edge - 1 + height)
        return is_first, is_last

    def fill(row, windows, into):
        lane = lax.broadcasted_iota(jnp.int32, (8, LANES), 1)
        col = lax.broadcasted_iota(jnp.int32, (8, LANES), 0)
        low = (lane < 16) | (lane >= 96)
        left_end = (col == 0) & ((lane & 63) < 16)
        right_end = (col == 7) & ((lane & 63) >= 32) & ((lane & 63) < 48)
        stack_row = jnp.clip(start - 2 + row, 0, units * owners - 1)
        source = lax.rem(stack_row, owners)
        unit = first_unit(start, 2, source, owners, units, capacity)
        slot = jnp.clip(lax.div(stack_row, owners) - unit, 0, capacity - 1)
        base = source * per_source + slot * 12
        rolled = [{}, {}]
        for frame in range(CT + F):
            for half in range(2):
                at_row = pl.ds(base + half * (CT + F) + frame, 1)
                for turn in range(2):
                    if turn == 1 and not 1 <= frame <= F:
                        continue
                    value = jnp.broadcast_to(xs[turn, at_row, :], (8, LANES))
                    rolled[turn][half, frame] = pltpu.roll(value, 0, 1, stride=16, stride_axis=0)
        for frame in range(F):
            pair = [
                jnp.where(low, rolled[0][half, frame], rolled[1][half, frame + 1])
                for half in range(2)
            ]
            last = [rolled[0][half, frame + 2] for half in range(2)]
            for lanes, (left, right) in enumerate((pair, last)):
                near = jnp.where(left_end, 0.0, jnp.where(right_end, right, left))
                far = jnp.where(right_end, 0.0, jnp.where(left_end, left, right))
                windows[
                    into,
                    frame * COLS : (frame + 1) * COLS,
                    lanes * LANES : (lanes + 1) * LANES,
                ] = jnp.concatenate([near, far], axis=0).astype(BF16)

    def fill_block(row, count, windows):
        for at in range(count + 2):
            fill(row + at, windows, at)

    def convolve_first(row, count, windows):
        pieces = [[], [], []]
        for at in range(count):
            is_first, is_last = clip_edges(row + at)
            pieces[0].append(windows[jnp.where(is_first, window_zero, at)])
            pieces[1].append(windows[at + 1])
            pieces[2].append(windows[jnp.where(is_last, window_zero, at + 2)])
        slab = jnp.concatenate([jnp.concatenate(part, axis=0) for part in pieces], axis=1)
        return jnp.dot(slab, table[...], preferred_element_type=F32)

    def activate(sums, count, into, first, act):
        first[into * size : (into + count) * size, :] = sums
        for at in range(count):
            value = sums[at * size : (at + 1) * size]
            mean_square = jnp.mean(value * value, axis=-1, keepdims=True)
            half = value * lax.rsqrt(mean_square + EPSILON) * half_gain
            value = half + half * jnp.tanh(half)
            act[into + at] = value.astype(BF16).reshape(F, COLS, channels)

    def copy_out(number):
        rows = pl.ds(number * block, block)
        return pltpu.make_async_copy(
            late.at[rows], out_ref.at[rows, pl.ds(2, 2)], out_sems.at[number]
        )

    def convolve(number, first, act):
        begin = number * block
        source_rows = [[], [], []]
        for row in range(block):
            is_first, is_last = clip_edges(begin + row + 1)
            source_rows[0].append(jnp.where(is_first, act_zero, row))
            source_rows[1].append(row + 1)
            source_rows[2].append(jnp.where(is_last, act_zero, row + 2))

        def finish(frames, weight_from, frame_from, count):
            pieces = []
            for frame in frames:
                for row_tap in range(3):
                    parts = [
                        act[at, frame : frame + count].reshape(count * COLS, channels)
                        for at in source_rows[row_tap]
                    ]
                    pieces.append(jnp.concatenate(parts, axis=0))
            slab = jnp.concatenate(pieces, axis=1)
            sums = jnp.dot(slab, weights[weight_from:, :], preferred_element_type=F32)
            total = shift_columns(sums, channels)
            parts = []
            for row in range(block):
                at = (row + 1) * size + frame_from * COLS
                parts.append(first[at : at + count * COLS, :])
            return total + jnp.concatenate(parts, axis=0)

        taps = 3 * channels
        rows = pl.ds(begin, block)
        value = finish([0, 1, 2], 0, 2, 2)
        at_row = lax.broadcasted_iota(jnp.int32, value.shape, 0) // (2 * COLS)
        value = jnp.where(at_row < live - begin, value, 0.0)
        late[rows] = value.astype(BF16).reshape(block, 2, COLS, channels)
        part_ref[rows, 1] = finish([0, 1], taps, 1, 1).reshape(block, COLS, channels)
        part_ref[rows, 0] = finish([0], 2 * taps, 0, 1).reshape(block, COLS, channels)

    used = lax.div(live + block - 1, block)

    def step(number, windows, first, act, next_windows, next_first, next_act):
        convolve(number, first, act)
        copy_out(number).start()

        @pl.when(number + 1 < used)
        def _():
            sums = convolve_first((number + 1) * block + 2, block, windows)
            for row in range(2):
                next_act[row] = act[block + row]
            next_first[: 2 * size, :] = first[block * size :, :]
            activate(sums, block, 2, next_first, next_act)
            fill_block((number + 2) * block + 2, block, next_windows)

    fill_block(0, block + 2, windows_b)
    activate(convolve_first(0, block + 2, windows_b), block + 2, 0, first_a, act_a)
    fill_block(block + 2, block, windows_a)

    def two_steps(pair, carry):
        step(2 * pair, windows_a, first_a, act_a, windows_b, first_b, act_b)

        @pl.when(2 * pair + 1 < used)
        def _():
            step(2 * pair + 1, windows_b, first_b, act_b, windows_a, first_a, act_a)

        return carry

    lax.fori_loop(0, lax.div(used + 1, 2), two_steps, 0)

    def clear(number, carry):
        late[pl.ds(number * block, block)] = jnp.zeros((block, 2, COLS, channels), BF16)
        copy_out(number).start()
        return carry

    lax.fori_loop(used, blocks, clear, 0)
    for number in range(blocks):
        copy_out(number).wait()


def cached_frames(
    bands, part_ref, weights, late_ref, *refs,
    owners, units, capacity, height, block, band_max, channels,
):
    del late_ref
    parts, (out_ref, cache, early, out_sems, cache_sems) = refs[:owners], refs[owners:]
    group = lax.axis_index("seq")
    owner = lax.axis_index("dec")
    live = bands[group, owner]
    start = band_start(bands, group, owner, owners)
    depth = channels // LANES
    blocks = band_max // block
    edge = lax.rem(height - lax.rem(start - 1 + height, height), height)

    def slot_of(at):
        row = jnp.clip(start - 1 + at, 0, units * owners - 1)
        source = lax.rem(row, owners)
        unit = first_unit(start, 1, source, owners, units, capacity)
        return source * capacity + jnp.clip(lax.div(row, owners) - unit, 0, capacity - 1)

    def copy_out(number):
        rows = pl.ds(number * block, block)
        return pltpu.make_async_copy(
            early.at[rows], out_ref.at[rows, pl.ds(0, 2)], out_sems.at[number]
        )

    copies = []
    for other, part in enumerate(parts):
        into = cache.at[pl.ds((owner ^ other) * capacity, capacity)]
        arrived = part.at[pl.ds(0, capacity)]
        copies.append(pltpu.make_async_copy(arrived, into, cache_sems.at[other]))
    for copy in copies:
        copy.start()
    slots = owners * capacity
    cache[slots] = jnp.zeros(cache.shape[1:], BF16)
    for copy in copies:
        copy.wait()
    used = lax.div(live + block - 1, block)

    def convolve(number, carry):
        begin = number * block
        source_rows = [[], [], []]
        for row in range(block):
            at = begin + row + 1
            is_first = (at == edge) | (at == edge + height)
            is_last = (at == edge - 1) | (at == edge - 1 + height)
            source_rows[0].append(jnp.where(is_first, slots, slot_of(at - 1)))
            source_rows[1].append(slot_of(at))
            source_rows[2].append(jnp.where(is_last, slots, slot_of(at + 1)))

        def slab(frames):
            pieces = []
            for frame in frames:
                for row_tap in range(3):
                    for part in range(depth):
                        tile = pl.ds((frame * depth + part) * COLS, COLS)
                        values = [cache[at, tile, :] for at in source_rows[row_tap]]
                        pieces.append(jnp.concatenate(values, axis=0))
            return jnp.concatenate(pieces, axis=1)

        at_row = lax.broadcasted_iota(jnp.int32, (block * COLS, channels), 0) // COLS
        taps = 3 * channels
        rows = pl.ds(begin, block)
        for frame, frames in ((0, (0, 1)), (1, (1,))):
            sums = jnp.dot(
                slab(frames), weights[: len(frames) * taps, :], preferred_element_type=F32
            )
            total = shift_columns(sums, channels) + part_ref[rows, frame].reshape(
                block * COLS, channels
            )
            total = jnp.where(at_row < live - begin, total, 0.0)
            early[rows, frame] = total.astype(BF16).reshape(block, COLS, channels)
        copy_out(number).start()
        return carry

    lax.fori_loop(0, used, convolve, 0)

    def clear(number, carry):
        early[pl.ds(number * block, block)] = jnp.zeros((block, 2, COLS, channels), BF16)
        copy_out(number).start()
        return carry

    lax.fori_loop(used, blocks, clear, 0)
    for number in range(blocks):
        copy_out(number).wait()


def params(mebibytes, **extra):
    return pltpu.CompilerParams(vmem_limit_bytes=mebibytes * 1024 * 1024, **extra)


def shards(latents, cache_lat, cache_act, w_in, w_mid, norm_gain, clip_group, band_rows):
    groups = lax.axis_size("seq")
    owners = lax.axis_size("dec")
    clips = latents.shape[1]
    per_owner = latents.shape[2]
    channels = w_mid.shape[2]
    units = groups * per_owner
    height = per_owner * owners
    stack_rows = groups * height
    band_max = 2 * stack_rows // owners
    act_capacity = (band_max + 2 + owners - 1) // owners
    block = next(size for size in (16, 8) if band_max % size == 0)
    any_space = pl.BlockSpec(memory_space=pl.ANY)
    in_vmem = pl.BlockSpec(memory_space=pltpu.VMEM)
    in_hbm = pl.BlockSpec(memory_space=pltpu.HBM)

    def rows_first(array):
        return jnp.transpose(array[0, :, :, 0, :], (1, 0, 2))

    lat, old, act = rows_first(latents), rows_first(cache_lat), rows_first(cache_act)
    tiles = act.shape[2] // LANES
    lat_rows = (per_owner * 12 + 15) // 16 * 16
    per_step = 3
    packed = pl.pallas_call(
        functools.partial(
            pack_clips, per_owner=per_owner, per_step=per_step, clips=clips
        ),
        grid_spec=pltpu.PrefetchScalarGridSpec(
            num_scalar_prefetch=1,
            grid=(),
            in_specs=[in_hbm, in_hbm, in_hbm],
            out_specs=[in_vmem] * clips,
            scratch_shapes=[
                pltpu.VMEM(lat.shape, BF16),
                pltpu.VMEM(old.shape, BF16),
                pltpu.VMEM(act.shape, BF16),
                pltpu.VMEM((clips * lat_rows, LANES), F32),
                pltpu.VMEM((2, clips * per_step * tiles, LANES), F32),
                pltpu.SemaphoreType.DMA((2 + per_owner // per_step,)),
            ],
        ),
        out_shape=[jax.ShapeDtypeStruct((per_owner * tiles + lat_rows, LANES), BF16)] * clips,
        compiler_params=params(56),
        name="pack_clips",
    )(clip_group, lat, old, act)

    def trade(parts, axis):
        count = lax.axis_size(axis)
        return [parts[0]] + [
            lax.ppermute(part, axis, [(i, i ^ other) for i in range(count)])
            for other, part in enumerate(parts)
            if other
        ]

    traded = trade(packed, "seq")
    wide_mid, table = pl.pallas_call(
        widen_weights,
        in_specs=[in_hbm, in_vmem],
        out_specs=[in_vmem, in_vmem],
        scratch_shapes=[pltpu.SemaphoreType.DMA((27,))],
        out_shape=[
            jax.ShapeDtypeStruct((9 * channels, 3 * channels), BF16),
            jax.ShapeDtypeStruct((6 * LANES, channels), BF16),
        ],
        compiler_params=params(16),
        cost_estimate=pl.CostEstimate(
            flops=0, bytes_accessed=4 * 27 * channels * channels, transcendentals=0
        ),
        name="widen_weights",
    )(w_mid, w_in)
    lat_capacity = (band_max + 4 + owners - 1) // owners
    slice_rows = (lat_capacity * 12 + 15) // 16 * 16
    slice_both = (act_capacity * tiles + slice_rows + tiles - 1) // tiles * tiles
    slice_act = jax.ShapeDtypeStruct((act_capacity * tiles, LANES), BF16)
    slice_two = jax.ShapeDtypeStruct((2 * act_capacity * tiles, LANES), BF16)
    sliced = pl.pallas_call(
        functools.partial(
            slice_bands, owners=owners, units=units, lat_capacity=lat_capacity,
            act_capacity=act_capacity, per_owner=per_owner, tiles=tiles, groups=groups,
        ),
        grid_spec=pltpu.PrefetchScalarGridSpec(
            num_scalar_prefetch=1,
            grid=(),
            in_specs=[in_vmem] * (1 + clips),
            out_specs=[in_vmem] * (2 * owners - 2),
            scratch_shapes=[
                pltpu.VMEM((units * 12 + slice_rows, LANES), F32),
                pltpu.VMEM((units * tiles, LANES), BF16),
                pltpu.SemaphoreType.DMA((clips,)),
                pltpu.SemaphoreType.DMA((owners,)),
            ],
        ),
        out_shape=[
            jax.ShapeDtypeStruct((slice_both if other == 1 else slice_rows, LANES), BF16)
            for other in range(owners)
        ]
        + [slice_act, slice_two]
        + [slice_act] * (owners - 4),
        compiler_params=params(16),
        name="slice_bands",
    )(band_rows, table, *traded)
    band_lat, band_act = lax.optimization_barrier(
        (trade(sliced[:owners], "dec"), sliced[owners:])
    )

    def send(part, other):
        return lax.ppermute(part, "dec", [(i, i ^ other) for i in range(owners)])

    own, *band_act = band_act
    far = [send(part, other) for other, part in enumerate(band_act[1:], 4)]
    two = send(band_act[0], 2)

    late, part = pl.pallas_call(
        functools.partial(
            new_frames, owners=owners, units=units, capacity=lat_capacity, height=height,
            block=block, band_max=band_max, channels=channels, cache_rows=act_capacity * tiles,
        ),
        grid_spec=pltpu.PrefetchScalarGridSpec(
            num_scalar_prefetch=1,
            grid=(),
            in_specs=[in_vmem] * (3 + owners),
            out_specs=[in_hbm, in_vmem],
            scratch_shapes=[
                pltpu.VMEM((2, owners * slice_rows, LANES), F32),
                pltpu.VMEM((block + 5, F * COLS, 2 * LANES), BF16),
                pltpu.VMEM((block + 5, F * COLS, 2 * LANES), BF16),
                pltpu.VMEM(((block + 2) * F * COLS, channels), F32),
                pltpu.VMEM(((block + 2) * F * COLS, channels), F32),
                pltpu.VMEM((block + 3, F, COLS, channels), BF16),
                pltpu.VMEM((block + 3, F, COLS, channels), BF16),
                pltpu.VMEM((band_max, 2, COLS, channels), BF16),
                pltpu.SemaphoreType.DMA((band_max // block,)),
            ],
        ),
        out_shape=[
            jax.ShapeDtypeStruct((band_max, F, COLS, channels), BF16),
            jax.ShapeDtypeStruct((band_max, 2, COLS, channels), F32),
        ],
        compiler_params=params(36),
        cost_estimate=pl.CostEstimate(
            flops=2 * band_max * 9 * COLS * 9 * channels * channels,
            bytes_accessed=16 * 1024 * 1024,
            transcendentals=0,
        ),
        name="new_frames",
    )(band_rows, table, norm_gain.reshape(1, channels), wide_mid, *band_lat)

    slots = owners * act_capacity
    two, part = lax.optimization_barrier((two, part))
    handed = send(two[act_capacity * tiles :], 1)
    band_act = [rows.reshape(-1, tiles, LANES) for rows in (own, band_lat[1], two, handed, *far)]
    decoded = pl.pallas_call(
        functools.partial(
            cached_frames, owners=owners, units=units, capacity=act_capacity, height=height,
            block=block, band_max=band_max, channels=channels,
        ),
        grid_spec=pltpu.PrefetchScalarGridSpec(
            num_scalar_prefetch=1,
            grid=(),
            in_specs=[in_vmem, in_vmem, in_hbm] + [any_space] * owners,
            out_specs=in_hbm,
            scratch_shapes=[
                pltpu.VMEM((slots + 1, tiles, LANES), BF16),
                pltpu.VMEM((band_max, 2, COLS, channels), BF16),
                pltpu.SemaphoreType.DMA((band_max // block,)),
                pltpu.SemaphoreType.DMA((owners,)),
            ],
        ),
        out_shape=jax.ShapeDtypeStruct((band_max, F, COLS, channels), BF16),
        input_output_aliases={3: 0},
        compiler_params=params(24),
        cost_estimate=pl.CostEstimate(
            flops=2 * band_max * 3 * COLS * 9 * channels * channels,
            bytes_accessed=16 * 1024 * 1024,
            transcendentals=0,
        ),
        name="cached_frames",
    )(band_rows, part, wide_mid, late, *band_act)
    return decoded.reshape((1, 1) + decoded.shape)


def solution(mesh):
    placed = (
        P("seq", None, None, "dec", None),
        P("seq", None, None, "dec", None),
        P("seq", None, None, "dec", None),
        P(),
        P(),
        P(),
        P(),
        P(),
    )
    return jax.shard_map(
        shards,
        mesh=mesh,
        in_specs=placed,
        out_specs=P("seq", "dec", None, None, None, None),
        check_vma=False,
    )
```

```python
import functools

import jax
import jax.numpy as jnp
from jax import lax
from jax.experimental import pallas as pl
from jax.experimental.pallas import tpu as pltpu
from jax.sharding import PartitionSpec as P

F = 4
CT = 2
COLS = 16
LANES = 128
EPSILON = 1e-06
F32 = jnp.float32
BF16 = jnp.bfloat16


def band_start(bands, group, owner, owners):
    total = jnp.int32(0)
    for other in range(owners):
        total = total + jnp.where(other < owner, bands[group, other], 0)
    return total


def first_unit(start, margin, source, owners, units, capacity):
    unit = (start - margin - source + owners - 1 + 2 * owners) // owners - 2
    return jnp.clip(unit, 0, units - capacity)


def clip_of(groups_ref, shard, group, clips):
    found = jnp.int32(0)
    for clip in range(clips):
        found = found + jnp.where(groups_ref[shard, clip] == group, clip, 0)
    return found


def pack_clips(groups_ref, lat_in, old_in, act_in, *refs, per_owner, per_step, clips):
    *outs, lat_ref, old_ref, act_ref, lat_scratch, act_scratch, sems = refs
    shard = lax.axis_index("seq")
    copies = [
        pltpu.make_async_copy(lat_in, lat_ref, sems.at[0]),
        pltpu.make_async_copy(old_in, old_ref, sems.at[1]),
    ]
    steps = per_owner // per_step
    for step in range(steps):
        rows = pl.ds(step * per_step, per_step)
        copies.append(
            pltpu.make_async_copy(act_in.at[rows], act_ref.at[rows], sems.at[2 + step])
        )
    for copy in copies:
        copy.start()
    chosen = [clip_of(groups_ref, shard, shard ^ other, clips) for other in range(clips)]
    tiles = act_ref.shape[2] // LANES
    depth = tiles // (CT * COLS)
    size = per_step * tiles
    lat_rows = outs[0].shape[0] - per_owner * tiles
    copies[0].wait()
    copies[1].wait()
    for row in range(per_owner):
        for frame in range(CT + F):
            for half in range(2):
                if frame < CT:
                    tile = frame * 2 + half
                    value = old_ref[row, :, tile * LANES : (tile + 1) * LANES]
                else:
                    tile = (frame - CT) * 2 + half
                    value = lat_ref[row, :, tile * LANES : (tile + 1) * LANES]
                at = row * 12 + half * (CT + F) + frame
                lat_scratch[pl.ds(at, clips, stride=lat_rows), :] = value.astype(F32)
    for out, clip in zip(outs, chosen):
        rows = pl.ds(pl.multiple_of(clip * lat_rows, 8), lat_rows)
        out[per_owner * tiles :, :] = lat_scratch[rows, :].astype(BF16)
    for step in range(steps):
        copies[2 + step].wait()
        for row in range(per_step):
            for frame in range(CT):
                for col in range(COLS):
                    for part in range(depth):
                        tile = (frame * COLS + col) * depth + part
                        at = row * tiles + (frame * depth + part) * COLS + col
                        value = act_ref[
                            step * per_step + row, :, tile * LANES : (tile + 1) * LANES
                        ]
                        act_scratch[step % 2, pl.ds(at, clips, stride=size), :] = value.astype(F32)
        for out, clip in zip(outs, chosen):
            rows = pl.ds(pl.multiple_of(clip * size, 8), size)
            out[step * size : (step + 1) * size, :] = act_scratch[step % 2, rows, :].astype(BF16)


def slice_bands(
    bands, _, *refs, owners, units, lat_capacity, act_capacity, per_owner, tiles, groups
):
    ins, lat_outs, act_outs = refs[:groups], refs[groups : groups + owners], refs[groups + owners : -4]
    lat_scratch, scratch, in_sems, sems = refs[-4:]
    group = lax.axis_index("seq")
    source = lax.axis_index("dec")
    size = per_owner * tiles
    copies = []
    for other, in_ref in enumerate(ins):
        into = scratch.at[pl.ds(pl.multiple_of((group ^ other) * size, 16), size)]
        copies.append(pltpu.make_async_copy(in_ref.at[pl.ds(0, size)], into, in_sems.at[other]))
    for copy in copies:
        copy.start()
    rows = lat_outs[0].shape[0]
    lat_size = per_owner * 12
    for other, in_ref in enumerate(ins):
        value = in_ref[size : size + lat_size, :].astype(F32)
        lat_scratch[pl.ds((group ^ other) * lat_size, lat_size), :] = value
    value = pltpu.roll(lat_scratch[: units * 12, :], 64, 1)
    lane = lax.broadcasted_iota(jnp.int32, value.shape, 1)
    for width in (32, 16):
        up, down = pltpu.roll(value, width, 1), pltpu.roll(value, LANES - width, 1)
        value = jnp.where(lane & width == 0, down, up)
    lat_scratch[: units * 12, :] = value
    starts = [band_start(bands, group, source ^ other, owners) for other in range(owners)]
    for copy in copies:
        copy.wait()
    copies = []
    into = [(act_outs[0], 0), (lat_outs[1], 0), (act_outs[1], 0), (act_outs[1], 1)]
    into += [(out, 0) for out in act_outs[2:]]
    length = act_capacity * tiles
    for other, (out_ref, place) in enumerate(into):
        unit = first_unit(starts[other], 1, source, owners, units, act_capacity)
        rows_in = pl.ds(pl.multiple_of(unit * tiles, 16), length)
        rows_out = pl.ds(place * length, length)
        copies.append(
            pltpu.make_async_copy(scratch.at[rows_in], out_ref.at[rows_out], sems.at[other])
        )
    for copy in copies:
        copy.start()
    for other, out_ref in enumerate(lat_outs):
        unit = first_unit(starts[other], 2, source, owners, units, lat_capacity)
        value = lat_scratch[pl.ds(unit * 12, rows), :].astype(BF16)
        out_ref[pl.ds(length if other == 1 else 0, rows), :] = value
    for copy in copies:
        copy.wait()


def shift_columns(sums, width):
    rows = sums.shape[0]
    col = lax.rem(lax.broadcasted_iota(jnp.int32, (rows, width), 0), COLS)
    left = pltpu.roll(sums[:, :width], 1, 0)
    right = pltpu.roll(sums[:, 2 * width :], rows - 1, 0)
    total = sums[:, width : 2 * width] + jnp.where(col > 0, left, 0.0)
    return total + jnp.where(col < COLS - 1, right, 0.0)


def widen_weights(mid_ref, win_ref, out_ref, table, sems):
    channels = mid_ref.shape[1]
    copies = []
    for tap in range(27):
        into = out_ref.at[
            pl.ds(tap // 3 * channels, channels), pl.ds(tap % 3 * channels, channels)
        ]
        copies.append(pltpu.make_async_copy(mid_ref.at[tap], into, sems.at[tap]))
    for copy in copies:
        copy.start()
    table[...] = jnp.zeros(table.shape, BF16)
    for time_tap in range(3):
        for row_tap in range(3):
            for col_tap in range(3):
                into = row_tap * 2 * LANES + (0, 64, LANES)[time_tap]
                into += ((0, 112, 96), (0, -16, -32), (0, 112, 96))[time_tap][col_tap]
                table[pl.ds(into, 16), :] = win_ref[time_tap * 9 + row_tap * 3 + col_tap]
    for copy in copies:
        copy.wait()


def new_frames(
    bands, table, gain_ref, weights, *refs,
    owners, units, capacity, height, block, band_max, channels, cache_rows,
):
    group = lax.axis_index("seq")
    owner = lax.axis_index("dec")
    lat_refs, refs = refs[:owners], refs[owners:]
    out_ref, part_ref, xs, windows_a, windows_b, first_a, first_b = refs[:7]
    act_a, act_b, late, out_sems = refs[7:]
    live = bands[group, owner]
    start = band_start(bands, group, owner, owners)
    edge = lax.rem(height - lax.rem(start - 1 + height, height), height)
    blocks = band_max // block
    size = F * COLS
    per_source = lat_refs[0].shape[0]
    for other, lat_ref in enumerate(lat_refs):
        from_row = lat_ref.shape[0] - per_source if other != 1 else cache_rows
        value = lat_ref[pl.ds(from_row, per_source), :].astype(F32)
        rows = pl.ds(pl.multiple_of((owner ^ other) * per_source, 8), per_source)
        xs[0, rows, :] = value
        xs[1, rows, :] = pltpu.roll(value, 64, 1)
    window_zero, act_zero = block + 4, block + 2
    for windows in (windows_a, windows_b):
        windows[window_zero] = jnp.zeros(windows.shape[1:], BF16)
    for act in (act_a, act_b):
        act[act_zero] = jnp.zeros((F, COLS, channels), BF16)
    half_gain = 0.5 * gain_ref[...]

    def clip_edges(at):
        is_first = (at == edge) | (at == edge + height)
        is_last = (at == edge - 1) | (at == edge - 1 + height)
        return is_first, is_last

    def fill(row, windows, into):
        lane = lax.broadcasted_iota(jnp.int32, (8, LANES), 1)
        col = lax.broadcasted_iota(jnp.int32, (8, LANES), 0)
        low = (lane < 16) | (lane >= 96)
        left_end = (col == 0) & ((lane & 63) < 16)
        right_end = (col == 7) & ((lane & 63) >= 32) & ((lane & 63) < 48)
        stack_row = jnp.clip(start - 2 + row, 0, units * owners - 1)
        source = lax.rem(stack_row, owners)
        unit = first_unit(start, 2, source, owners, units, capacity)
        slot = jnp.clip(lax.div(stack_row, owners) - unit, 0, capacity - 1)
        base = source * per_source + slot * 12
        rolled = [{}, {}]
        for frame in range(CT + F):
            for half in range(2):
                at_row = pl.ds(base + half * (CT + F) + frame, 1)
                for turn in range(2):
                    if turn == 1 and not 1 <= frame <= F:
                        continue
                    value = jnp.broadcast_to(xs[turn, at_row, :], (8, LANES))
                    rolled[turn][half, frame] = pltpu.roll(value, 0, 1, stride=16, stride_axis=0)
        for frame in range(F):
            pair = [
                jnp.where(low, rolled[0][half, frame], rolled[1][half, frame + 1])
                for half in range(2)
            ]
            last = [rolled[0][half, frame + 2] for half in range(2)]
            for lanes, (left, right) in enumerate((pair, last)):
                near = jnp.where(left_end, 0.0, jnp.where(right_end, right, left))
                far = jnp.where(right_end, 0.0, jnp.where(left_end, left, right))
                windows[
                    into,
                    frame * COLS : (frame + 1) * COLS,
                    lanes * LANES : (lanes + 1) * LANES,
                ] = jnp.concatenate([near, far], axis=0).astype(BF16)

    def fill_block(row, count, windows):
        for at in range(count + 2):
            fill(row + at, windows, at)

    def convolve_first(row, count, windows):
        pieces = [[], [], []]
        for at in range(count):
            is_first, is_last = clip_edges(row + at)
            pieces[0].append(windows[jnp.where(is_first, window_zero, at)])
            pieces[1].append(windows[at + 1])
            pieces[2].append(windows[jnp.where(is_last, window_zero, at + 2)])
        slab = jnp.concatenate([jnp.concatenate(part, axis=0) for part in pieces], axis=1)
        return jnp.dot(slab, table[...], preferred_element_type=F32)

    def activate(sums, count, into, first, act):
        first[into * size : (into + count) * size, :] = sums
        for at in range(count):
            value = sums[at * size : (at + 1) * size]
            mean_square = jnp.mean(value * value, axis=-1, keepdims=True)
            half = value * lax.rsqrt(mean_square + EPSILON) * half_gain
            value = half + half * jnp.tanh(half)
            act[into + at] = value.astype(BF16).reshape(F, COLS, channels)

    def copy_out(number):
        rows = pl.ds(number * block, block)
        return pltpu.make_async_copy(
            late.at[rows], out_ref.at[rows, pl.ds(2, 2)], out_sems.at[number]
        )

    def convolve(number, first, act):
        begin = number * block
        source_rows = [[], [], []]
        for row in range(block):
            is_first, is_last = clip_edges(begin + row + 1)
            source_rows[0].append(jnp.where(is_first, act_zero, row))
            source_rows[1].append(row + 1)
            source_rows[2].append(jnp.where(is_last, act_zero, row + 2))

        def finish(frames, weight_from, frame_from, count):
            pieces = []
            for frame in frames:
                for row_tap in range(3):
                    parts = [
                        act[at, frame : frame + count].reshape(count * COLS, channels)
                        for at in source_rows[row_tap]
                    ]
                    pieces.append(jnp.concatenate(parts, axis=0))
            slab = jnp.concatenate(pieces, axis=1)
            sums = jnp.dot(slab, weights[weight_from:, :], preferred_element_type=F32)
            total = shift_columns(sums, channels)
            parts = []
            for row in range(block):
                at = (row + 1) * size + frame_from * COLS
                parts.append(first[at : at + count * COLS, :])
            return total + jnp.concatenate(parts, axis=0)

        taps = 3 * channels
        rows = pl.ds(begin, block)
        value = finish([0, 1, 2], 0, 2, 2)
        at_row = lax.broadcasted_iota(jnp.int32, value.shape, 0) // (2 * COLS)
        value = jnp.where(at_row < live - begin, value, 0.0)
        late[rows] = value.astype(BF16).reshape(block, 2, COLS, channels)
        part_ref[rows, 1] = finish([0, 1], taps, 1, 1).reshape(block, COLS, channels)
        part_ref[rows, 0] = finish([0], 2 * taps, 0, 1).reshape(block, COLS, channels)

    used = lax.div(live + block - 1, block)

    used = lax.div(live + block - 1, block)

    def step(number, windows, first, act, next_windows, next_first, next_act):
        sums = convolve_first((number + 1) * block + 2, block, windows)
        for row in range(2):
            next_act[row] = act[block + row]
        next_first[: 2 * size, :] = first[block * size :, :]
        activate(sums, block, 2, next_first, next_act)
        convolve(number, first, act)
        fill_block((number + 2) * block + 2, block, next_windows)
        copy_out(number).start()

    fill_block(0, block + 2, windows_b)
    activate(convolve_first(0, block + 2, windows_b), block + 2, 0, first_a, act_a)
    fill_block(block + 2, block, windows_a)

    def two_steps(pair, carry):
        step(2 * pair, windows_a, first_a, act_a, windows_b, first_b, act_b)

        @pl.when(2 * pair + 2 < used)
        def _():
            step(2 * pair + 1, windows_b, first_b, act_b, windows_a, first_a, act_a)

        @pl.when(2 * pair + 2 == used)
        def _():
            convolve(2 * pair + 1, first_b, act_b)
            copy_out(2 * pair + 1).start()

        return carry

    lax.fori_loop(0, lax.div(used + 1, 2), two_steps, 0)

    def clear(number, carry):
        late[pl.ds(number * block, block)] = jnp.zeros((block, 2, COLS, channels), BF16)
        copy_out(number).start()
        return carry

    lax.fori_loop(used, blocks, clear, 0)
    for number in range(blocks):
        copy_out(number).wait()


def cached_frames(
    bands, part_ref, weights, late_ref, *refs,
    owners, units, capacity, height, block, band_max, channels,
):
    del late_ref
    parts, (out_ref, cache, early, out_sems, cache_sems) = refs[:owners], refs[owners:]
    group = lax.axis_index("seq")
    owner = lax.axis_index("dec")
    live = bands[group, owner]
    start = band_start(bands, group, owner, owners)
    depth = channels // LANES
    blocks = band_max // block
    edge = lax.rem(height - lax.rem(start - 1 + height, height), height)

    def slot_of(at):
        row = jnp.clip(start - 1 + at, 0, units * owners - 1)
        source = lax.rem(row, owners)
        unit = first_unit(start, 1, source, owners, units, capacity)
        return source * capacity + jnp.clip(lax.div(row, owners) - unit, 0, capacity - 1)

    def copy_out(number):
        rows = pl.ds(number * block, block)
        return pltpu.make_async_copy(
            early.at[rows], out_ref.at[rows, pl.ds(0, 2)], out_sems.at[number]
        )

    copies = []
    for other, part in enumerate(parts):
        into = cache.at[pl.ds((owner ^ other) * capacity, capacity)]
        arrived = part.at[pl.ds(0, capacity)]
        copies.append(pltpu.make_async_copy(arrived, into, cache_sems.at[other]))
    for copy in copies:
        copy.start()
    slots = owners * capacity
    cache[slots] = jnp.zeros(cache.shape[1:], BF16)
    for copy in copies:
        copy.wait()
    used = lax.div(live + block - 1, block)

    def convolve(number, carry):
        begin = number * block
        source_rows = [[], [], []]
        for row in range(block):
            at = begin + row + 1
            is_first = (at == edge) | (at == edge + height)
            is_last = (at == edge - 1) | (at == edge - 1 + height)
            source_rows[0].append(jnp.where(is_first, slots, slot_of(at - 1)))
            source_rows[1].append(slot_of(at))
            source_rows[2].append(jnp.where(is_last, slots, slot_of(at + 1)))

        def slab(frames):
            pieces = []
            for frame in frames:
                for row_tap in range(3):
                    for part in range(depth):
                        tile = pl.ds((frame * depth + part) * COLS, COLS)
                        values = [cache[at, tile, :] for at in source_rows[row_tap]]
                        pieces.append(jnp.concatenate(values, axis=0))
            return jnp.concatenate(pieces, axis=1)

        at_row = lax.broadcasted_iota(jnp.int32, (block * COLS, channels), 0) // COLS
        taps = 3 * channels
        rows = pl.ds(begin, block)
        for frame, frames in ((0, (0, 1)), (1, (1,))):
            sums = jnp.dot(
                slab(frames), weights[: len(frames) * taps, :], preferred_element_type=F32
            )
            total = shift_columns(sums, channels) + part_ref[rows, frame].reshape(
                block * COLS, channels
            )
            total = jnp.where(at_row < live - begin, total, 0.0)
            early[rows, frame] = total.astype(BF16).reshape(block, COLS, channels)
        copy_out(number).start()
        return carry

    lax.fori_loop(0, used, convolve, 0)

    def clear(number, carry):
        early[pl.ds(number * block, block)] = jnp.zeros((block, 2, COLS, channels), BF16)
        copy_out(number).start()
        return carry

    lax.fori_loop(used, blocks, clear, 0)
    for number in range(blocks):
        copy_out(number).wait()


def params(mebibytes, **extra):
    return pltpu.CompilerParams(vmem_limit_bytes=mebibytes * 1024 * 1024, **extra)


def shards(latents, cache_lat, cache_act, w_in, w_mid, norm_gain, clip_group, band_rows):
    groups = lax.axis_size("seq")
    owners = lax.axis_size("dec")
    clips = latents.shape[1]
    per_owner = latents.shape[2]
    channels = w_mid.shape[2]
    units = groups * per_owner
    height = per_owner * owners
    stack_rows = groups * height
    band_max = 2 * stack_rows // owners
    act_capacity = (band_max + 2 + owners - 1) // owners
    block = next(size for size in (16, 8) if band_max % size == 0)
    any_space = pl.BlockSpec(memory_space=pl.ANY)
    in_vmem = pl.BlockSpec(memory_space=pltpu.VMEM)
    in_hbm = pl.BlockSpec(memory_space=pltpu.HBM)

    def rows_first(array):
        return jnp.transpose(array[0, :, :, 0, :], (1, 0, 2))

    lat, old, act = rows_first(latents), rows_first(cache_lat), rows_first(cache_act)
    tiles = act.shape[2] // LANES
    lat_rows = (per_owner * 12 + 15) // 16 * 16
    per_step = 3
    packed = pl.pallas_call(
        functools.partial(
            pack_clips, per_owner=per_owner, per_step=per_step, clips=clips
        ),
        grid_spec=pltpu.PrefetchScalarGridSpec(
            num_scalar_prefetch=1,
            grid=(),
            in_specs=[in_hbm, in_hbm, in_hbm],
            out_specs=[in_vmem] * clips,
            scratch_shapes=[
                pltpu.VMEM(lat.shape, BF16),
                pltpu.VMEM(old.shape, BF16),
                pltpu.VMEM(act.shape, BF16),
                pltpu.VMEM((clips * lat_rows, LANES), F32),
                pltpu.VMEM((2, clips * per_step * tiles, LANES), F32),
                pltpu.SemaphoreType.DMA((2 + per_owner // per_step,)),
            ],
        ),
        out_shape=[jax.ShapeDtypeStruct((per_owner * tiles + lat_rows, LANES), BF16)] * clips,
        compiler_params=params(56),
        name="pack_clips",
    )(clip_group, lat, old, act)

    def trade(parts, axis):
        count = lax.axis_size(axis)
        return [parts[0]] + [
            lax.ppermute(part, axis, [(i, i ^ other) for i in range(count)])
            for other, part in enumerate(parts)
            if other
        ]

    traded = trade(packed, "seq")
    wide_mid, table = pl.pallas_call(
        widen_weights,
        in_specs=[in_hbm, in_vmem],
        out_specs=[in_vmem, in_vmem],
        scratch_shapes=[pltpu.SemaphoreType.DMA((27,))],
        out_shape=[
            jax.ShapeDtypeStruct((9 * channels, 3 * channels), BF16),
            jax.ShapeDtypeStruct((6 * LANES, channels), BF16),
        ],
        compiler_params=params(16),
        cost_estimate=pl.CostEstimate(
            flops=0, bytes_accessed=4 * 27 * channels * channels, transcendentals=0
        ),
        name="widen_weights",
    )(w_mid, w_in)
    lat_capacity = (band_max + 4 + owners - 1) // owners
    slice_rows = (lat_capacity * 12 + 15) // 16 * 16
    slice_both = (act_capacity * tiles + slice_rows + tiles - 1) // tiles * tiles
    slice_act = jax.ShapeDtypeStruct((act_capacity * tiles, LANES), BF16)
    slice_two = jax.ShapeDtypeStruct((2 * act_capacity * tiles, LANES), BF16)
    sliced = pl.pallas_call(
        functools.partial(
            slice_bands, owners=owners, units=units, lat_capacity=lat_capacity,
            act_capacity=act_capacity, per_owner=per_owner, tiles=tiles, groups=groups,
        ),
        grid_spec=pltpu.PrefetchScalarGridSpec(
            num_scalar_prefetch=1,
            grid=(),
            in_specs=[in_vmem] * (1 + clips),
            out_specs=[in_vmem] * (2 * owners - 2),
            scratch_shapes=[
                pltpu.VMEM((units * 12 + slice_rows, LANES), F32),
                pltpu.VMEM((units * tiles, LANES), BF16),
                pltpu.SemaphoreType.DMA((clips,)),
                pltpu.SemaphoreType.DMA((owners,)),
            ],
        ),
        out_shape=[
            jax.ShapeDtypeStruct((slice_both if other == 1 else slice_rows, LANES), BF16)
            for other in range(owners)
        ]
        + [slice_act, slice_two]
        + [slice_act] * (owners - 4),
        compiler_params=params(16),
        name="slice_bands",
    )(band_rows, table, *traded)
    band_lat, band_act = lax.optimization_barrier(
        (trade(sliced[:owners], "dec"), sliced[owners:])
    )

    def send(part, other):
        return lax.ppermute(part, "dec", [(i, i ^ other) for i in range(owners)])

    own, *band_act = band_act
    far = [send(part, other) for other, part in enumerate(band_act[1:], 4)]
    two = send(band_act[0], 2)

    late, part = pl.pallas_call(
        functools.partial(
            new_frames, owners=owners, units=units, capacity=lat_capacity, height=height,
            block=block, band_max=band_max, channels=channels, cache_rows=act_capacity * tiles,
        ),
        grid_spec=pltpu.PrefetchScalarGridSpec(
            num_scalar_prefetch=1,
            grid=(),
            in_specs=[in_vmem] * (3 + owners),
            out_specs=[in_hbm, in_vmem],
            scratch_shapes=[
                pltpu.VMEM((2, owners * slice_rows, LANES), F32),
                pltpu.VMEM((block + 5, F * COLS, 2 * LANES), BF16),
                pltpu.VMEM((block + 5, F * COLS, 2 * LANES), BF16),
                pltpu.VMEM(((block + 2) * F * COLS, channels), F32),
                pltpu.VMEM(((block + 2) * F * COLS, channels), F32),
                pltpu.VMEM((block + 3, F, COLS, channels), BF16),
                pltpu.VMEM((block + 3, F, COLS, channels), BF16),
                pltpu.VMEM((band_max, 2, COLS, channels), BF16),
                pltpu.SemaphoreType.DMA((band_max // block,)),
            ],
        ),
        out_shape=[
            jax.ShapeDtypeStruct((band_max, F, COLS, channels), BF16),
            jax.ShapeDtypeStruct((band_max, 2, COLS, channels), F32),
        ],
        compiler_params=params(36),
        cost_estimate=pl.CostEstimate(
            flops=2 * band_max * 9 * COLS * 9 * channels * channels,
            bytes_accessed=16 * 1024 * 1024,
            transcendentals=0,
        ),
        name="new_frames",
    )(band_rows, table, norm_gain.reshape(1, channels), wide_mid, *band_lat)

    slots = owners * act_capacity
    two, part = lax.optimization_barrier((two, part))
    handed = send(two[act_capacity * tiles :], 1)
    band_act = [rows.reshape(-1, tiles, LANES) for rows in (own, band_lat[1], two, handed, *far)]
    decoded = pl.pallas_call(
        functools.partial(
            cached_frames, owners=owners, units=units, capacity=act_capacity, height=height,
            block=block, band_max=band_max, channels=channels,
        ),
        grid_spec=pltpu.PrefetchScalarGridSpec(
            num_scalar_prefetch=1,
            grid=(),
            in_specs=[in_vmem, in_vmem, in_hbm] + [any_space] * owners,
            out_specs=in_hbm,
            scratch_shapes=[
                pltpu.VMEM((slots + 1, tiles, LANES), BF16),
                pltpu.VMEM((band_max, 2, COLS, channels), BF16),
                pltpu.SemaphoreType.DMA((band_max // block,)),
                pltpu.SemaphoreType.DMA((owners,)),
            ],
        ),
        out_shape=jax.ShapeDtypeStruct((band_max, F, COLS, channels), BF16),
        input_output_aliases={3: 0},
        compiler_params=params(24),
        cost_estimate=pl.CostEstimate(
            flops=2 * band_max * 3 * COLS * 9 * channels * channels,
            bytes_accessed=16 * 1024 * 1024,
            transcendentals=0,
        ),
        name="cached_frames",
    )(band_rows, part, wide_mid, late, *band_act)
    return decoded.reshape((1, 1) + decoded.shape)


def solution(mesh):
    placed = (
        P("seq", None, None, "dec", None),
        P("seq", None, None, "dec", None),
        P("seq", None, None, "dec", None),
        P(),
        P(),
        P(),
        P(),
        P(),
    )
    return jax.shard_map(
        shards,
        mesh=mesh,
        in_specs=placed,
        out_specs=P("seq", "dec", None, None, None, None),
        check_vma=False,
    )
```
